128 devices in a mesh: gx: 8 (over z, x_hi), gy: 16 (over y, x_lo, core).
Axes of the slice: x: 4 (x_hi: 2, x_lo: 2; x = x_hi * 2 + x_lo), y: 4, z: 4, core: 2. Of those that a mesh axis runs over, the one named last changes fastest.
Arguments:
- intensity: bfloat16 [16, 128, 1024], P(None, 'gy', 'gx'), may hold values from -6 to 6
- first_kernel: bfloat16 [3, 3, 3, 1, 64], replicated, may hold values from -1.25 to 1.25
- second_kernel: bfloat16 [3, 3, 3, 64, 64], replicated, may hold values from -0.21875 to 0.21875
- third_kernel: bfloat16 [3, 3, 3, 64, 64], replicated, may hold values from -0.21875 to 0.21875
- head_weight: bfloat16 [64, 75], replicated, may hold values from -1.5 to 1.5
Outputs:
- affinity: float32 [3, 16, 128, 1024], P(None, None, 'gy', 'gx')
The draws below stay inside these ranges and needn't reach their ends.
All inputs are finite; a program needn't handle non-finite values.
Results may differ from the reference program's by a relative error of at most 0.00075.
Values may be sent and summed in bfloat16 or wider, within the bound.
A program may use at most 128 MiB of HBM per device.

```python
import jax
import jax.numpy as jnp
from jax import lax

C = 64
R = 2
Z = 16
NX = 1024
NY = 128


def block_scale(stream_key, shape, split, low, largest):
    loudness = 1.0
    for dim, blocks in split:
        draws = jax.random.uniform(jax.random.fold_in(jax.random.fold_in(stream_key, 6), dim), (blocks,), jnp.float32, low / len(split), largest / len(split))
        loudness = loudness * jnp.repeat(jnp.exp(draws), shape[dim] // blocks).reshape((-1,) + (1,) * (len(shape) - 1 - dim))
    return loudness


def scatter_about(rng, dims, scale, reach, shards=(), kind=jnp.bfloat16):
    entries = scale * jax.random.normal(rng, dims, jnp.float32)
    if shards:
        entries = entries * block_scale(rng, dims, shards, -0.22, 0.18)
    return jnp.clip(entries, -reach, reach).astype(kind)


def setup_inputs(seed: int = 0) -> dict:
    key_list = jax.random.split(jax.random.key(seed), 6)
    return {
        "intensity": scatter_about(key_list[0], (Z, NY, NX), 1.0, 6.0, ((1, 16), (2, 8))),
        "first_kernel": scatter_about(key_list[1], (3, 3, 3, 1, C), 27 ** -0.5, 1.25),
        "second_kernel": scatter_about(key_list[2], (3, 3, 3, C, C), (27 * C // 2) ** -0.5, 0.21875),
        "third_kernel": scatter_about(key_list[3], (3, 3, 3, C, C), (27 * C // 2) ** -0.5, 0.21875),
        "head_weight": scatter_about(key_list[4], (C, (2 * R + 1) * (2 * R + 1) * 3), (C // 4) ** -0.5, 1.5),
    }


def convolve(volume, kernel):
    return lax.conv_general_dilated(volume[None], kernel, (1, 1, 1), [(1, 1), (1, 1), (1, 1)], dimension_numbers=("NDHWC", "DHWIO", "NDHWC"), preferred_element_type=jnp.float32)[0]


def coverage(length, blending):
    covered = jnp.zeros((length + 2 * R,), jnp.float32)
    for offset in range(2 * R + 1):
        covered = covered.at[offset:offset + length].add(blending[offset])
    return covered[R:R + length]


def reference(intensity, first_kernel, second_kernel, third_kernel, head_weight):
    stem_feat = jax.nn.relu(convolve(intensity[..., None], first_kernel)).astype(jnp.bfloat16)
    inner_feat = jax.nn.relu(convolve(stem_feat, second_kernel)).astype(jnp.bfloat16)
    block_feat = jax.nn.relu(convolve(inner_feat, third_kernel) + stem_feat.astype(jnp.float32)).astype(jnp.bfloat16)
    window = 2 * R + 1
    blending = (R + 1 - jnp.abs(jnp.arange(window) - R)).astype(jnp.float32)
    flattened = block_feat.reshape(Z * NY * NX, block_feat.shape[-1])
    numerator = jnp.zeros((3, Z, NY + 2 * R, NX + 2 * R), jnp.float32)
    for offset_x in range(window):
        for offset_y in range(window):
            column = (offset_x * window + offset_y) * 3
            logits = jnp.dot(flattened, head_weight[:, column:column + 3], preferred_element_type=jnp.float32)
            contrib = jax.nn.sigmoid(logits) * (blending[offset_x] * blending[offset_y])
            contrib = contrib.reshape(Z, NY, NX, 3).transpose(3, 0, 1, 2)
            numerator = numerator.at[:, :, offset_y:offset_y + NY, offset_x:offset_x + NX].add(contrib)
    numerator = numerator[:, :, R:R + NY, R:R + NX]
    weight_total = coverage(NY, blending)[:, None] * coverage(NX, blending)[None, :]
    return numerator / weight_total[None, None, :, :]
```

```python
import functools

import jax
import jax.numpy as jnp
import numpy as np
from jax import lax
from jax.experimental import pallas as pl
from jax.experimental.pallas import tpu as pltpu
from jax.sharding import PartitionSpec as P

R = 2
C = 64
Z = 16
TY = 8
TX = 128
BF = jnp.bfloat16
F32 = jnp.float32
MESH = pl.DeviceIdType.MESH

STEM_PAIRS = 8
INNER_PAIRS = 7
BLOCK_PAIRS = 6
STEM_X = 68
INNER_X = 67
BLOCK_X = 66
XT = 17


def exchange_kernel(tile_ref, out_ref, send_sem, recv_sem, local_sem):
    gx, gy = lax.axis_index("gx"), lax.axis_index("gy")
    nx, ny = lax.axis_size("gx"), lax.axis_size("gy")
    around = [(dy, dx) for dy in (-1, 0, 1) for dx in (-1, 0, 1) if (dy, dx) != (0, 0)]

    def device(dy, dx):
        return (lax.rem(gx + dx + nx, nx), lax.rem(gy + dy + ny, ny))

    barrier = pltpu.get_barrier_semaphore()
    for dy, dx in around:
        pl.semaphore_signal(barrier, inc=1, device_id=device(dy, dx), device_id_type=MESH)
    own = pltpu.make_async_copy(tile_ref, out_ref.at[4], local_sem)
    own.start()
    pl.semaphore_wait(barrier, len(around))
    copies = []
    for n, (dy, dx) in enumerate(around):
        slot = (1 - dy) * 3 + (1 - dx)
        copies.append(
            pltpu.make_async_remote_copy(
                src_ref=tile_ref,
                dst_ref=out_ref.at[slot],
                send_sem=send_sem.at[n],
                recv_sem=recv_sem.at[n],
                device_id=device(dy, dx),
                device_id_type=MESH,
            )
        )
        copies[-1].start()
    own.wait()
    for copy in copies:
        copy.wait()


def exchange(tile):
    return pl.pallas_call(
        exchange_kernel,
        out_shape=jax.ShapeDtypeStruct((9,) + tile.shape, tile.dtype),
        in_specs=[pl.BlockSpec(memory_space=pltpu.VMEM)],
        out_specs=pl.BlockSpec(memory_space=pltpu.VMEM),
        scratch_shapes=[
            pltpu.SemaphoreType.DMA((8,)),
            pltpu.SemaphoreType.DMA((8,)),
            pltpu.SemaphoreType.DMA,
        ],
        compiler_params=pltpu.CompilerParams(collective_id=0, has_side_effects=True),
        name="exchange_tiles",
    )(tile)


def store_shifted(ref, pair, parity, start, count, value, row):
    below = jnp.where(row == 0, 0.0, pltpu.roll(value, 1, axis=1))
    above = jnp.where(row == Z - 1, 0.0, pltpu.roll(value, Z - 1, axis=1))
    for shift, part in enumerate((below, value, above)):
        ref[shift, pair, parity, pl.ds(start, count)] = part.astype(BF)


def conv_operand(ref, pair, start, count):
    parts = []
    for shift in range(3):
        for offset in range(4):
            for k in range(2):
                part = ref[shift, pair + k, offset % 2, pl.ds(start + offset // 2, count)]
                parts.append(part.reshape(count * Z, 2 * C))
    return jnp.concatenate(parts, axis=1)


def build_conv_weights(kernel_ref, out_ref):
    zero = jnp.zeros((C, C), BF)
    for shift in range(3):
        for offset in range(4):
            for source in range(4):
                rows = ((shift * 4 + offset) * 4 + source) * C
                for qx in range(2):
                    blocks = []
                    for qy in range(2):
                        dx, dy = offset - qx, source - qy
                        inside = 0 <= dx < 3 and 0 <= dy < 3
                        blocks.append(kernel_ref[(shift * 3 + dy) * 3 + dx] if inside else zero)
                    out_ref[rows : rows + C, qx * 128 : qx * 128 + 128] = jnp.concatenate(blocks, axis=1)


def zero_pairs(ref, pair, lower=None):
    count = ref.shape[3]
    lane = lax.broadcasted_iota(jnp.int32, (Z, 2 * C), 1)

    def body(i, carry):
        for shift in range(3):
            for parity in range(2):
                if lower is None:
                    ref[shift, pair, parity, i] = jnp.zeros((Z, 2 * C), BF)
                else:
                    old = ref[shift, pair, parity, i].astype(F32)
                    keep = lane >= C if lower else lane < C
                    ref[shift, pair, parity, i] = jnp.where(keep, old, 0.0).astype(BF)
        return carry

    lax.fori_loop(0, count, body, 0)


def zero_columns(ref, columns):
    for pair in range(ref.shape[1]):
        for x in columns:
            for shift in range(3):
                ref[shift, pair, x % 2, x // 2] = jnp.zeros((Z, 2 * C), BF)


def coverage_of(position, length):
    total = jnp.zeros(position.shape, F32)
    for b in range(2 * R + 1):
        source = position - (b - R)
        total += jnp.where((source >= 0) & (source < length), float(R + 1 - abs(b - R)), 0.0)
    return total


def compute_kernel(
    tiles_ref, place_ref, first_ref, second_ref, third_ref, head_ref, columns_ref, blend_ref,
    out_ref,
    w1, w2, w3, wh, main, edge, qf, qb, stem, inner, pred, total,
):
    gx, gy = lax.axis_index("gx"), lax.axis_index("gy")
    nx, ny = lax.axis_size("gx"), lax.axis_size("gy")
    at_low_x, at_high_x = gx == 0, gx == nx - 1
    at_low_y, at_high_y = gy == 0, gy == ny - 1

    build_conv_weights(second_ref, w2)
    build_conv_weights(third_ref, w3)
    for pair in range(STEM_PAIRS):
        w1[pair] = jnp.dot(place_ref[pair], first_ref[...], preferred_element_type=F32).astype(BF)
    for py in range(2):
        wh[py * C : py * C + C, :] = jnp.dot(
            head_ref[...], columns_ref[py], preferred_element_type=F32
        ).astype(BF)

    lane8 = lax.broadcasted_iota(jnp.int32, (TY, TX), 1)
    for buffer in (main, edge):
        buffer[0] = jnp.zeros((3 * TY, TX), F32)
        buffer[Z + 1] = jnp.zeros((3 * TY, TX), F32)
    right_ok = jnp.where(at_high_x, 0, 64)
    left_ok = jnp.where(at_low_x, 128, 64)

    def spread_z(z, carry):
        for ty in range(3):
            middle = tiles_ref[ty * 3 + 1, z].astype(F32)
            left = tiles_ref[ty * 3, z].astype(F32)
            right = tiles_ref[ty * 3 + 2, z].astype(F32)
            sides = jnp.where(lane8 < right_ok, right, jnp.where(lane8 >= left_ok, left, 0.0))
            if ty == 0:
                middle, sides = jnp.where(at_low_y, 0.0, middle), jnp.where(at_low_y, 0.0, sides)
            if ty == 2:
                middle, sides = jnp.where(at_high_y, 0.0, middle), jnp.where(at_high_y, 0.0, sides)
            main[z + 1, ty * TY : ty * TY + TY, :] = middle
            edge[z + 1, ty * TY : ty * TY + TY, :] = sides
        return carry

    lax.fori_loop(0, Z, spread_z, 0)
    filler = jnp.zeros((128 - 9 * TY, TX), F32)
    for z in range(Z):
        middle = jnp.concatenate([main[z], main[z + 1], main[z + 2], filler], axis=0).T
        sides = jnp.concatenate([edge[z], edge[z + 1], edge[z + 2], filler], axis=0).T
        qf[pl.ds(8 * Z + z, TX, stride=Z), :] = middle
        qf[pl.ds(z, 8, stride=Z), :] = sides[120:128]
        qf[pl.ds(136 * Z + z, 8, stride=Z), :] = sides[0:8]

    def round_pair(m, carry):
        for parity in range(2):
            qb[parity, m] = qf[pl.ds(pl.multiple_of((2 * m + parity) * Z, Z), Z), :].astype(BF)
        return carry

    lax.fori_loop(0, 72, round_pair, 0)

    row = lax.broadcasted_iota(jnp.int32, (XT, Z, 2 * C), 1)

    def stem_body(step, carry):
        pair, j = step // 4, (step % 4) * XT
        parts = []
        for offset in range(4):
            at = offset + 3
            parts.append(qb[at % 2, pl.ds(j + at // 2, XT)].reshape(XT * Z, 128))
        acc = jnp.dot(jnp.concatenate(parts, axis=1), w1[pair], preferred_element_type=F32)
        acc = jnp.maximum(acc, 0.0)
        for qx in range(2):
            value = acc[:, qx * 128 : qx * 128 + 128].reshape(XT, Z, 128)
            store_shifted(stem, pair, qx, j, XT, value, row)
        return carry

    lax.fori_loop(0, STEM_PAIRS * 4, stem_body, 0)

    @pl.when(at_low_y)
    def _():
        zero_pairs(stem, 0)
        zero_pairs(stem, 1)

    @pl.when(at_high_y)
    def _():
        zero_pairs(stem, 6)
        zero_pairs(stem, 7)

    @pl.when(at_low_x)
    def _():
        zero_columns(stem, range(4))

    @pl.when(at_high_x)
    def _():
        zero_columns(stem, range(132, 136))

    for pair in range(STEM_PAIRS):
        for shift in range(3):
            for parity in range(2):
                stem[shift, pair, parity, STEM_X] = jnp.zeros((Z, 2 * C), BF)

    def inner_body(step, carry):
        pair, j = step // 4, (step % 4) * XT
        acc = jnp.dot(conv_operand(stem, pair, j, XT), w2[...], preferred_element_type=F32)
        acc = jnp.maximum(acc, 0.0)
        for qx in range(2):
            value = acc[:, qx * 128 : qx * 128 + 128].reshape(XT, Z, 128)
            store_shifted(inner, pair, qx, j, XT, value, row)
        return carry

    lax.fori_loop(0, INNER_PAIRS * 4, inner_body, 0)

    @pl.when(at_low_y)
    def _():
        zero_pairs(inner, 0)
        zero_pairs(inner, 1, lower=True)

    @pl.when(at_high_y)
    def _():
        zero_pairs(inner, 5, lower=False)
        zero_pairs(inner, 6)

    @pl.when(at_low_x)
    def _():
        zero_columns(inner, range(3))

    @pl.when(at_high_x)
    def _():
        zero_columns(inner, range(131, 134))

    for pair in range(INNER_PAIRS):
        for shift in range(3):
            for parity in range(2):
                inner[shift, pair, parity, STEM_X] = jnp.zeros((Z, 2 * C), BF)

    def block_body(step, carry):
        pair, j = step // 4, (step % 4) * XT
        acc = jnp.dot(conv_operand(inner, pair, j, XT), w3[...], preferred_element_type=F32)
        for qx in range(2):
            old = stem[1, pair + 1, qx, pl.ds(j + 1, XT)].reshape(XT * Z, 128).astype(F32)
            value = jnp.maximum(acc[:, qx * 128 : qx * 128 + 128] + old, 0.0).astype(BF)
            logits = jnp.dot(value, wh[...], preferred_element_type=F32)
            pred[pair, qx, pl.ds(j, XT)] = jnp.tanh(logits).astype(BF).reshape(XT, Z, 256)
        return carry

    lax.fori_loop(0, BLOCK_PAIRS * 4, block_body, 0)

    def zero_pred(pair):
        def body(i, carry):
            for parity in range(2):
                pred[pair, parity, i] = jnp.zeros((Z, 256), BF)
            return carry

        lax.fori_loop(0, BLOCK_X, body, 0)

    @pl.when(at_low_y)
    def _():
        zero_pred(0)

    @pl.when(at_high_y)
    def _():
        zero_pred(5)

    @pl.when(at_low_x)
    def _():
        for pair in range(BLOCK_PAIRS):
            for parity in range(2):
                pred[pair, parity, 0] = jnp.zeros((Z, 256), BF)

    @pl.when(at_high_x)
    def _():
        for pair in range(BLOCK_PAIRS):
            for parity in range(2):
                pred[pair, parity, 65] = jnp.zeros((Z, 256), BF)

    lanes = lax.broadcasted_iota(jnp.int32, (1, Z, 128), 2)
    XB = 8

    def blend_body(step, carry):
        j = step * XB
        for qx in range(2):
            operands = []
            for target in range(TY // 2):
                for half in range(2):
                    chosen = None
                    for a in (0, 1, 2) if half == 0 else (2, 3, 4):
                        at = qx - a + 4
                        for k in range(3):
                            part = pred[target + k, at % 2, pl.ds(j + at // 2, XB), :, half * 128 : half * 128 + 128]
                            if chosen is None:
                                chosen = part
                            else:
                                group = (a - (0 if half == 0 else 2)) * 3 + k
                                chosen = jnp.where(lanes >= GROUP_START[half][group], part, chosen)
                    operands.append(chosen.reshape(XB * Z, 128))
            added = jnp.dot(jnp.concatenate(operands, axis=1), blend_ref[...], preferred_element_type=F32)
            total[qx, pl.ds(pl.multiple_of(j * Z, XB * Z), XB * Z), :] = added
        return carry

    lax.fori_loop(0, TX // 2 // XB, blend_body, 0)

    y = gy * TY + lax.broadcasted_iota(jnp.int32, (TY, TX), 0)
    x = gx * TX + lane8
    scale = 0.5 / (coverage_of(y, ny * TY) * coverage_of(x, nx * TX))

    for z in range(Z):
        even = total[0, pl.ds(z, TX // 2, stride=Z), :]
        odd = total[1, pl.ds(z, TX // 2, stride=Z), :]
        both = jnp.stack([even, odd], axis=1).reshape(TX, 128).T
        for c in range(3):
            out_ref[c, z] = 0.5 + both[c * TY : c * TY + TY, :] * scale


def lane_plan():
    plan, starts = [], []
    for half in range(2):
        lanes, begin = [], []
        for a in (0, 1, 2) if half == 0 else (2, 3, 4):
            for k in range(3):
                begin.append(len(lanes))
                for py in range(2):
                    if a == 2 and py != half:
                        continue
                    for b in range(5):
                        if -((py + b - 4) // 2) == k:
                            lanes += [(a, py, b, c) for c in range(3)]
        plan.append(lanes)
        starts.append(begin)
    return plan, starts


LANES, GROUP_START = lane_plan()


def constants():
    place = np.zeros((STEM_PAIRS, 4, 128, 128), np.float32)
    for pair in range(STEM_PAIRS):
        for qx in range(2):
            for qy in range(2):
                for dz in range(3):
                    for dy in range(3):
                        for dx in range(3):
                            y = 3 + 2 * pair + qy + dy
                            place[pair, qx + dx, dz * 24 + y, (qx * 2 + qy) * 32 + (dz * 3 + dy) * 3 + dx] = 1
    columns = np.zeros((2, 75, 256), np.float32)
    blend = np.zeros((TY // 2, 256, 128), np.float32)
    for half in range(2):
        for n, (a, py, b, c) in enumerate(LANES[half]):
            columns[py, (a * 5 + b) * 3 + c, half * 128 + n] = 0.5
            for target in range(TY // 2):
                weight = (R + 1 - abs(a - R)) * (R + 1 - abs(b - R))
                blend[target, half * 128 + n, c * TY + 2 * target + (py + b) % 2] = weight
    return (
        jnp.asarray(place.reshape(STEM_PAIRS, 512, 128), BF),
        jnp.asarray(columns, BF),
        jnp.asarray(blend.reshape(-1, 128), BF),
    )


def local(intensity, first_kernel, second_kernel, third_kernel, head_weight):
    tiles = exchange(intensity)
    place, columns, blend = constants()
    taps = jnp.pad(first_kernel.reshape(27, C), ((0, 5), (0, 0)))
    first = (jnp.eye(4, dtype=BF)[:, None, :, None] * taps[None, :, None, :]).reshape(128, 256)
    padded = STEM_X + 2
    return pl.pallas_call(
        compute_kernel,
        out_shape=jax.ShapeDtypeStruct((3, Z, TY, TX), F32),
        in_specs=[pl.BlockSpec(memory_space=pltpu.VMEM)] * 8,
        out_specs=pl.BlockSpec(memory_space=pltpu.VMEM),
        scratch_shapes=[
            pltpu.VMEM((STEM_PAIRS, 512, 256), BF),
            pltpu.VMEM((3072, 256), BF),
            pltpu.VMEM((3072, 256), BF),
            pltpu.VMEM((128, 256), BF),
            pltpu.VMEM((Z + 2, 3 * TY, TX), F32),
            pltpu.VMEM((Z + 2, 3 * TY, TX), F32),
            pltpu.VMEM((144 * Z, 128), F32),
            pltpu.VMEM((2, 72, Z, 128), BF),
            pltpu.VMEM((3, STEM_PAIRS, 2, padded, Z, 128), BF),
            pltpu.VMEM((3, INNER_PAIRS, 2, padded, Z, 128), BF),
            pltpu.VMEM((BLOCK_PAIRS, 2, STEM_X, Z, 256), BF),
            pltpu.VMEM((2, TX // 2 * Z, 128), F32),
        ],
        compiler_params=pltpu.CompilerParams(vmem_limit_bytes=60 * 2**20),
        name="convnet",
    )(
        tiles, place, first,
        second_kernel.reshape(27, C, C), third_kernel.reshape(27, C, C), head_weight, columns, blend,
    )


def solution(mesh):
    in_specs = (P(None, "gy", "gx"), P(), P(), P(), P())
    out_specs = P(None, None, "gy", "gx")
    return jax.shard_map(local, mesh=mesh, in_specs=in_specs, out_specs=out_specs, check_vma=False)
```

```python
import functools

import jax
import jax.numpy as jnp
import numpy as np
from jax import lax
from jax.experimental import pallas as pl
from jax.experimental.pallas import tpu as pltpu
from jax.sharding import PartitionSpec as P

R = 2
C = 64
Z = 16
TY = 8
TX = 128
BF = jnp.bfloat16
F32 = jnp.float32
MESH = pl.DeviceIdType.MESH


STEM_PAIRS = 6
INNER_PAIRS = 5
BLOCK_PAIRS = 4
STEM_X = 68
INNER_X = 67
BLOCK_X = 66
XB = 16
AROUND = [(dy, dx) for dy in (-1, 0, 1) for dx in (-1, 0, 1) if (dy, dx) != (0, 0)]


def store_shifted(ref, pair, parity, value):
    count = value.shape[0]
    row = lax.broadcasted_iota(jnp.int32, (1, Z, 2 * C), 1)
    below = jnp.where(row == 0, 0.0, pltpu.roll(value, 1, axis=1))
    above = jnp.where(row == Z - 1, 0.0, pltpu.roll(value, Z - 1, axis=1))
    for shift, part in enumerate((below, value, above)):
        ref[shift, pair, parity, 0:count] = part.astype(BF)


def conv_operand(ref, pair, count):
    parts = []
    for shift in range(3):
        for offset in range(4):
            for k in range(2):
                first = offset // 2
                part = ref[shift, pair + k, offset % 2, first : first + count]
                parts.append(part.reshape(count * Z, 2 * C))
    return jnp.concatenate(parts, axis=1)


def build_conv_weights(kernel_ref, out_ref):
    zero = jnp.zeros((C, C), BF)
    for shift in range(3):
        for offset in range(4):
            for source in range(4):
                rows = ((shift * 4 + offset) * 4 + source) * C
                for qx in range(2):
                    blocks = []
                    for qy in range(2):
                        dx, dy = offset - qx, source - qy
                        inside = 0 <= dx < 3 and 0 <= dy < 3
                        blocks.append(kernel_ref[(shift * 3 + dy) * 3 + dx] if inside else zero)
                    out_ref[rows : rows + C, qx * 128 : qx * 128 + 128] = jnp.concatenate(blocks, axis=1)


def zero_columns(ref, columns):
    for pair in range(ref.shape[1]):
        for x in columns:
            for shift in range(3):
                ref[shift, pair, x % 2, x // 2] = jnp.zeros((Z, 2 * C), BF)


def coverage_of(position, length):
    total = jnp.zeros(position.shape, F32)
    for b in range(2 * R + 1):
        source = position - (b - R)
        total += jnp.where((source >= 0) & (source < length), float(R + 1 - abs(b - R)), 0.0)
    return total


def compute_kernel(
    tile_ref, place_hbm, first_ref, second_hbm, third_hbm, head_ref, columns_ref, blend_hbm,
    out_ref,
    place, second, third, blend,
    strips, rows_in, sides_in, edge_out, edge_in,
    taps, w1, w2, w3, wh, main, edge, qf, qb, stem, inner, pred, total,
    load_sem, send_sem, recv_sem, edge_send_sem, edge_recv_sem,
):
    gx, gy = lax.axis_index("gx"), lax.axis_index("gy")
    nx, ny = lax.axis_size("gx"), lax.axis_size("gy")
    at_low_x, at_high_x = gx == 0, gx == nx - 1
    at_low_y, at_high_y = gy == 0, gy == ny - 1

    def device(dy, dx):
        return (lax.rem(gx + dx + nx, nx), lax.rem(gy + dy + ny, ny))

    barrier = pltpu.get_barrier_semaphore()
    for dy, dx in AROUND:
        pl.semaphore_signal(barrier, inc=1, device_id=device(dy, dx), device_id_type=MESH)
    loads = []
    for n, (source, target) in enumerate(
        ((second_hbm, second), (third_hbm, third), (place_hbm, place), (blend_hbm, blend))
    ):
        loads.append(pltpu.make_async_copy(source, target, load_sem.at[n]))
        loads[-1].start()

    turned = tile_ref[...].astype(F32).reshape(Z * TY, TX).T
    strips[0] = turned[0:16].astype(BF)
    strips[1] = turned[TX - 16 : TX].astype(BF)
    pl.semaphore_wait(barrier, len(AROUND))
    copies = []
    for n, (dy, dx) in enumerate(AROUND):
        if dx == 0:
            source, target = tile_ref, rows_in.at[0 if dy == 1 else 1]
        else:
            source, target = strips.at[0 if dx == -1 else 1], sides_in.at[1 - dy, 0 if dx == 1 else 1]
        copies.append(
            pltpu.make_async_remote_copy(
                src_ref=source,
                dst_ref=target,
                send_sem=send_sem.at[n],
                recv_sem=recv_sem.at[n],
                device_id=device(dy, dx),
                device_id_type=MESH,
            )
        )
        copies[-1].start()

    for load in loads:
        load.wait()
    build_conv_weights(second, w2)
    build_conv_weights(third, w3)
    taps[...] = jnp.zeros((32, C), F32)
    for n in range(9):
        taps[3 * n : 3 * n + 3, :] = first_ref[n].astype(F32)
    tap = taps[...].astype(BF)
    nothing = jnp.zeros((32, C), BF)
    spread = jnp.concatenate(
        [jnp.concatenate([tap if i == q else nothing for i in range(4)], axis=1) for q in range(4)], axis=0
    )
    for pair in range(STEM_PAIRS):
        w1[pair] = jnp.dot(place[pair], spread, preferred_element_type=F32).astype(BF)
    for py in range(2):
        wh[py * C : py * C + C, :] = jnp.dot(
            head_ref[...], columns_ref[py], preferred_element_type=F32
        ).astype(BF)

    for copy in copies:
        copy.wait()

    lane8 = lax.broadcasted_iota(jnp.int32, (TY, TX), 1)
    lane128 = lax.broadcasted_iota(jnp.int32, (Z * TY, TX), 1)
    for buffer in (main, edge):
        buffer[0] = jnp.zeros((3 * TY, TX), F32)
        buffer[Z + 1] = jnp.zeros((3 * TY, TX), F32)
    right_ok = jnp.where(at_high_x, 0, 64)
    left_ok = jnp.where(at_low_x, 128, 64)
    between = jnp.zeros((TX - 32, Z * TY), F32)
    for ty in range(3):
        left, right = sides_in[ty, 0].astype(F32), sides_in[ty, 1].astype(F32)
        sides = jnp.concatenate([right, between, left], axis=0).T
        sides = jnp.where((lane128 < right_ok) | (lane128 >= left_ok), sides, 0.0)
        middle = (tile_ref[...] if ty == 1 else rows_in[ty // 2]).astype(F32)
        sides = sides.reshape(Z, TY, TX)
        if ty != 1:
            outside = at_low_y if ty == 0 else at_high_y
            middle, sides = jnp.where(outside, 0.0, middle), jnp.where(outside, 0.0, sides)
        main[1 : Z + 1, ty * TY : ty * TY + TY, :] = middle
        edge[1 : Z + 1, ty * TY : ty * TY + TY, :] = sides
    filler = jnp.zeros((128 - 9 * TY, TX), F32)
    for z in range(Z):
        middle = jnp.concatenate([main[z], main[z + 1], main[z + 2], filler], axis=0).T
        sides = jnp.concatenate([edge[z], edge[z + 1], edge[z + 2], filler], axis=0).T
        qf[pl.ds(8 * Z + z, TX, stride=Z), :] = middle
        qf[pl.ds(z, 8, stride=Z), :] = sides[120:128]
        qf[pl.ds(136 * Z + z, 8, stride=Z), :] = sides[0:8]

    def round_pair(m, carry):
        for parity in range(2):
            qb[parity, m] = qf[pl.ds(pl.multiple_of((2 * m + parity) * Z, Z), Z), :].astype(BF)
        return carry

    lax.fori_loop(0, 72, round_pair, 0, unroll=4)

    def stem_body(pair, carry):
        parts = []
        for offset in range(4):
            at = offset + 3
            parts.append(qb[at % 2, at // 2 : at // 2 + STEM_X].reshape(STEM_X * Z, 128))
        acc = jnp.dot(jnp.concatenate(parts, axis=1), w1[pair], preferred_element_type=F32)
        outside = (at_low_y & (pair == 0)) | (at_high_y & (pair == STEM_PAIRS - 1))
        acc = jnp.maximum(acc, 0.0) * jnp.where(outside, 0.0, 1.0)
        for qx in range(2):
            value = acc[:, qx * 128 : qx * 128 + 128].reshape(STEM_X, Z, 128)
            store_shifted(stem, pair, qx, value)
        return carry

    lax.fori_loop(0, STEM_PAIRS, stem_body, 0)

    @pl.when(at_low_x)
    def _():
        zero_columns(stem, range(4))

    @pl.when(at_high_x)
    def _():
        zero_columns(stem, range(132, 136))

    upper = (lax.broadcasted_iota(jnp.int32, (1, 128), 1) // C).astype(jnp.int32)

    def inner_body(pair, carry):
        acc = jnp.dot(conv_operand(stem, pair, INNER_X), w2[...], preferred_element_type=F32)
        low = jnp.where(at_low_y & (pair == 0), 0, -1)
        high = jnp.where(at_high_y & (pair == INNER_PAIRS - 1), 1, -1)
        keep = jnp.where((upper == low) | (upper == high), 0.0, 1.0)
        for qx in range(2):
            value = jnp.maximum(acc[:, qx * 128 : qx * 128 + 128], 0.0) * keep
            store_shifted(inner, pair, qx, value.reshape(INNER_X, Z, 128))
        return carry

    lax.fori_loop(0, INNER_PAIRS, inner_body, 0)

    @pl.when(at_low_x)
    def _():
        zero_columns(inner, range(3))

    @pl.when(at_high_x)
    def _():
        zero_columns(inner, range(131, 134))

    def block_body(pair):
        acc = jnp.dot(conv_operand(inner, pair, BLOCK_X), w3[...], preferred_element_type=F32)
        for qx in range(2):
            old = stem[1, pair + 1, qx, 1 : 1 + BLOCK_X].reshape(BLOCK_X * Z, 128).astype(F32)
            value = jnp.maximum(acc[:, qx * 128 : qx * 128 + 128] + old, 0.0).astype(BF)
            logits = jnp.dot(value, wh[...], preferred_element_type=F32)
            pred[pair, qx] = jnp.tanh(logits).astype(BF).reshape(BLOCK_X, Z, 256)

        @pl.when(at_low_x)
        def _():
            for parity in range(2):
                pred[pair, parity, 0] = jnp.zeros((Z, 256), BF)

        @pl.when(at_high_x)
        def _():
            for parity in range(2):
                pred[pair, parity, BLOCK_X - 1] = jnp.zeros((Z, 256), BF)

    lanes = lax.broadcasted_iota(jnp.int32, (1, Z, 128), 2)

    def blend_rows(targets, first):
        def body(step, carry):
            j = step * XB
            for qx in range(2):
                operands = []
                for target in targets:
                    for half in range(2):
                        chosen = None
                        for n, a in enumerate((0, 1, 2) if half == 0 else (2, 3, 4)):
                            at = qx - a + 4
                            for k in range(3):
                                pair = target + k - 1
                                if not 0 <= pair < BLOCK_PAIRS:
                                    continue
                                part = pred[pair, at % 2, pl.ds(j + at // 2, XB), :, half * 128 : half * 128 + 128]
                                if chosen is None:
                                    chosen = part
                                else:
                                    chosen = jnp.where(lanes >= GROUP_START[half][n * 3 + k], part, chosen)
                        operands.append(chosen.reshape(XB * Z, 128))
                added = jnp.dot(
                    jnp.concatenate(operands, axis=1),
                    blend[first : first + 256 * len(targets), :],
                    preferred_element_type=F32,
                )
                total[qx, pl.ds(pl.multiple_of(j * Z, XB * Z), XB * Z), :] = added
            return carry

        lax.fori_loop(0, TX // 2 // XB, body, 0)

    def turned_total(z):
        even = total[0, pl.ds(z, TX // 2, stride=Z), :]
        odd = total[1, pl.ds(z, TX // 2, stride=Z), :]
        return jnp.stack([even, odd], axis=1).reshape(TX, 128).T

    def outer_body(step, carry):
        block_body(step * (BLOCK_PAIRS - 1))
        return carry

    lax.fori_loop(0, 2, outer_body, 0)
    blend_rows((-1, BLOCK_PAIRS), 0)
    for z in range(Z):
        both = turned_total(z)
        for side in range(2):
            edge_out[side, z] = both[24 + 8 * side : 32 + 8 * side]
    edges = []
    for side, dy in enumerate((-1, 1)):
        edges.append(
            pltpu.make_async_remote_copy(
                src_ref=edge_out.at[side],
                dst_ref=edge_in.at[side],
                send_sem=edge_send_sem.at[side],
                recv_sem=edge_recv_sem.at[side],
                device_id=device(dy, 0),
                device_id_type=MESH,
            )
        )
        edges[-1].start()

    def middle_body(step, carry):
        block_body(step + 1)
        return carry

    lax.fori_loop(0, BLOCK_PAIRS - 2, middle_body, 0)
    blend_rows(tuple(range(BLOCK_PAIRS)), 512)

    y8 = lax.broadcasted_iota(jnp.int32, (TY, TX), 0)
    scale = 0.5 / (coverage_of(gy * TY + y8, ny * TY) * coverage_of(gx * TX + lane8, nx * TX))
    from_above = (y8 < 2) & (gy > 0)
    from_below = (y8 >= TY - 2) & (gy < ny - 1)
    for copy in edges:
        copy.wait()
    for z in range(Z):
        both = turned_total(z)
        below, above = edge_in[0, z], edge_in[1, z]
        for c in range(3):
            added = both[c * TY : c * TY + TY, :]
            added += jnp.where(from_above, above if c == 0 else pltpu.roll(above, TY - 2 * c, axis=0), 0.0)
            added += jnp.where(from_below, pltpu.roll(below, TY - 2 - 2 * c, axis=0), 0.0)
            out_ref[c, z] = 0.5 + added * scale


def lane_plan():
    plan, starts = [], []
    for half in range(2):
        lanes, begin = [], []
        for a in (0, 1, 2) if half == 0 else (2, 3, 4):
            for k in range(3):
                begin.append(len(lanes))
                for py in range(2):
                    if a == 2 and py != half:
                        continue
                    for b in range(5):
                        if -((py + b - 4) // 2) == k:
                            lanes += [(a, py, b, c) for c in range(3)]
        plan.append(lanes)
        starts.append(begin)
    return plan, starts


LANES, GROUP_START = lane_plan()


def constants():
    place = np.zeros((STEM_PAIRS, 4, 128, 128), np.float32)
    for pair in range(STEM_PAIRS):
        for qx in range(2):
            for qy in range(2):
                for dz in range(3):
                    for dy in range(3):
                        for dx in range(3):
                            y = 5 + 2 * pair + qy + dy
                            place[pair, qx + dx, dz * 24 + y, (qx * 2 + qy) * 32 + (dz * 3 + dy) * 3 + dx] = 1
    columns = np.zeros((2, 75, 256), np.float32)
    targets = (-1, BLOCK_PAIRS) + tuple(range(BLOCK_PAIRS))
    blend = np.zeros((len(targets), 256, 128), np.float32)
    for half in range(2):
        for n, (a, py, b, c) in enumerate(LANES[half]):
            columns[py, (a * 5 + b) * 3 + c, half * 128 + n] = 0.5
            weight = (R + 1 - abs(a - R)) * (R + 1 - abs(b - R))
            for i, target in enumerate(targets):
                if not 0 <= target + 1 - (py + b) // 2 < BLOCK_PAIRS:
                    continue
                qy = (py + b) % 2
                if target < 0:
                    lane = 24 + 2 * c + qy
                elif target == BLOCK_PAIRS:
                    lane = 32 + 2 * c + qy
                else:
                    lane = c * TY + 2 * target + qy
                blend[i, half * 128 + n, lane] = weight
    return (
        jnp.asarray(place.reshape(STEM_PAIRS, 512, 128), BF),
        jnp.asarray(columns, BF),
        jnp.asarray(blend.reshape(-1, 128), BF),
    )


def local(intensity, first_kernel, second_kernel, third_kernel, head_weight):
    place, columns, blend = constants()
    vmem = pl.BlockSpec(memory_space=pltpu.VMEM)
    hbm = pl.BlockSpec(memory_space=pl.ANY)
    return pl.pallas_call(
        compute_kernel,
        out_shape=jax.ShapeDtypeStruct((3, Z, TY, TX), F32),
        in_specs=[vmem, hbm, vmem, hbm, hbm, vmem, vmem, hbm],
        out_specs=vmem,
        scratch_shapes=[
            pltpu.VMEM(place.shape, BF),
            pltpu.VMEM((27, C, C), BF),
            pltpu.VMEM((27, C, C), BF),
            pltpu.VMEM(blend.shape, BF),
            pltpu.VMEM((2, 16, Z * TY), BF),
            pltpu.VMEM((2, Z, TY, TX), BF),
            pltpu.VMEM((3, 2, 16, Z * TY), BF),
            pltpu.VMEM((2, Z, TY, TX), F32),
            pltpu.VMEM((2, Z, TY, TX), F32),
            pltpu.VMEM((32, C), F32),
            pltpu.VMEM((STEM_PAIRS, 512, 256), BF),
            pltpu.VMEM((3072, 256), BF),
            pltpu.VMEM((3072, 256), BF),
            pltpu.VMEM((128, 256), BF),
            pltpu.VMEM((Z + 2, 3 * TY, TX), F32),
            pltpu.VMEM((Z + 2, 3 * TY, TX), F32),
            pltpu.VMEM((144 * Z, 128), F32),
            pltpu.VMEM((2, 72, Z, 128), BF),
            pltpu.VMEM((3, STEM_PAIRS, 2, STEM_X, Z, 128), BF),
            pltpu.VMEM((3, INNER_PAIRS, 2, INNER_X, Z, 128), BF),
            pltpu.VMEM((BLOCK_PAIRS, 2, BLOCK_X, Z, 256), BF),
            pltpu.VMEM((2, TX // 2 * Z, 128), F32),
            pltpu.SemaphoreType.DMA((4,)),
            pltpu.SemaphoreType.DMA((8,)),
            pltpu.SemaphoreType.DMA((8,)),
            pltpu.SemaphoreType.DMA((2,)),
            pltpu.SemaphoreType.DMA((2,)),
        ],
        compiler_params=pltpu.CompilerParams(
            collective_id=0, has_side_effects=True, vmem_limit_bytes=56 * 2**20
        ),
        name="convnet",
    )(
        intensity, place, first_kernel.reshape(9, 3, C),
        second_kernel.reshape(27, C, C), third_kernel.reshape(27, C, C), head_weight, columns, blend,
    )


def solution(mesh):
    in_specs = (P(None, "gy", "gx"), P(), P(), P(), P())
    out_specs = P(None, None, "gy", "gx")
    return jax.shard_map(local, mesh=mesh, in_specs=in_specs, out_specs=out_specs, check_vma=False)
```

```python
import functools

import jax
import jax.numpy as jnp
import numpy as np
from jax import lax
from jax.experimental import pallas as pl
from jax.experimental.pallas import tpu as pltpu
from jax.sharding import PartitionSpec as P

R = 2
C = 64
Z = 16
TY = 8
TX = 128
BF = jnp.bfloat16
F32 = jnp.float32
MESH = pl.DeviceIdType.MESH


STEM_PAIRS = 6
INNER_PAIRS = 5
BLOCK_PAIRS = 4
STEM_X = 68
INNER_X = 67
BLOCK_X = 66
XB = 32
AROUND = [(dy, dx) for dy in (-1, 0, 1) for dx in (-1, 0, 1) if (dy, dx) != (0, 0)]


def conv_rows(ref, pair, count, near, far):
    def operand(offsets):
        parts = []
        for offset in offsets:
            for k in range(2):
                part = ref[pair + k, offset % 2, offset // 2 : offset // 2 + count]
                parts.append(part.reshape(count * Z, 2 * C))
        return jnp.concatenate(parts, axis=1)

    row = lax.broadcasted_iota(jnp.int32, (1, Z, 2 * C), 1)
    third = jnp.dot(operand(range(4)), far[...], preferred_element_type=F32)
    out = []
    for qx in range(2):
        both = jnp.dot(operand(range(qx, qx + 3)), near[...], preferred_element_type=F32)
        below = both[:, :128].reshape(count, Z, 128)
        above = third[:, qx * 128 : qx * 128 + 128].reshape(count, Z, 128)
        total = both[:, 128:].reshape(count, Z, 128)
        total += jnp.where(row == 0, 0.0, pltpu.roll(below, 1, axis=1))
        total += jnp.where(row == Z - 1, 0.0, pltpu.roll(above, Z - 1, axis=1))
        out.append(total)
    return out


def build_conv_weights(kernel_ref, near, far):
    zero = jnp.zeros((C, C), BF)

    def band(dz, dx, source):
        blocks = []
        for qy in range(2):
            dy = source - qy
            inside = 0 <= dx < 3 and 0 <= dy < 3
            blocks.append(kernel_ref[(dz * 3 + dy) * 3 + dx] if inside else zero)
        return jnp.concatenate(blocks, axis=1)

    for source in range(4):
        for dx in range(3):
            rows = (dx * 4 + source) * C
            for dz in range(2):
                near[rows : rows + C, dz * 128 : dz * 128 + 128] = band(dz, dx, source)
        for offset in range(4):
            rows = (offset * 4 + source) * C
            for qx in range(2):
                far[rows : rows + C, qx * 128 : qx * 128 + 128] = band(2, offset - qx, source)


def zero_columns(ref, columns):
    for pair in range(ref.shape[0]):
        for x in columns:
            ref[pair, x % 2, x // 2] = jnp.zeros((Z, 2 * C), BF)


def coverage_of(position, length):
    total = jnp.zeros(position.shape, F32)
    for b in range(2 * R + 1):
        source = position - (b - R)
        total += jnp.where((source >= 0) & (source < length), float(R + 1 - abs(b - R)), 0.0)
    return total


def compute_kernel(
    tile_hbm, place_hbm, first_hbm, second_hbm, third_hbm, head_hbm, columns_hbm, blend_hbm,
    out_ref,
    tile_ref, place, first_ref, second, third, head_ref, columns_ref, blend,
    strips, rows_in, sides_in, edge_out, edge_in,
    taps, w1, near2, far2, near3, far3, wh, main, edge, qf, qb, stem, inner, pred, total,
    load_sem, send_sem, recv_sem, edge_send_sem, edge_recv_sem,
):
    gx, gy = lax.axis_index("gx"), lax.axis_index("gy")
    nx, ny = lax.axis_size("gx"), lax.axis_size("gy")
    at_low_x, at_high_x = gx == 0, gx == nx - 1
    at_low_y, at_high_y = gy == 0, gy == ny - 1

    def device(dy, dx):
        return (lax.rem(gx + dx + nx, nx), lax.rem(gy + dy + ny, ny))

    barrier = pltpu.get_barrier_semaphore()
    for dy, dx in AROUND:
        pl.semaphore_signal(barrier, inc=1, device_id=device(dy, dx), device_id_type=MESH)
    loads = []
    for n, (source, target) in enumerate(
        (
            (tile_hbm, tile_ref), (second_hbm, second), (third_hbm, third), (first_hbm, first_ref),
            (place_hbm, place), (head_hbm, head_ref), (columns_hbm, columns_ref), (blend_hbm, blend),
        )
    ):
        loads.append(pltpu.make_async_copy(source, target, load_sem.at[n]))
        loads[-1].start()

    loads[0].wait()
    turned = tile_ref[...].astype(F32).reshape(Z * TY, TX).T
    strips[0] = turned[0:16].astype(BF)
    strips[1] = turned[TX - 16 : TX].astype(BF)
    pl.semaphore_wait(barrier, len(AROUND))
    copies = []
    for n, (dy, dx) in enumerate(AROUND):
        if dx == 0:
            source, target = tile_ref, rows_in.at[0 if dy == 1 else 1]
        else:
            source, target = strips.at[0 if dx == -1 else 1], sides_in.at[1 - dy, 0 if dx == 1 else 1]
        copies.append(
            pltpu.make_async_remote_copy(
                src_ref=source,
                dst_ref=target,
                send_sem=send_sem.at[n],
                recv_sem=recv_sem.at[n],
                device_id=device(dy, dx),
                device_id_type=MESH,
            )
        )
        copies[-1].start()

    for load in loads[1:]:
        load.wait()
    build_conv_weights(second, near2, far2)
    build_conv_weights(third, near3, far3)
    taps[...] = jnp.zeros((32, C), F32)
    for n in range(9):
        taps[3 * n : 3 * n + 3, :] = first_ref[n].astype(F32)
    tap = taps[...].astype(BF)
    nothing = jnp.zeros((32, C), BF)
    spread = jnp.concatenate(
        [jnp.concatenate([tap if i == q else nothing for i in range(4)], axis=1) for q in range(4)], axis=0
    )
    for pair in range(STEM_PAIRS):
        w1[pair] = jnp.dot(place[pair], spread, preferred_element_type=F32).astype(BF)
    for py in range(2):
        wh[py * C : py * C + C, :] = jnp.dot(
            head_ref[...], columns_ref[py], preferred_element_type=F32
        ).astype(BF)

    for copy in copies:
        copy.wait()

    lane8 = lax.broadcasted_iota(jnp.int32, (TY, TX), 1)
    lane128 = lax.broadcasted_iota(jnp.int32, (Z * TY, TX), 1)
    for buffer in (main, edge):
        for half in range(2):
            buffer[half, 0] = jnp.zeros((2 * TY, TX), F32)
            buffer[half, Z + 1] = jnp.zeros((2 * TY, TX), F32)
    right_ok = jnp.where(at_high_x, 0, 64)
    left_ok = jnp.where(at_low_x, 128, 64)
    between = jnp.zeros((TX - 32, Z * TY), F32)
    middles, sideways = [], []
    for ty in range(3):
        left, right = sides_in[ty, 0].astype(F32), sides_in[ty, 1].astype(F32)
        sides = jnp.concatenate([right, between, left], axis=0).T
        sides = jnp.where((lane128 < right_ok) | (lane128 >= left_ok), sides, 0.0)
        middle = (tile_ref[...] if ty == 1 else rows_in[ty // 2]).astype(F32)
        sides = sides.reshape(Z, TY, TX)
        if ty != 1:
            outside = at_low_y if ty == 0 else at_high_y
            middle, sides = jnp.where(outside, 0.0, middle), jnp.where(outside, 0.0, sides)
        middles.append(middle)
        sideways.append(sides)
    row8 = lax.broadcasted_iota(jnp.int32, (1, TY, TX), 1)
    end = lax.broadcasted_iota(jnp.int32, (1, TY, TX), 2) == TX - 1
    for part in range(2):
        if part == 0:
            middle, sides = middles[1], sideways[1]
        else:
            middle = jnp.where(row8 < 4, middles[2], middles[0])
            sides = jnp.where(row8 < 4, sideways[2], sideways[0])
        next_middle, next_sides = pltpu.roll(middle, TX - 1, axis=2), pltpu.roll(sides, TX - 1, axis=2)
        rows = slice(part * TY, part * TY + TY)
        main[0, 1 : Z + 1, rows, :] = middle
        main[1, 1 : Z + 1, rows, :] = jnp.where(end, next_sides, next_middle)
        edge[0, 1 : Z + 1, rows, :] = sides
        edge[1, 1 : Z + 1, rows, :] = jnp.where(end, next_middle, next_sides)
    filler = jnp.zeros((2 * TY, TX), F32)
    for z in range(Z):
        turns = []
        for buffer in (main, edge):
            parts = []
            for half in range(2):
                parts += [buffer[half, z], buffer[half, z + 1], buffer[half, z + 2], filler]
            turns.append(jnp.concatenate(parts, axis=0).T)
        middle, sides = turns
        qf[pl.ds(8 * Z + z, TX, stride=Z), :] = middle
        qf[pl.ds(z, 8, stride=Z), :] = sides[120:128]
        qf[pl.ds(136 * Z + z, 8, stride=Z), :] = sides[0:8]

    for m in range(STEM_X + 1):
        qb[m] = qf[(2 * m + 3) * Z : (2 * m + 4) * Z, :].astype(BF)

    def stem_body(pair, carry):
        parts = [qb[k : k + STEM_X].reshape(STEM_X * Z, 128) for k in range(2)]
        acc = jnp.dot(jnp.concatenate(parts, axis=1), w1[pair], preferred_element_type=F32)
        outside = (at_low_y & (pair == 0)) | (at_high_y & (pair == STEM_PAIRS - 1))
        acc = jnp.maximum(acc, 0.0) * jnp.where(outside, 0.0, 1.0)
        for qx in range(2):
            value = acc[:, qx * 128 : qx * 128 + 128].reshape(STEM_X, Z, 128)
            stem[pair, qx] = value.astype(BF)
        return carry

    lax.fori_loop(0, STEM_PAIRS, stem_body, 0)

    @pl.when(at_low_x)
    def _():
        zero_columns(stem, range(4))

    @pl.when(at_high_x)
    def _():
        zero_columns(stem, range(132, 136))

    upper = (lax.broadcasted_iota(jnp.int32, (1, 1, 128), 2) // C)

    def inner_body(pair, carry):
        sums = conv_rows(stem, pair, INNER_X, near2, far2)
        low = jnp.where(at_low_y & (pair == 0), 0, -1)
        high = jnp.where(at_high_y & (pair == INNER_PAIRS - 1), 1, -1)
        keep = jnp.where((upper == low) | (upper == high), 0.0, 1.0)
        for qx in range(2):
            inner[pair, qx] = (jnp.maximum(sums[qx], 0.0) * keep).astype(BF)
        return carry

    lax.fori_loop(0, INNER_PAIRS, inner_body, 0)

    @pl.when(at_low_x)
    def _():
        zero_columns(inner, range(3))

    @pl.when(at_high_x)
    def _():
        zero_columns(inner, range(131, 134))

    def block_body(pair):
        sums = conv_rows(inner, pair, BLOCK_X, near3, far3)
        for qx in range(2):
            old = stem[pair + 1, qx, 1 : 1 + BLOCK_X].astype(F32)
            value = jnp.maximum(sums[qx] + old, 0.0).astype(BF).reshape(BLOCK_X * Z, 128)
            logits = jnp.dot(value, wh[...], preferred_element_type=F32)
            pred[pair, qx] = jnp.tanh(logits).astype(BF).reshape(BLOCK_X, Z, 256)

        @pl.when(at_low_x)
        def _():
            for parity in range(2):
                pred[pair, parity, 0] = jnp.zeros((Z, 256), BF)

        @pl.when(at_high_x)
        def _():
            for parity in range(2):
                pred[pair, parity, BLOCK_X - 1] = jnp.zeros((Z, 256), BF)

    lanes = lax.broadcasted_iota(jnp.int32, (1, Z, 128), 2)

    def blend_rows(pairs, first, more):
        def body(step, carry):
            j = step * XB
            for qx in range(2):
                operands = []
                for pair in pairs:
                    for half in range(2):
                        chosen = None
                        for n, a in enumerate((0, 1, 2) if half == 0 else (2, 3, 4)):
                            at = qx - a + 4
                            part = pred[pair, at % 2, pl.ds(j + at // 2, XB), :, half * 128 : half * 128 + 128]
                            chosen = part if n == 0 else jnp.where(lanes >= A_START[half][n], part, chosen)
                        operands.append(chosen.reshape(XB * Z, 128))
                added = jnp.dot(
                    jnp.concatenate(operands, axis=1),
                    blend[first : first + 256 * len(pairs), :],
                    preferred_element_type=F32,
                )
                rows = pl.ds(pl.multiple_of(j * Z, XB * Z), XB * Z)
                total[qx, rows, :] = total[qx, rows, :] + added if more else added
            return carry

        lax.fori_loop(0, TX // 2 // XB, body, 0)

    def turned_total(z):
        even = total[0, pl.ds(z, TX // 2, stride=Z), :]
        odd = total[1, pl.ds(z, TX // 2, stride=Z), :]
        return jnp.stack([even, odd], axis=1).reshape(TX, 128).T

    def outer_body(step, carry):
        block_body(step * (BLOCK_PAIRS - 1))
        return carry

    lax.fori_loop(0, 2, outer_body, 0)
    blend_rows((0, BLOCK_PAIRS - 1), 0, False)
    for z in range(Z):
        both = turned_total(z)
        for side in range(2):
            edge_out[side, z] = both[24 + 8 * side : 32 + 8 * side]
    edges = []
    for side, dy in enumerate((-1, 1)):
        edges.append(
            pltpu.make_async_remote_copy(
                src_ref=edge_out.at[side],
                dst_ref=edge_in.at[side],
                send_sem=edge_send_sem.at[side],
                recv_sem=edge_recv_sem.at[side],
                device_id=device(dy, 0),
                device_id_type=MESH,
            )
        )
        edges[-1].start()

    def middle_body(step, carry):
        block_body(step + 1)
        return carry

    lax.fori_loop(0, BLOCK_PAIRS - 2, middle_body, 0)
    blend_rows(tuple(range(1, BLOCK_PAIRS - 1)), 512, True)

    y8 = lax.broadcasted_iota(jnp.int32, (TY, TX), 0)
    scale = 0.5 / (coverage_of(gy * TY + y8, ny * TY) * coverage_of(gx * TX + lane8, nx * TX))
    from_above = (y8 < 2) & (gy > 0)
    from_below = (y8 >= TY - 2) & (gy < ny - 1)
    for copy in edges:
        copy.wait()
    for z in range(Z):
        both = turned_total(z)
        below, above = edge_in[0, z], edge_in[1, z]
        for c in range(3):
            added = both[c * TY : c * TY + TY, :]
            added += jnp.where(from_above, above if c == 0 else pltpu.roll(above, TY - 2 * c, axis=0), 0.0)
            added += jnp.where(from_below, pltpu.roll(below, TY - 2 - 2 * c, axis=0), 0.0)
            out_ref[c, z] = 0.5 + added * scale


def lane_plan():
    plan, starts = [], []
    for half in range(2):
        lanes, begin = [], []
        for a in (0, 1, 2) if half == 0 else (2, 3, 4):
            begin.append(len(lanes))
            for py in range(2):
                if a == 2 and py != half:
                    continue
                lanes += [(a, py, b, c) for b in range(5) for c in range(3)]
        plan.append(lanes)
        starts.append(begin)
    return plan, starts


LANES, A_START = lane_plan()


def constants():
    place = np.zeros((STEM_PAIRS, 4, 64, 128), np.float32)
    for pair in range(STEM_PAIRS):
        for qx in range(2):
            for qy in range(2):
                for dz in range(3):
                    for dy in range(3):
                        for dx in range(3):
                            y = (2 * pair + qy + dy - 3) % 16
                            place[pair, qx + dx, dz * 16 + y, (qx * 2 + qy) * 32 + (dz * 3 + dy) * 3 + dx] = 1
    columns = np.zeros((2, 75, 256), np.float32)
    pairs = (0, BLOCK_PAIRS - 1) + tuple(range(1, BLOCK_PAIRS - 1))
    blend = np.zeros((len(pairs), 256, 128), np.float32)
    for half in range(2):
        for n, (a, py, b, c) in enumerate(LANES[half]):
            columns[py, (a * 5 + b) * 3 + c, half * 128 + n] = 0.5
            for i, pair in enumerate(pairs):
                y = 2 * pair + py + b - R
                if y < 0:
                    lane = 24 + 2 * c + y + R
                elif y >= TY:
                    lane = 32 + 2 * c + y - TY
                else:
                    lane = c * TY + y
                blend[i, half * 128 + n, lane] = (R + 1 - abs(a - R)) * (R + 1 - abs(b - R))
    return (
        jnp.asarray(place.reshape(STEM_PAIRS, 256, 128), BF),
        jnp.asarray(columns, BF),
        jnp.asarray(blend.reshape(-1, 128), BF),
    )


def local(intensity, first_kernel, second_kernel, third_kernel, head_weight):
    place, columns, blend = constants()
    vmem = pl.BlockSpec(memory_space=pltpu.VMEM)
    hbm = pl.BlockSpec(memory_space=pltpu.HBM)
    return pl.pallas_call(
        compute_kernel,
        out_shape=jax.ShapeDtypeStruct((3, Z, TY, TX), F32),
        in_specs=[hbm] * 8,
        out_specs=vmem,
        scratch_shapes=[
            pltpu.VMEM(intensity.shape, BF),
            pltpu.VMEM(place.shape, BF),
            pltpu.VMEM((9, 3, C), BF),
            pltpu.VMEM((27, C, C), BF),
            pltpu.VMEM((27, C, C), BF),
            pltpu.VMEM(head_weight.shape, BF),
            pltpu.VMEM(columns.shape, BF),
            pltpu.VMEM(blend.shape, BF),
            pltpu.VMEM((2, 16, Z * TY), BF),
            pltpu.VMEM((2, Z, TY, TX), BF),
            pltpu.VMEM((3, 2, 16, Z * TY), BF),
            pltpu.VMEM((2, Z, TY, TX), F32),
            pltpu.VMEM((2, Z, TY, TX), F32),
            pltpu.VMEM((32, C), F32),
            pltpu.VMEM((STEM_PAIRS, 256, 256), BF),
            pltpu.VMEM((768, 256), BF),
            pltpu.VMEM((1024, 256), BF),
            pltpu.VMEM((768, 256), BF),
            pltpu.VMEM((1024, 256), BF),
            pltpu.VMEM((128, 256), BF),
            pltpu.VMEM((2, Z + 2, 2 * TY, TX), F32),
            pltpu.VMEM((2, Z + 2, 2 * TY, TX), F32),
            pltpu.VMEM((144 * Z, 128), F32),
            pltpu.VMEM((STEM_X + 1, Z, 128), BF),
            pltpu.VMEM((STEM_PAIRS, 2, STEM_X, Z, 128), BF),
            pltpu.VMEM((INNER_PAIRS, 2, INNER_X, Z, 128), BF),
            pltpu.VMEM((BLOCK_PAIRS, 2, BLOCK_X, Z, 256), BF),
            pltpu.VMEM((2, TX // 2 * Z, 128), F32),
            pltpu.SemaphoreType.DMA((8,)),
            pltpu.SemaphoreType.DMA((8,)),
            pltpu.SemaphoreType.DMA((8,)),
            pltpu.SemaphoreType.DMA((2,)),
            pltpu.SemaphoreType.DMA((2,)),
        ],
        compiler_params=pltpu.CompilerParams(
            collective_id=0, has_side_effects=True, vmem_limit_bytes=56 * 2**20
        ),
        name="convnet",
    )(
        intensity, place, first_kernel.reshape(9, 3, C),
        second_kernel.reshape(27, C, C), third_kernel.reshape(27, C, C), head_weight, columns, blend,
    )


def solution(mesh):
    in_specs = (P(None, "gy", "gx"), P(), P(), P(), P())
    out_specs = P(None, None, "gy", "gx")
    return jax.shard_map(local, mesh=mesh, in_specs=in_specs, out_specs=out_specs, check_vma=False)
```

```python
import functools

import jax
import jax.numpy as jnp
import numpy as np
from jax import lax
from jax.experimental import pallas as pl
from jax.experimental.pallas import tpu as pltpu
from jax.sharding import PartitionSpec as P

R = 2
C = 64
Z = 16
TY = 8
TX = 128
BF = jnp.bfloat16
F32 = jnp.float32
MESH = pl.DeviceIdType.MESH


STEM_PAIRS = 6
INNER_PAIRS = 5
BLOCK_PAIRS = 4
STEM_X = 68
INNER_X = 67
BLOCK_X = 66
XB = 32
STEM_OWN, STEM_SIDES = ((3, 65),), ((0, 3), (65, STEM_X))
INNER_OWN, INNER_SIDES = ((3, 64),), ((0, 3), (64, INNER_X))
AROUND = [(dy, dx) for dy in (-1, 0, 1) for dx in (-1, 0, 1) if (dy, dx) != (0, 0)]


def join(parts):
    return parts[0] if len(parts) == 1 else jnp.concatenate(parts, axis=0)


def conv_rows(ref, pair, spans, near, far):
    count = sum(end - begin for begin, end in spans)

    def operand(offsets):
        parts = []
        for offset in offsets:
            for k in range(2):
                at = offset // 2
                part = join([ref[pair + k, offset % 2, begin + at : end + at] for begin, end in spans])
                parts.append(part.reshape(count * Z, 2 * C))
        return jnp.concatenate(parts, axis=1)

    row = lax.broadcasted_iota(jnp.int32, (1, Z, 2 * C), 1)
    third = jnp.dot(operand(range(4)), far[...], preferred_element_type=F32)
    out = []
    for qx in range(2):
        both = jnp.dot(operand(range(qx, qx + 3)), near[...], preferred_element_type=F32)
        below = both[:, :128].reshape(count, Z, 128)
        above = third[:, qx * 128 : qx * 128 + 128].reshape(count, Z, 128)
        total = both[:, 128:].reshape(count, Z, 128)
        total += jnp.where(row == 0, 0.0, pltpu.roll(below, 1, axis=1))
        total += jnp.where(row == Z - 1, 0.0, pltpu.roll(above, Z - 1, axis=1))
        out.append(total)
    return out


def build_conv_weights(kernel_ref, near, far):
    zero = jnp.zeros((C, C), BF)

    def band(dz, dx, source):
        blocks = []
        for qy in range(2):
            dy = source - qy
            inside = 0 <= dx < 3 and 0 <= dy < 3
            blocks.append(kernel_ref[(dz * 3 + dy) * 3 + dx] if inside else zero)
        return jnp.concatenate(blocks, axis=1)

    for source in range(4):
        for dx in range(3):
            rows = (dx * 4 + source) * C
            for dz in range(2):
                near[rows : rows + C, dz * 128 : dz * 128 + 128] = band(dz, dx, source)
        for offset in range(4):
            rows = (offset * 4 + source) * C
            for qx in range(2):
                far[rows : rows + C, qx * 128 : qx * 128 + 128] = band(2, offset - qx, source)


def zero_columns(ref, columns):
    for pair in range(ref.shape[0]):
        for x in columns:
            ref[pair, x % 2, x // 2] = jnp.zeros((Z, 2 * C), BF)


def coverage_of(position, length):
    total = jnp.zeros(position.shape, F32)
    for b in range(2 * R + 1):
        source = position - (b - R)
        total += jnp.where((source >= 0) & (source < length), float(R + 1 - abs(b - R)), 0.0)
    return total


def compute_kernel(
    tile_hbm, place_hbm, first_hbm, second_hbm, third_hbm, head_hbm, columns_hbm, blend_hbm,
    out_ref,
    tile_ref, place, first_ref, second, third, head_ref, columns_ref, blend,
    strips, rows_in, sides_in, edge_out, edge_in,
    taps, w1, near2, far2, near3, far3, wh, main, edge, qf, qb, stem, inner, pred, total,
    load_sem, send_sem, recv_sem, edge_send_sem, edge_recv_sem,
):
    gx, gy = lax.axis_index("gx"), lax.axis_index("gy")
    nx, ny = lax.axis_size("gx"), lax.axis_size("gy")
    at_low_x, at_high_x = gx == 0, gx == nx - 1
    at_low_y, at_high_y = gy == 0, gy == ny - 1

    def device(dy, dx):
        return (lax.rem(gx + dx + nx, nx), lax.rem(gy + dy + ny, ny))

    barrier = pltpu.get_barrier_semaphore()
    for dy, dx in AROUND:
        pl.semaphore_signal(barrier, inc=1, device_id=device(dy, dx), device_id_type=MESH)
    loads = []
    for n, (source, target) in enumerate(
        (
            (tile_hbm, tile_ref), (second_hbm, second), (third_hbm, third), (first_hbm, first_ref),
            (place_hbm, place), (head_hbm, head_ref), (columns_hbm, columns_ref), (blend_hbm, blend),
        )
    ):
        loads.append(pltpu.make_async_copy(source, target, load_sem.at[n]))
        loads[-1].start()

    loads[0].wait()
    turned = tile_ref[...].astype(F32).reshape(Z * TY, TX).T
    strips[0] = turned[0:16].astype(BF)
    strips[1] = turned[TX - 16 : TX].astype(BF)
    pl.semaphore_wait(barrier, len(AROUND))
    copies = []
    for n, (dy, dx) in enumerate(AROUND):
        if dx == 0:
            source, target = tile_ref, rows_in.at[0 if dy == 1 else 1]
        else:
            source, target = strips.at[0 if dx == -1 else 1], sides_in.at[1 - dy, 0 if dx == 1 else 1]
        copies.append(
            pltpu.make_async_remote_copy(
                src_ref=source,
                dst_ref=target,
                send_sem=send_sem.at[n],
                recv_sem=recv_sem.at[n],
                device_id=device(dy, dx),
                device_id_type=MESH,
            )
        )
        copies[-1].start()

    for load in loads[1:]:
        load.wait()
    build_conv_weights(second, near2, far2)
    build_conv_weights(third, near3, far3)
    taps[...] = jnp.zeros((32, C), F32)
    for n in range(9):
        taps[3 * n : 3 * n + 3, :] = first_ref[n].astype(F32)
    tap = taps[...].astype(BF)
    nothing = jnp.zeros((32, C), BF)
    spread = jnp.concatenate(
        [jnp.concatenate([tap if i == q else nothing for i in range(4)], axis=1) for q in range(4)], axis=0
    )
    for pair in range(STEM_PAIRS):
        w1[pair] = jnp.dot(place[pair], spread, preferred_element_type=F32).astype(BF)
    for py in range(2):
        wh[py * C : py * C + C, :] = jnp.dot(
            head_ref[...], columns_ref[py], preferred_element_type=F32
        ).astype(BF)

    lane8 = lax.broadcasted_iota(jnp.int32, (TY, TX), 1)
    lane128 = lax.broadcasted_iota(jnp.int32, (Z * TY, TX), 1)
    end = lax.broadcasted_iota(jnp.int32, (1, TY, TX), 2) == TX - 1
    for buffer in (main, edge):
        for half in range(2):
            buffer[half, 0] = jnp.zeros((2 * TY, TX), F32)
            buffer[half, Z + 1] = jnp.zeros((2 * TY, TX), F32)
    filler = jnp.zeros((2 * TY, TX), F32)

    def turn(buffer, z):
        parts = []
        for half in range(2):
            parts += [buffer[half, z], buffer[half, z + 1], buffer[half, z + 2], filler]
        return jnp.concatenate(parts, axis=0).T

    own = tile_ref[...].astype(F32)
    main[0, 1 : Z + 1, 0:TY, :] = own
    main[1, 1 : Z + 1, 0:TY, :] = jnp.where(end, 0.0, pltpu.roll(own, TX - 1, axis=2))
    for half in range(2):
        main[half, 1 : Z + 1, TY : 2 * TY, :] = jnp.zeros((Z, TY, TX), F32)
    for z in range(Z):
        qf[pl.ds(8 * Z + z, TX, stride=Z), :] = turn(main, z)
    for m in range(3, STEM_X - 2):
        qb[m] = qf[(2 * m + 3) * Z : (2 * m + 4) * Z, :].astype(BF)

    def stem_rows(pair, spans):
        parts = []
        for k in range(2):
            part = join([qb[begin + k : end + k] for begin, end in spans])
            parts.append(part.reshape(-1, 128))
        acc = jnp.dot(jnp.concatenate(parts, axis=1), w1[pair], preferred_element_type=F32)
        outside = (at_low_y & (pair == 0)) | (at_high_y & (pair == STEM_PAIRS - 1))
        acc = jnp.maximum(acc, 0.0) * jnp.where(outside, 0.0, 1.0)
        for qx in range(2):
            value = acc[:, qx * 128 : qx * 128 + 128].astype(BF).reshape(-1, Z, 128)
            at = 0
            for begin, end in spans:
                stem[pair, qx, begin:end] = value[at : at + end - begin]
                at += end - begin

    upper = lax.broadcasted_iota(jnp.int32, (1, 1, 128), 2) // C

    def inner_rows(pair, spans):
        sums = conv_rows(stem, pair, spans, near2, far2)
        low = jnp.where(at_low_y & (pair == 0), 0, -1)
        high = jnp.where(at_high_y & (pair == INNER_PAIRS - 1), 1, -1)
        keep = jnp.where((upper == low) | (upper == high), 0.0, 1.0)
        for qx in range(2):
            value = (jnp.maximum(sums[qx], 0.0) * keep).astype(BF)
            at = 0
            for begin, end in spans:
                inner[pair, qx, begin:end] = value[at : at + end - begin]
                at += end - begin

    def loop(count, pair_of, body):
        def step(n, carry):
            body(pair_of(n))
            return carry

        lax.fori_loop(0, count, step, 0)

    loop(2, lambda n: n + 2, lambda pair: stem_rows(pair, STEM_OWN))
    inner_rows(2, INNER_OWN)

    for copy in copies:
        copy.wait()

    right_ok = jnp.where(at_high_x, 0, 64)
    left_ok = jnp.where(at_low_x, 128, 64)
    between = jnp.zeros((TX - 32, Z * TY), F32)
    middles, sideways = [], []
    for ty in range(3):
        left, right = sides_in[ty, 0].astype(F32), sides_in[ty, 1].astype(F32)
        sides = jnp.concatenate([right, between, left], axis=0).T
        sides = jnp.where((lane128 < right_ok) | (lane128 >= left_ok), sides, 0.0)
        sides = sides.reshape(Z, TY, TX)
        middle = own if ty == 1 else rows_in[ty // 2].astype(F32)
        if ty != 1:
            outside = at_low_y if ty == 0 else at_high_y
            middle, sides = jnp.where(outside, 0.0, middle), jnp.where(outside, 0.0, sides)
        middles.append(middle)
        sideways.append(sides)
    row8 = lax.broadcasted_iota(jnp.int32, (1, TY, TX), 1)
    for part in range(2):
        if part == 0:
            middle, sides = middles[1], sideways[1]
        else:
            middle = jnp.where(row8 < 4, middles[2], middles[0])
            sides = jnp.where(row8 < 4, sideways[2], sideways[0])
        next_middle, next_sides = pltpu.roll(middle, TX - 1, axis=2), pltpu.roll(sides, TX - 1, axis=2)
        rows = slice(part * TY, part * TY + TY)
        main[0, 1 : Z + 1, rows, :] = middle
        main[1, 1 : Z + 1, rows, :] = jnp.where(end, next_sides, next_middle)
        edge[0, 1 : Z + 1, rows, :] = sides
        edge[1, 1 : Z + 1, rows, :] = jnp.where(end, next_middle, next_sides)
    for z in range(Z):
        sides = turn(edge, z)
        qf[pl.ds(8 * Z + z, TX, stride=Z), :] = turn(main, z)
        qf[pl.ds(z, 8, stride=Z), :] = sides[120:128]
        qf[pl.ds(136 * Z + z, 8, stride=Z), :] = sides[0:8]
    for m in range(STEM_X + 1):
        qb[m] = qf[(2 * m + 3) * Z : (2 * m + 4) * Z, :].astype(BF)

    loop(4, lambda n: n + n // 2 * 2, lambda pair: stem_rows(pair, ((0, STEM_X),)))
    loop(2, lambda n: n + 2, lambda pair: stem_rows(pair, STEM_SIDES))

    @pl.when(at_low_x)
    def _():
        zero_columns(stem, range(4))

    @pl.when(at_high_x)
    def _():
        zero_columns(stem, range(132, 136))

    loop(4, lambda n: n + n // 2, lambda pair: inner_rows(pair, ((0, INNER_X),)))
    inner_rows(2, INNER_SIDES)

    @pl.when(at_low_x)
    def _():
        zero_columns(inner, range(3))

    @pl.when(at_high_x)
    def _():
        zero_columns(inner, range(131, 134))

    def block_body(pair):
        sums = conv_rows(inner, pair, ((0, BLOCK_X),), near3, far3)
        for qx in range(2):
            old = stem[pair + 1, qx, 1 : 1 + BLOCK_X].astype(F32)
            value = jnp.maximum(sums[qx] + old, 0.0).astype(BF).reshape(BLOCK_X * Z, 128)
            logits = jnp.dot(value, wh[...], preferred_element_type=F32)
            pred[pair, qx] = jnp.tanh(logits).astype(BF).reshape(BLOCK_X, Z, 256)

        @pl.when(at_low_x)
        def _():
            for parity in range(2):
                pred[pair, parity, 0] = jnp.zeros((Z, 256), BF)

        @pl.when(at_high_x)
        def _():
            for parity in range(2):
                pred[pair, parity, BLOCK_X - 1] = jnp.zeros((Z, 256), BF)

    lanes = lax.broadcasted_iota(jnp.int32, (1, Z, 128), 2)

    def blend_rows(pairs, first, more):
        def body(step, carry):
            j = step * XB
            for qx in range(2):
                operands = []
                for pair in pairs:
                    for half in range(2):
                        chosen = None
                        for n, a in enumerate((0, 1, 2) if half == 0 else (2, 3, 4)):
                            at = qx - a + 4
                            part = pred[pair, at % 2, pl.ds(j + at // 2, XB), :, half * 128 : half * 128 + 128]
                            chosen = part if n == 0 else jnp.where(lanes >= A_START[half][n], part, chosen)
                        operands.append(chosen.reshape(XB * Z, 128))
                added = jnp.dot(
                    jnp.concatenate(operands, axis=1),
                    blend[first : first + 256 * len(pairs), :],
                    preferred_element_type=F32,
                )
                added = added.reshape(XB, Z, 128)
                at = pl.ds(j, XB)
                total[at, qx] = total[at, qx] + added if more else added
            return carry

        lax.fori_loop(0, TX // 2 // XB, body, 0)

    def turned_total(z):
        return total.reshape(TX * Z, 128)[pl.ds(z, TX, stride=Z), :].T

    def outer_body(step, carry):
        block_body(step * (BLOCK_PAIRS - 1))
        return carry

    lax.fori_loop(0, 2, outer_body, 0)
    blend_rows((0, BLOCK_PAIRS - 1), 0, False)
    for z in range(Z):
        both = turned_total(z)
        for side in range(2):
            edge_out[side, z] = both[24 + 8 * side : 32 + 8 * side]
    edges = []
    for side, dy in enumerate((-1, 1)):
        edges.append(
            pltpu.make_async_remote_copy(
                src_ref=edge_out.at[side],
                dst_ref=edge_in.at[side],
                send_sem=edge_send_sem.at[side],
                recv_sem=edge_recv_sem.at[side],
                device_id=device(dy, 0),
                device_id_type=MESH,
            )
        )
        edges[-1].start()

    def middle_body(step, carry):
        block_body(step + 1)
        return carry

    lax.fori_loop(0, BLOCK_PAIRS - 2, middle_body, 0)
    blend_rows(tuple(range(1, BLOCK_PAIRS - 1)), 512, True)

    y8 = lax.broadcasted_iota(jnp.int32, (TY, TX), 0)
    scale = 0.5 / (coverage_of(gy * TY + y8, ny * TY) * coverage_of(gx * TX + lane8, nx * TX))
    from_above = (y8 < 2) & (gy > 0)
    from_below = (y8 >= TY - 2) & (gy < ny - 1)
    for copy in edges:
        copy.wait()
    for z in range(Z):
        both = turned_total(z)
        below, above = edge_in[0, z], edge_in[1, z]
        for c in range(3):
            added = both[c * TY : c * TY + TY, :]
            added += jnp.where(from_above, above if c == 0 else pltpu.roll(above, TY - 2 * c, axis=0), 0.0)
            added += jnp.where(from_below, pltpu.roll(below, TY - 2 - 2 * c, axis=0), 0.0)
            out_ref[c, z] = 0.5 + added * scale


def lane_plan():
    plan, starts = [], []
    for half in range(2):
        lanes, begin = [], []
        for a in (0, 1, 2) if half == 0 else (2, 3, 4):
            begin.append(len(lanes))
            for py in range(2):
                if a == 2 and py != half:
                    continue
                lanes += [(a, py, b, c) for b in range(5) for c in range(3)]
        plan.append(lanes)
        starts.append(begin)
    return plan, starts


LANES, A_START = lane_plan()


def constants():
    place = np.zeros((STEM_PAIRS, 4, 64, 128), np.float32)
    for pair in range(STEM_PAIRS):
        for qx in range(2):
            for qy in range(2):
                for dz in range(3):
                    for dy in range(3):
                        for dx in range(3):
                            y = (2 * pair + qy + dy - 3) % 16
                            place[pair, qx + dx, dz * 16 + y, (qx * 2 + qy) * 32 + (dz * 3 + dy) * 3 + dx] = 1
    columns = np.zeros((2, 75, 256), np.float32)
    pairs = (0, BLOCK_PAIRS - 1) + tuple(range(1, BLOCK_PAIRS - 1))
    blend = np.zeros((len(pairs), 256, 128), np.float32)
    for half in range(2):
        for n, (a, py, b, c) in enumerate(LANES[half]):
            columns[py, (a * 5 + b) * 3 + c, half * 128 + n] = 0.5
            for i, pair in enumerate(pairs):
                y = 2 * pair + py + b - R
                if y < 0:
                    lane = 24 + 2 * c + y + R
                elif y >= TY:
                    lane = 32 + 2 * c + y - TY
                else:
                    lane = c * TY + y
                blend[i, half * 128 + n, lane] = (R + 1 - abs(a - R)) * (R + 1 - abs(b - R))
    return (
        jnp.asarray(place.reshape(STEM_PAIRS, 256, 128), BF),
        jnp.asarray(columns, BF),
        jnp.asarray(blend.reshape(-1, 128), BF),
    )


def local(intensity, first_kernel, second_kernel, third_kernel, head_weight):
    place, columns, blend = constants()
    vmem = pl.BlockSpec(memory_space=pltpu.VMEM)
    hbm = pl.BlockSpec(memory_space=pltpu.HBM)
    return pl.pallas_call(
        compute_kernel,
        out_shape=jax.ShapeDtypeStruct((3, Z, TY, TX), F32),
        in_specs=[hbm] * 8,
        out_specs=vmem,
        scratch_shapes=[
            pltpu.VMEM(intensity.shape, BF),
            pltpu.VMEM(place.shape, BF),
            pltpu.VMEM((9, 3, C), BF),
            pltpu.VMEM((27, C, C), BF),
            pltpu.VMEM((27, C, C), BF),
            pltpu.VMEM(head_weight.shape, BF),
            pltpu.VMEM(columns.shape, BF),
            pltpu.VMEM(blend.shape, BF),
            pltpu.VMEM((2, 16, Z * TY), BF),
            pltpu.VMEM((2, Z, TY, TX), BF),
            pltpu.VMEM((3, 2, 16, Z * TY), BF),
            pltpu.VMEM((2, Z, TY, TX), F32),
            pltpu.VMEM((2, Z, TY, TX), F32),
            pltpu.VMEM((32, C), F32),
            pltpu.VMEM((STEM_PAIRS, 256, 256), BF),
            pltpu.VMEM((768, 256), BF),
            pltpu.VMEM((1024, 256), BF),
            pltpu.VMEM((768, 256), BF),
            pltpu.VMEM((1024, 256), BF),
            pltpu.VMEM((128, 256), BF),
            pltpu.VMEM((2, Z + 2, 2 * TY, TX), F32),
            pltpu.VMEM((2, Z + 2, 2 * TY, TX), F32),
            pltpu.VMEM((144 * Z, 128), F32),
            pltpu.VMEM((STEM_X + 1, Z, 128), BF),
            pltpu.VMEM((STEM_PAIRS, 2, STEM_X, Z, 128), BF),
            pltpu.VMEM((INNER_PAIRS, 2, INNER_X, Z, 128), BF),
            pltpu.VMEM((BLOCK_PAIRS, 2, BLOCK_X, Z, 256), BF),
            pltpu.VMEM((TX // 2, 2, Z, 128), F32),
            pltpu.SemaphoreType.DMA((8,)),
            pltpu.SemaphoreType.DMA((8,)),
            pltpu.SemaphoreType.DMA((8,)),
            pltpu.SemaphoreType.DMA((2,)),
            pltpu.SemaphoreType.DMA((2,)),
        ],
        compiler_params=pltpu.CompilerParams(
            collective_id=0, has_side_effects=True, vmem_limit_bytes=56 * 2**20
        ),
        name="convnet",
    )(
        intensity, place, first_kernel.reshape(9, 3, C),
        second_kernel.reshape(27, C, C), third_kernel.reshape(27, C, C), head_weight, columns, blend,
    )


def solution(mesh):
    in_specs = (P(None, "gy", "gx"), P(), P(), P(), P())
    out_specs = P(None, None, "gy", "gx")
    return jax.shard_map(local, mesh=mesh, in_specs=in_specs, out_specs=out_specs, check_vma=False)
```

```python
import functools

import jax
import jax.numpy as jnp
import numpy as np
from jax import lax
from jax.experimental import pallas as pl
from jax.experimental.pallas import tpu as pltpu
from jax.sharding import PartitionSpec as P

R = 2
C = 64
Z = 16
TY = 8
TX = 128
BF = jnp.bfloat16
F32 = jnp.float32
MESH = pl.DeviceIdType.MESH


STEM_PAIRS = 6
INNER_PAIRS = 5
BLOCK_PAIRS = 4
STEM_X = 68
INNER_X = 67
BLOCK_X = 66
XB = 32
STEM_OWN, STEM_SIDES = ((3, 65),), ((0, 3), (65, STEM_X))
INNER_OWN, INNER_SIDES = ((3, 64),), ((0, 3), (64, INNER_X))
AROUND = [(dy, dx) for dy in (-1, 0, 1) for dx in (-1, 0, 1) if (dy, dx) != (0, 0)]


def join(parts):
    return parts[0] if len(parts) == 1 else jnp.concatenate(parts, axis=0)


def conv_rows(ref, pair, spans, near, far):
    count = sum(end - begin for begin, end in spans)

    def operand(offsets):
        parts = []
        for offset in offsets:
            for k in range(2):
                at = offset // 2
                part = join([ref[pair + k, offset % 2, begin + at : end + at] for begin, end in spans])
                parts.append(part.reshape(count * Z, 2 * C))
        return jnp.concatenate(parts, axis=1)

    row = lax.broadcasted_iota(jnp.int32, (1, Z, 2 * C), 1)
    third = jnp.dot(operand(range(4)), far[...], preferred_element_type=F32)
    out = []
    for qx in range(2):
        both = jnp.dot(operand(range(qx, qx + 3)), near[...], preferred_element_type=F32)
        below = both[:, :128].reshape(count, Z, 128)
        above = third[:, qx * 128 : qx * 128 + 128].reshape(count, Z, 128)
        total = both[:, 128:].reshape(count, Z, 128)
        total += jnp.where(row == 0, 0.0, pltpu.roll(below, 1, axis=1))
        total += jnp.where(row == Z - 1, 0.0, pltpu.roll(above, Z - 1, axis=1))
        out.append(total)
    return out


def build_conv_weights(kernel_ref, near, far):
    zero = jnp.zeros((C, C), BF)

    def band(dz, dx, source):
        blocks = []
        for qy in range(2):
            dy = source - qy
            inside = 0 <= dx < 3 and 0 <= dy < 3
            blocks.append(kernel_ref[(dz * 3 + dy) * 3 + dx] if inside else zero)
        return jnp.concatenate(blocks, axis=1)

    for source in range(4):
        for dx in range(3):
            rows = (dx * 4 + source) * C
            for dz in range(2):
                near[rows : rows + C, dz * 128 : dz * 128 + 128] = band(dz, dx, source)
        for offset in range(4):
            rows = (offset * 4 + source) * C
            for qx in range(2):
                far[rows : rows + C, qx * 128 : qx * 128 + 128] = band(2, offset - qx, source)


def zero_columns(ref, columns):
    for pair in range(ref.shape[0]):
        for x in columns:
            ref[pair, x % 2, x // 2] = jnp.zeros((Z, 2 * C), BF)


def coverage_of(position, length):
    total = jnp.zeros(position.shape, F32)
    for b in range(2 * R + 1):
        source = position - (b - R)
        total += jnp.where((source >= 0) & (source < length), float(R + 1 - abs(b - R)), 0.0)
    return total


def compute_kernel(
    tile_hbm, place_hbm, first_hbm, second_hbm, third_hbm, head_hbm, columns_hbm, blend_hbm,
    out_ref,
    tile_ref, place, first_ref, second, third, head_ref, columns_ref, blend,
    strips, rows_in, sides_in, edge_out, edge_in,
    taps, w1, near2, far2, near3, far3, wh, main, edge, qf, qb, stem, inner, pred, total,
    load_sem, send_sem, recv_sem, edge_send_sem, edge_recv_sem,
):
    gx, gy = lax.axis_index("gx"), lax.axis_index("gy")
    nx, ny = lax.axis_size("gx"), lax.axis_size("gy")
    at_low_x, at_high_x = gx == 0, gx == nx - 1
    at_low_y, at_high_y = gy == 0, gy == ny - 1

    def device(dy, dx):
        return (lax.rem(gx + dx + nx, nx), lax.rem(gy + dy + ny, ny))

    def inside(dy, dx):
        found = None
        for step, low, high in ((dy, at_low_y, at_high_y), (dx, at_low_x, at_high_x)):
            if step:
                here = jnp.logical_not(low if step < 0 else high)
                found = here if found is None else found & here
        return found

    barrier = pltpu.get_barrier_semaphore()
    for dy, dx in AROUND:

        @pl.when(inside(dy, dx))
        def _():
            pl.semaphore_signal(barrier, inc=1, device_id=device(dy, dx), device_id_type=MESH)

    loads = []
    for n, (source, target) in enumerate(
        (
            (tile_hbm, tile_ref), (second_hbm, second), (third_hbm, third), (first_hbm, first_ref),
            (place_hbm, place), (head_hbm, head_ref), (columns_hbm, columns_ref), (blend_hbm, blend),
        )
    ):
        loads.append(pltpu.make_async_copy(source, target, load_sem.at[n]))
        loads[-1].start()

    loads[0].wait()
    turned = tile_ref[...].astype(F32).reshape(Z * TY, TX).T
    strips[0] = turned[0:16].astype(BF)
    strips[1] = turned[TX - 16 : TX].astype(BF)
    beside_y = 2 - at_low_y.astype(jnp.int32) - at_high_y.astype(jnp.int32)
    beside_x = 2 - at_low_x.astype(jnp.int32) - at_high_x.astype(jnp.int32)
    pl.semaphore_wait(barrier, (beside_y + 1) * (beside_x + 1) - 1)
    copies = []
    for n, (dy, dx) in enumerate(AROUND):
        if dx == 0:
            source, target = tile_ref, rows_in.at[0 if dy == 1 else 1]
        else:
            source, target = strips.at[0 if dx == -1 else 1], sides_in.at[1 - dy, 0 if dx == 1 else 1]
        copies.append(
            pltpu.make_async_remote_copy(
                src_ref=source,
                dst_ref=target,
                send_sem=send_sem.at[n],
                recv_sem=recv_sem.at[n],
                device_id=device(dy, dx),
                device_id_type=MESH,
            )
        )
        pl.when(inside(dy, dx))(copies[-1].start)

    for load in loads[1:]:
        load.wait()
    build_conv_weights(second, near2, far2)
    build_conv_weights(third, near3, far3)
    taps[...] = jnp.zeros((32, C), F32)
    for n in range(9):
        taps[3 * n : 3 * n + 3, :] = first_ref[n].astype(F32)
    tap = taps[...].astype(BF)
    nothing = jnp.zeros((32, C), BF)
    spread = jnp.concatenate(
        [jnp.concatenate([tap if i == q else nothing for i in range(4)], axis=1) for q in range(4)], axis=0
    )
    for pair in range(STEM_PAIRS):
        w1[pair] = jnp.dot(place[pair], spread, preferred_element_type=F32).astype(BF)
    for py in range(2):
        wh[py * C : py * C + C, :] = jnp.dot(
            head_ref[...], columns_ref[py], preferred_element_type=F32
        ).astype(BF)

    lane8 = lax.broadcasted_iota(jnp.int32, (TY, TX), 1)
    lane128 = lax.broadcasted_iota(jnp.int32, (Z * TY, TX), 1)
    end = lax.broadcasted_iota(jnp.int32, (1, TY, TX), 2) == TX - 1
    for buffer in (main, edge):
        for half in range(2):
            buffer[half, 0] = jnp.zeros((2 * TY, TX), F32)
            buffer[half, Z + 1] = jnp.zeros((2 * TY, TX), F32)
    filler = jnp.zeros((2 * TY, TX), F32)

    def turn(buffer, z):
        parts = []
        for half in range(2):
            parts += [buffer[half, z], buffer[half, z + 1], buffer[half, z + 2], filler]
        return jnp.concatenate(parts, axis=0).T

    own = tile_ref[...].astype(F32)
    main[0, 1 : Z + 1, 0:TY, :] = own
    main[1, 1 : Z + 1, 0:TY, :] = jnp.where(end, 0.0, pltpu.roll(own, TX - 1, axis=2))
    for half in range(2):
        main[half, 1 : Z + 1, TY : 2 * TY, :] = jnp.zeros((Z, TY, TX), F32)
    for z in range(Z):
        qf[pl.ds(8 * Z + z, TX, stride=Z), :] = turn(main, z)
    for m in range(3, STEM_X - 2):
        qb[m] = qf[(2 * m + 3) * Z : (2 * m + 4) * Z, :].astype(BF)

    def stem_rows(pair, spans):
        parts = []
        for k in range(2):
            part = join([qb[begin + k : end + k] for begin, end in spans])
            parts.append(part.reshape(-1, 128))
        acc = jnp.dot(jnp.concatenate(parts, axis=1), w1[pair], preferred_element_type=F32)
        outside = (at_low_y & (pair == 0)) | (at_high_y & (pair == STEM_PAIRS - 1))
        acc = jnp.maximum(acc, 0.0) * jnp.where(outside, 0.0, 1.0)
        for qx in range(2):
            value = acc[:, qx * 128 : qx * 128 + 128].astype(BF).reshape(-1, Z, 128)
            at = 0
            for begin, end in spans:
                stem[pair, qx, begin:end] = value[at : at + end - begin]
                at += end - begin

    upper = lax.broadcasted_iota(jnp.int32, (1, 1, 128), 2) // C

    def inner_rows(pair, spans):
        sums = conv_rows(stem, pair, spans, near2, far2)
        low = jnp.where(at_low_y & (pair == 0), 0, -1)
        high = jnp.where(at_high_y & (pair == INNER_PAIRS - 1), 1, -1)
        keep = jnp.where((upper == low) | (upper == high), 0.0, 1.0)
        for qx in range(2):
            value = (jnp.maximum(sums[qx], 0.0) * keep).astype(BF)
            at = 0
            for begin, end in spans:
                inner[pair, qx, begin:end] = value[at : at + end - begin]
                at += end - begin

    def loop(count, pair_of, body):
        def step(n, carry):
            body(pair_of(n))
            return carry

        lax.fori_loop(0, count, step, 0)

    loop(2, lambda n: n + 2, lambda pair: stem_rows(pair, STEM_OWN))
    inner_rows(2, INNER_OWN)

    for copy, (dy, dx) in zip(copies, AROUND):
        pl.when(inside(dy, dx))(copy.wait_send)
        pl.when(inside(-dy, -dx))(copy.wait_recv)

    right_ok = jnp.where(at_high_x, 0, 64)
    left_ok = jnp.where(at_low_x, 128, 64)
    between = jnp.zeros((TX - 32, Z * TY), F32)
    middles, sideways = [], []
    for ty in range(3):
        left, right = sides_in[ty, 0].astype(F32), sides_in[ty, 1].astype(F32)
        sides = jnp.concatenate([right, between, left], axis=0).T
        sides = jnp.where((lane128 < right_ok) | (lane128 >= left_ok), sides, 0.0)
        sides = sides.reshape(Z, TY, TX)
        middle = own if ty == 1 else rows_in[ty // 2].astype(F32)
        if ty != 1:
            outside = at_low_y if ty == 0 else at_high_y
            middle, sides = jnp.where(outside, 0.0, middle), jnp.where(outside, 0.0, sides)
        middles.append(middle)
        sideways.append(sides)
    row8 = lax.broadcasted_iota(jnp.int32, (1, TY, TX), 1)
    for part in range(2):
        if part == 0:
            middle, sides = middles[1], sideways[1]
        else:
            middle = jnp.where(row8 < 4, middles[2], middles[0])
            sides = jnp.where(row8 < 4, sideways[2], sideways[0])
        next_middle, next_sides = pltpu.roll(middle, TX - 1, axis=2), pltpu.roll(sides, TX - 1, axis=2)
        rows = slice(part * TY, part * TY + TY)
        main[0, 1 : Z + 1, rows, :] = middle
        main[1, 1 : Z + 1, rows, :] = jnp.where(end, next_sides, next_middle)
        edge[0, 1 : Z + 1, rows, :] = sides
        edge[1, 1 : Z + 1, rows, :] = jnp.where(end, next_middle, next_sides)
    for z in range(Z):
        sides = turn(edge, z)
        qf[pl.ds(8 * Z + z, TX, stride=Z), :] = turn(main, z)
        qf[pl.ds(z, 8, stride=Z), :] = sides[120:128]
        qf[pl.ds(136 * Z + z, 8, stride=Z), :] = sides[0:8]
    for m in range(STEM_X + 1):
        qb[m] = qf[(2 * m + 3) * Z : (2 * m + 4) * Z, :].astype(BF)

    loop(4, lambda n: n + n // 2 * 2, lambda pair: stem_rows(pair, ((0, STEM_X),)))
    loop(2, lambda n: n + 2, lambda pair: stem_rows(pair, STEM_SIDES))

    @pl.when(at_low_x)
    def _():
        zero_columns(stem, range(4))

    @pl.when(at_high_x)
    def _():
        zero_columns(stem, range(132, 136))

    loop(4, lambda n: n + n // 2, lambda pair: inner_rows(pair, ((0, INNER_X),)))
    inner_rows(2, INNER_SIDES)

    @pl.when(at_low_x)
    def _():
        zero_columns(inner, range(3))

    @pl.when(at_high_x)
    def _():
        zero_columns(inner, range(131, 134))

    def block_body(pair):
        sums = conv_rows(inner, pair, ((0, BLOCK_X),), near3, far3)
        for qx in range(2):
            old = stem[pair + 1, qx, 1 : 1 + BLOCK_X].astype(F32)
            value = jnp.maximum(sums[qx] + old, 0.0).astype(BF).reshape(BLOCK_X * Z, 128)
            logits = jnp.dot(value, wh[...], preferred_element_type=F32)
            pred[pair, qx] = jnp.tanh(logits).astype(BF).reshape(BLOCK_X, Z, 256)

        @pl.when(at_low_x)
        def _():
            for parity in range(2):
                pred[pair, parity, 0] = jnp.zeros((Z, 256), BF)

        @pl.when(at_high_x)
        def _():
            for parity in range(2):
                pred[pair, parity, BLOCK_X - 1] = jnp.zeros((Z, 256), BF)

    lanes = lax.broadcasted_iota(jnp.int32, (1, Z, 128), 2)

    def blend_rows(pairs, first, more):
        def body(step, carry):
            j = step * XB
            for qx in range(2):
                operands = []
                for pair in pairs:
                    for half in range(2):
                        chosen = None
                        for n, a in enumerate((0, 1, 2) if half == 0 else (2, 3, 4)):
                            at = qx - a + 4
                            part = pred[pair, at % 2, pl.ds(j + at // 2, XB), :, half * 128 : half * 128 + 128]
                            chosen = part if n == 0 else jnp.where(lanes >= A_START[half][n], part, chosen)
                        operands.append(chosen.reshape(XB * Z, 128))
                added = jnp.dot(
                    jnp.concatenate(operands, axis=1),
                    blend[first : first + 256 * len(pairs), :],
                    preferred_element_type=F32,
                )
                added = added.reshape(XB, Z, 128)
                at = pl.ds(j, XB)
                total[at, qx] = total[at, qx] + added if more else added
            return carry

        lax.fori_loop(0, TX // 2 // XB, body, 0)

    def turned_total(z):
        return total.reshape(TX * Z, 128)[pl.ds(z, TX, stride=Z), :].T

    def outer_body(step, carry):
        block_body(step * (BLOCK_PAIRS - 1))
        return carry

    lax.fori_loop(0, 2, outer_body, 0)
    blend_rows((0, BLOCK_PAIRS - 1), 0, False)
    for z in range(Z):
        both = turned_total(z)
        for side in range(2):
            edge_out[side, z] = both[24 + 8 * side : 32 + 8 * side]
    edges = []
    for side, dy in enumerate((-1, 1)):
        edges.append(
            pltpu.make_async_remote_copy(
                src_ref=edge_out.at[side],
                dst_ref=edge_in.at[side],
                send_sem=edge_send_sem.at[side],
                recv_sem=edge_recv_sem.at[side],
                device_id=device(dy, 0),
                device_id_type=MESH,
            )
        )
        pl.when(inside(dy, 0))(edges[-1].start)

    def middle_body(step, carry):
        block_body(step + 1)
        return carry

    lax.fori_loop(0, BLOCK_PAIRS - 2, middle_body, 0)
    blend_rows(tuple(range(1, BLOCK_PAIRS - 1)), 512, True)

    y8 = lax.broadcasted_iota(jnp.int32, (TY, TX), 0)
    scale = 0.5 / (coverage_of(gy * TY + y8, ny * TY) * coverage_of(gx * TX + lane8, nx * TX))
    from_above = (y8 < 2) & (gy > 0)
    from_below = (y8 >= TY - 2) & (gy < ny - 1)
    for copy, dy in zip(edges, (-1, 1)):
        pl.when(inside(dy, 0))(copy.wait_send)
        pl.when(inside(-dy, 0))(copy.wait_recv)
    for z in range(Z):
        both = turned_total(z)
        below, above = edge_in[0, z], edge_in[1, z]
        for c in range(3):
            added = both[c * TY : c * TY + TY, :]
            added += jnp.where(from_above, above if c == 0 else pltpu.roll(above, TY - 2 * c, axis=0), 0.0)
            added += jnp.where(from_below, pltpu.roll(below, TY - 2 - 2 * c, axis=0), 0.0)
            out_ref[c, z] = 0.5 + added * scale


def lane_plan():
    plan, starts = [], []
    for half in range(2):
        lanes, begin = [], []
        for a in (0, 1, 2) if half == 0 else (2, 3, 4):
            begin.append(len(lanes))
            for py in range(2):
                if a == 2 and py != half:
                    continue
                lanes += [(a, py, b, c) for b in range(5) for c in range(3)]
        plan.append(lanes)
        starts.append(begin)
    return plan, starts


LANES, A_START = lane_plan()


def constants():
    place = np.zeros((STEM_PAIRS, 4, 64, 128), np.float32)
    for pair in range(STEM_PAIRS):
        for qx in range(2):
            for qy in range(2):
                for dz in range(3):
                    for dy in range(3):
                        for dx in range(3):
                            y = (2 * pair + qy + dy - 3) % 16
                            place[pair, qx + dx, dz * 16 + y, (qx * 2 + qy) * 32 + (dz * 3 + dy) * 3 + dx] = 1
    columns = np.zeros((2, 75, 256), np.float32)
    pairs = (0, BLOCK_PAIRS - 1) + tuple(range(1, BLOCK_PAIRS - 1))
    blend = np.zeros((len(pairs), 256, 128), np.float32)
    for half in range(2):
        for n, (a, py, b, c) in enumerate(LANES[half]):
            columns[py, (a * 5 + b) * 3 + c, half * 128 + n] = 0.5
            for i, pair in enumerate(pairs):
                y = 2 * pair + py + b - R
                if y < 0:
                    lane = 24 + 2 * c + y + R
                elif y >= TY:
                    lane = 32 + 2 * c + y - TY
                else:
                    lane = c * TY + y
                blend[i, half * 128 + n, lane] = (R + 1 - abs(a - R)) * (R + 1 - abs(b - R))
    return (
        jnp.asarray(place.reshape(STEM_PAIRS, 256, 128), BF),
        jnp.asarray(columns, BF),
        jnp.asarray(blend.reshape(-1, 128), BF),
    )


def local(intensity, first_kernel, second_kernel, third_kernel, head_weight):
    place, columns, blend = constants()
    vmem = pl.BlockSpec(memory_space=pltpu.VMEM)
    hbm = pl.BlockSpec(memory_space=pltpu.HBM)
    return pl.pallas_call(
        compute_kernel,
        out_shape=jax.ShapeDtypeStruct((3, Z, TY, TX), F32),
        in_specs=[hbm] * 8,
        out_specs=vmem,
        scratch_shapes=[
            pltpu.VMEM(intensity.shape, BF),
            pltpu.VMEM(place.shape, BF),
            pltpu.VMEM((9, 3, C), BF),
            pltpu.VMEM((27, C, C), BF),
            pltpu.VMEM((27, C, C), BF),
            pltpu.VMEM(head_weight.shape, BF),
            pltpu.VMEM(columns.shape, BF),
            pltpu.VMEM(blend.shape, BF),
            pltpu.VMEM((2, 16, Z * TY), BF),
            pltpu.VMEM((2, Z, TY, TX), BF),
            pltpu.VMEM((3, 2, 16, Z * TY), BF),
            pltpu.VMEM((2, Z, TY, TX), F32),
            pltpu.VMEM((2, Z, TY, TX), F32),
            pltpu.VMEM((32, C), F32),
            pltpu.VMEM((STEM_PAIRS, 256, 256), BF),
            pltpu.VMEM((768, 256), BF),
            pltpu.VMEM((1024, 256), BF),
            pltpu.VMEM((768, 256), BF),
            pltpu.VMEM((1024, 256), BF),
            pltpu.VMEM((128, 256), BF),
            pltpu.VMEM((2, Z + 2, 2 * TY, TX), F32),
            pltpu.VMEM((2, Z + 2, 2 * TY, TX), F32),
            pltpu.VMEM((144 * Z, 128), F32),
            pltpu.VMEM((STEM_X + 1, Z, 128), BF),
            pltpu.VMEM((STEM_PAIRS, 2, STEM_X, Z, 128), BF),
            pltpu.VMEM((INNER_PAIRS, 2, INNER_X, Z, 128), BF),
            pltpu.VMEM((BLOCK_PAIRS, 2, BLOCK_X, Z, 256), BF),
            pltpu.VMEM((TX // 2, 2, Z, 128), F32),
            pltpu.SemaphoreType.DMA((8,)),
            pltpu.SemaphoreType.DMA((8,)),
            pltpu.SemaphoreType.DMA((8,)),
            pltpu.SemaphoreType.DMA((2,)),
            pltpu.SemaphoreType.DMA((2,)),
        ],
        compiler_params=pltpu.CompilerParams(
            collective_id=0, has_side_effects=True, vmem_limit_bytes=56 * 2**20
        ),
        name="convnet",
    )(
        intensity, place, first_kernel.reshape(9, 3, C),
        second_kernel.reshape(27, C, C), third_kernel.reshape(27, C, C), head_weight, columns, blend,
    )


def solution(mesh):
    in_specs = (P(None, "gy", "gx"), P(), P(), P(), P())
    out_specs = P(None, None, "gy", "gx")
    return jax.shard_map(local, mesh=mesh, in_specs=in_specs, out_specs=out_specs, check_vma=False)
```

```python
import functools

import jax
import jax.numpy as jnp
import numpy as np
from jax import lax
from jax.experimental import pallas as pl
from jax.experimental.pallas import tpu as pltpu
from jax.sharding import PartitionSpec as P

R = 2
C = 64
Z = 16
TY = 8
TX = 128
BF = jnp.bfloat16
F32 = jnp.float32
MESH = pl.DeviceIdType.MESH


STEM_PAIRS = 6
INNER_PAIRS = 5
BLOCK_PAIRS = 4
STEM_X = 68
INNER_X = 67
BLOCK_X = 66
XB = 64
STEM_OWN, STEM_SIDES = ((3, 65),), ((0, 3), (65, STEM_X))
INNER_OWN, INNER_SIDES = ((3, 64),), ((0, 3), (64, INNER_X))
AROUND = [(dy, dx) for dy in (-1, 0, 1) for dx in (-1, 0, 1) if (dy, dx) != (0, 0)]


def join(parts):
    return parts[0] if len(parts) == 1 else jnp.concatenate(parts, axis=0)


def conv_rows(ref, pair, spans, near, far):
    count = sum(end - begin for begin, end in spans)

    def operand(offsets):
        parts = []
        for offset in offsets:
            for k in range(2):
                at = offset // 2
                part = join([ref[pair + k, offset % 2, begin + at : end + at] for begin, end in spans])
                parts.append(part.reshape(count * Z, 2 * C))
        return jnp.concatenate(parts, axis=1)

    row = lax.broadcasted_iota(jnp.int32, (1, Z, 2 * C), 1)
    third = jnp.dot(operand(range(4)), far[...], preferred_element_type=F32)
    out = []
    for qx in range(2):
        both = jnp.dot(operand(range(qx, qx + 3)), near[...], preferred_element_type=F32)
        below = both[:, :128].reshape(count, Z, 128)
        above = third[:, qx * 128 : qx * 128 + 128].reshape(count, Z, 128)
        total = both[:, 128:].reshape(count, Z, 128)
        total += jnp.where(row == 0, 0.0, pltpu.roll(below, 1, axis=1))
        total += jnp.where(row == Z - 1, 0.0, pltpu.roll(above, Z - 1, axis=1))
        out.append(total)
    return out


def build_conv_weights(kernel_ref, near, far):
    zero = jnp.zeros((C, C), BF)

    def band(dz, dx, source):
        blocks = []
        for qy in range(2):
            dy = source - qy
            inside = 0 <= dx < 3 and 0 <= dy < 3
            blocks.append(kernel_ref[(dz * 3 + dy) * 3 + dx] if inside else zero)
        return jnp.concatenate(blocks, axis=1)

    for source in range(4):
        for dx in range(3):
            rows = (dx * 4 + source) * C
            for dz in range(2):
                near[rows : rows + C, dz * 128 : dz * 128 + 128] = band(dz, dx, source)
        for offset in range(4):
            rows = (offset * 4 + source) * C
            for qx in range(2):
                far[rows : rows + C, qx * 128 : qx * 128 + 128] = band(2, offset - qx, source)


def zero_columns(ref, columns):
    for pair in range(ref.shape[0]):
        for x in columns:
            ref[pair, x % 2, x // 2] = jnp.zeros((Z, 2 * C), BF)


def coverage_of(position, length):
    total = jnp.zeros(position.shape, F32)
    for b in range(2 * R + 1):
        source = position - (b - R)
        total += jnp.where((source >= 0) & (source < length), float(R + 1 - abs(b - R)), 0.0)
    return total


def compute_kernel(
    tile_hbm, place_hbm, first_hbm, second_hbm, third_hbm, head_hbm, columns_hbm, blend_hbm,
    out_ref,
    tile_ref, place, first_ref, second, third, head_ref, columns_ref, blend,
    strips, rows_in, sides_in, edge_out, edge_in,
    taps, w1, near2, far2, near3, far3, wh, main, edge, qf, qb, stem, inner, pred, total,
    load_sem, send_sem, recv_sem, edge_send_sem, edge_recv_sem,
):
    gx, gy = lax.axis_index("gx"), lax.axis_index("gy")
    nx, ny = lax.axis_size("gx"), lax.axis_size("gy")
    at_low_x, at_high_x = gx == 0, gx == nx - 1
    at_low_y, at_high_y = gy == 0, gy == ny - 1

    def device(dy, dx):
        return (lax.rem(gx + dx + nx, nx), lax.rem(gy + dy + ny, ny))

    def inside(dy, dx):
        found = None
        for step, low, high in ((dy, at_low_y, at_high_y), (dx, at_low_x, at_high_x)):
            if step:
                here = jnp.logical_not(low if step < 0 else high)
                found = here if found is None else found & here
        return found

    barrier = pltpu.get_barrier_semaphore()
    for dy, dx in AROUND:

        @pl.when(inside(dy, dx))
        def _():
            pl.semaphore_signal(barrier, inc=1, device_id=device(dy, dx), device_id_type=MESH)

    loads = []
    for n, (source, target) in enumerate(
        (
            (tile_hbm, tile_ref), (second_hbm, second), (third_hbm, third), (first_hbm, first_ref),
            (place_hbm, place), (head_hbm, head_ref), (columns_hbm, columns_ref), (blend_hbm, blend),
        )
    ):
        loads.append(pltpu.make_async_copy(source, target, load_sem.at[n]))
        loads[-1].start()

    loads[0].wait()
    turned = tile_ref[...].astype(F32).reshape(Z * TY, TX).T
    strips[0] = turned[0:16].astype(BF)
    strips[1] = turned[TX - 16 : TX].astype(BF)
    beside_y = 2 - at_low_y.astype(jnp.int32) - at_high_y.astype(jnp.int32)
    beside_x = 2 - at_low_x.astype(jnp.int32) - at_high_x.astype(jnp.int32)
    pl.semaphore_wait(barrier, (beside_y + 1) * (beside_x + 1) - 1)
    copies = []
    for n, (dy, dx) in enumerate(AROUND):
        if dx == 0:
            source, target = tile_ref, rows_in.at[0 if dy == 1 else 1]
        else:
            source, target = strips.at[0 if dx == -1 else 1], sides_in.at[1 - dy, 0 if dx == 1 else 1]
        copies.append(
            pltpu.make_async_remote_copy(
                src_ref=source,
                dst_ref=target,
                send_sem=send_sem.at[n],
                recv_sem=recv_sem.at[n],
                device_id=device(dy, dx),
                device_id_type=MESH,
            )
        )
        pl.when(inside(dy, dx))(copies[-1].start)

    for load in loads[1:]:
        load.wait()
    build_conv_weights(second, near2, far2)
    build_conv_weights(third, near3, far3)
    taps[...] = jnp.zeros((32, C), F32)
    for n in range(9):
        taps[3 * n : 3 * n + 3, :] = first_ref[n].astype(F32)
    tap = taps[...].astype(BF)
    nothing = jnp.zeros((32, C), BF)
    spread = jnp.concatenate(
        [jnp.concatenate([tap if i == q else nothing for i in range(4)], axis=1) for q in range(4)], axis=0
    )
    for pair in range(STEM_PAIRS):
        w1[pair] = jnp.dot(place[pair], spread, preferred_element_type=F32).astype(BF)
    for py in range(2):
        wh[py * C : py * C + C, :] = jnp.dot(
            head_ref[...], columns_ref[py], preferred_element_type=F32
        ).astype(BF)

    lane8 = lax.broadcasted_iota(jnp.int32, (TY, TX), 1)
    lane128 = lax.broadcasted_iota(jnp.int32, (Z * TY, TX), 1)
    end = lax.broadcasted_iota(jnp.int32, (1, TY, TX), 2) == TX - 1
    for buffer in (main, edge):
        for half in range(2):
            buffer[half, 0] = jnp.zeros((2 * TY, TX), F32)
            buffer[half, Z + 1] = jnp.zeros((2 * TY, TX), F32)
    filler = jnp.zeros((2 * TY, TX), F32)

    def turn(buffer, z):
        parts = []
        for half in range(2):
            parts += [buffer[half, z], buffer[half, z + 1], buffer[half, z + 2], filler]
        return jnp.concatenate(parts, axis=0).T

    own = tile_ref[...].astype(F32)
    main[0, 1 : Z + 1, 0:TY, :] = own
    main[1, 1 : Z + 1, 0:TY, :] = jnp.where(end, 0.0, pltpu.roll(own, TX - 1, axis=2))
    for half in range(2):
        main[half, 1 : Z + 1, TY : 2 * TY, :] = jnp.zeros((Z, TY, TX), F32)
    for z in range(Z):
        qf[pl.ds(8 * Z + z, TX, stride=Z), :] = turn(main, z)
    for m in range(3, STEM_X - 2):
        qb[m] = qf[(2 * m + 3) * Z : (2 * m + 4) * Z, :].astype(BF)

    def stem_rows(pair, spans):
        parts = []
        for k in range(2):
            part = join([qb[begin + k : end + k] for begin, end in spans])
            parts.append(part.reshape(-1, 128))
        acc = jnp.dot(jnp.concatenate(parts, axis=1), w1[pair], preferred_element_type=F32)
        outside = (at_low_y & (pair == 0)) | (at_high_y & (pair == STEM_PAIRS - 1))
        acc = jnp.maximum(acc, 0.0) * jnp.where(outside, 0.0, 1.0)
        for qx in range(2):
            value = acc[:, qx * 128 : qx * 128 + 128].astype(BF).reshape(-1, Z, 128)
            at = 0
            for begin, end in spans:
                stem[pair, qx, begin:end] = value[at : at + end - begin]
                at += end - begin

    upper = lax.broadcasted_iota(jnp.int32, (1, 1, 128), 2) // C

    def inner_rows(pair, spans):
        sums = conv_rows(stem, pair, spans, near2, far2)
        low = jnp.where(at_low_y & (pair == 0), 0, -1)
        high = jnp.where(at_high_y & (pair == INNER_PAIRS - 1), 1, -1)
        keep = jnp.where((upper == low) | (upper == high), 0.0, 1.0)
        for qx in range(2):
            value = (jnp.maximum(sums[qx], 0.0) * keep).astype(BF)
            at = 0
            for begin, end in spans:
                inner[pair, qx, begin:end] = value[at : at + end - begin]
                at += end - begin

    def loop(count, pair_of, body):
        def step(n, carry):
            body(pair_of(n))
            return carry

        lax.fori_loop(0, count, step, 0, unroll=True)

    loop(2, lambda n: n + 2, lambda pair: stem_rows(pair, STEM_OWN))
    inner_rows(2, INNER_OWN)

    for copy, (dy, dx) in zip(copies, AROUND):
        pl.when(inside(dy, dx))(copy.wait_send)
        pl.when(inside(-dy, -dx))(copy.wait_recv)

    right_ok = jnp.where(at_high_x, 0, 64)
    left_ok = jnp.where(at_low_x, 128, 64)
    between = jnp.zeros((TX - 32, Z * TY), F32)
    middles, sideways = [], []
    for ty in range(3):
        left, right = sides_in[ty, 0].astype(F32), sides_in[ty, 1].astype(F32)
        sides = jnp.concatenate([right, between, left], axis=0).T
        sides = jnp.where((lane128 < right_ok) | (lane128 >= left_ok), sides, 0.0)
        sides = sides.reshape(Z, TY, TX)
        middle = own if ty == 1 else rows_in[ty // 2].astype(F32)
        if ty != 1:
            outside = at_low_y if ty == 0 else at_high_y
            middle, sides = jnp.where(outside, 0.0, middle), jnp.where(outside, 0.0, sides)
        middles.append(middle)
        sideways.append(sides)
    row8 = lax.broadcasted_iota(jnp.int32, (1, TY, TX), 1)
    for part in range(2):
        if part == 0:
            middle, sides = middles[1], sideways[1]
        else:
            middle = jnp.where(row8 < 4, middles[2], middles[0])
            sides = jnp.where(row8 < 4, sideways[2], sideways[0])
        next_middle, next_sides = pltpu.roll(middle, TX - 1, axis=2), pltpu.roll(sides, TX - 1, axis=2)
        rows = slice(part * TY, part * TY + TY)
        main[0, 1 : Z + 1, rows, :] = middle
        main[1, 1 : Z + 1, rows, :] = jnp.where(end, next_sides, next_middle)
        edge[0, 1 : Z + 1, rows, :] = sides
        edge[1, 1 : Z + 1, rows, :] = jnp.where(end, next_middle, next_sides)
    for z in range(Z):
        sides = turn(edge, z)
        qf[pl.ds(8 * Z + z, TX, stride=Z), :] = turn(main, z)
        qf[pl.ds(z, 8, stride=Z), :] = sides[120:128]
        qf[pl.ds(136 * Z + z, 8, stride=Z), :] = sides[0:8]
    for m in range(STEM_X + 1):
        qb[m] = qf[(2 * m + 3) * Z : (2 * m + 4) * Z, :].astype(BF)

    loop(4, lambda n: n + n // 2 * 2, lambda pair: stem_rows(pair, ((0, STEM_X),)))
    loop(2, lambda n: n + 2, lambda pair: stem_rows(pair, STEM_SIDES))

    @pl.when(at_low_x)
    def _():
        zero_columns(stem, range(4))

    @pl.when(at_high_x)
    def _():
        zero_columns(stem, range(132, 136))

    loop(4, lambda n: n + n // 2, lambda pair: inner_rows(pair, ((0, INNER_X),)))
    inner_rows(2, INNER_SIDES)

    @pl.when(at_low_x)
    def _():
        zero_columns(inner, range(3))

    @pl.when(at_high_x)
    def _():
        zero_columns(inner, range(131, 134))

    def block_body(pair):
        sums = conv_rows(inner, pair, ((0, BLOCK_X),), near3, far3)
        for qx in range(2):
            old = stem[pair + 1, qx, 1 : 1 + BLOCK_X].astype(F32)
            value = jnp.maximum(sums[qx] + old, 0.0).astype(BF).reshape(BLOCK_X * Z, 128)
            logits = jnp.dot(value, wh[...], preferred_element_type=F32)
            pred[pair, qx] = jnp.tanh(logits).astype(BF).reshape(BLOCK_X, Z, 256)

        @pl.when(at_low_x)
        def _():
            for parity in range(2):
                pred[pair, parity, 0] = jnp.zeros((Z, 256), BF)

        @pl.when(at_high_x)
        def _():
            for parity in range(2):
                pred[pair, parity, BLOCK_X - 1] = jnp.zeros((Z, 256), BF)

    lanes = lax.broadcasted_iota(jnp.int32, (1, Z, 128), 2)

    def blend_rows(pairs, first, more):
        def body(step, carry):
            j = step * XB
            for qx in range(2):
                operands = []
                for pair in pairs:
                    for half in range(2):
                        chosen = None
                        for n, a in enumerate((0, 1, 2) if half == 0 else (2, 3, 4)):
                            at = qx - a + 4
                            part = pred[pair, at % 2, pl.ds(j + at // 2, XB), :, half * 128 : half * 128 + 128]
                            chosen = part if n == 0 else jnp.where(lanes >= A_START[half][n], part, chosen)
                        operands.append(chosen.reshape(XB * Z, 128))
                added = jnp.dot(
                    jnp.concatenate(operands, axis=1),
                    blend[first : first + 256 * len(pairs), :],
                    preferred_element_type=F32,
                )
                added = added.reshape(XB, Z, 128)
                at = pl.ds(j, XB)
                total[at, qx] = total[at, qx] + added if more else added
            return carry

        lax.fori_loop(0, TX // 2 // XB, body, 0)

    def turned_total(z):
        return total.reshape(TX * Z, 128)[pl.ds(z, TX, stride=Z), :].T

    def outer_body(step, carry):
        block_body(step * (BLOCK_PAIRS - 1))
        return carry

    lax.fori_loop(0, 2, outer_body, 0)
    blend_rows((0, BLOCK_PAIRS - 1), 0, False)
    for z in range(Z):
        both = turned_total(z)
        for side in range(2):
            edge_out[side, z] = both[24 + 8 * side : 32 + 8 * side]
    edges = []
    for side, dy in enumerate((-1, 1)):
        edges.append(
            pltpu.make_async_remote_copy(
                src_ref=edge_out.at[side],
                dst_ref=edge_in.at[side],
                send_sem=edge_send_sem.at[side],
                recv_sem=edge_recv_sem.at[side],
                device_id=device(dy, 0),
                device_id_type=MESH,
            )
        )
        pl.when(inside(dy, 0))(edges[-1].start)

    def middle_body(step, carry):
        block_body(step + 1)
        return carry

    lax.fori_loop(0, BLOCK_PAIRS - 2, middle_body, 0)
    blend_rows(tuple(range(1, BLOCK_PAIRS - 1)), 512, True)

    y8 = lax.broadcasted_iota(jnp.int32, (TY, TX), 0)
    scale = 0.5 / (coverage_of(gy * TY + y8, ny * TY) * coverage_of(gx * TX + lane8, nx * TX))
    from_above = (y8 < 2) & (gy > 0)
    from_below = (y8 >= TY - 2) & (gy < ny - 1)
    for copy, dy in zip(edges, (-1, 1)):
        pl.when(inside(dy, 0))(copy.wait_send)
        pl.when(inside(-dy, 0))(copy.wait_recv)
    for z in range(Z):
        both = turned_total(z)
        below, above = edge_in[0, z], edge_in[1, z]
        for c in range(3):
            added = both[c * TY : c * TY + TY, :]
            added += jnp.where(from_above, above if c == 0 else pltpu.roll(above, TY - 2 * c, axis=0), 0.0)
            added += jnp.where(from_below, pltpu.roll(below, TY - 2 - 2 * c, axis=0), 0.0)
            out_ref[c, z] = 0.5 + added * scale


def lane_plan():
    plan, starts = [], []
    for half in range(2):
        lanes, begin = [], []
        for a in (0, 1, 2) if half == 0 else (2, 3, 4):
            begin.append(len(lanes))
            for py in range(2):
                if a == 2 and py != half:
                    continue
                lanes += [(a, py, b, c) for b in range(5) for c in range(3)]
        plan.append(lanes)
        starts.append(begin)
    return plan, starts


LANES, A_START = lane_plan()


def constants():
    place = np.zeros((STEM_PAIRS, 4, 64, 128), np.float32)
    for pair in range(STEM_PAIRS):
        for qx in range(2):
            for qy in range(2):
                for dz in range(3):
                    for dy in range(3):
                        for dx in range(3):
                            y = (2 * pair + qy + dy - 3) % 16
                            place[pair, qx + dx, dz * 16 + y, (qx * 2 + qy) * 32 + (dz * 3 + dy) * 3 + dx] = 1
    columns = np.zeros((2, 75, 256), np.float32)
    pairs = (0, BLOCK_PAIRS - 1) + tuple(range(1, BLOCK_PAIRS - 1))
    blend = np.zeros((len(pairs), 256, 128), np.float32)
    for half in range(2):
        for n, (a, py, b, c) in enumerate(LANES[half]):
            columns[py, (a * 5 + b) * 3 + c, half * 128 + n] = 0.5
            for i, pair in enumerate(pairs):
                y = 2 * pair + py + b - R
                if y < 0:
                    lane = 24 + 2 * c + y + R
                elif y >= TY:
                    lane = 32 + 2 * c + y - TY
                else:
                    lane = c * TY + y
                blend[i, half * 128 + n, lane] = (R + 1 - abs(a - R)) * (R + 1 - abs(b - R))
    return (
        jnp.asarray(place.reshape(STEM_PAIRS, 256, 128), BF),
        jnp.asarray(columns, BF),
        jnp.asarray(blend.reshape(-1, 128), BF),
    )


def local(intensity, first_kernel, second_kernel, third_kernel, head_weight):
    place, columns, blend = constants()
    vmem = pl.BlockSpec(memory_space=pltpu.VMEM)
    hbm = pl.BlockSpec(memory_space=pltpu.HBM)
    return pl.pallas_call(
        compute_kernel,
        out_shape=jax.ShapeDtypeStruct((3, Z, TY, TX), F32),
        in_specs=[hbm] * 8,
        out_specs=vmem,
        scratch_shapes=[
            pltpu.VMEM(intensity.shape, BF),
            pltpu.VMEM(place.shape, BF),
            pltpu.VMEM((9, 3, C), BF),
            pltpu.VMEM((27, C, C), BF),
            pltpu.VMEM((27, C, C), BF),
            pltpu.VMEM(head_weight.shape, BF),
            pltpu.VMEM(columns.shape, BF),
            pltpu.VMEM(blend.shape, BF),
            pltpu.VMEM((2, 16, Z * TY), BF),
            pltpu.VMEM((2, Z, TY, TX), BF),
            pltpu.VMEM((3, 2, 16, Z * TY), BF),
            pltpu.VMEM((2, Z, TY, TX), F32),
            pltpu.VMEM((2, Z, TY, TX), F32),
            pltpu.VMEM((32, C), F32),
            pltpu.VMEM((STEM_PAIRS, 256, 256), BF),
            pltpu.VMEM((768, 256), BF),
            pltpu.VMEM((1024, 256), BF),
            pltpu.VMEM((768, 256), BF),
            pltpu.VMEM((1024, 256), BF),
            pltpu.VMEM((128, 256), BF),
            pltpu.VMEM((2, Z + 2, 2 * TY, TX), F32),
            pltpu.VMEM((2, Z + 2, 2 * TY, TX), F32),
            pltpu.VMEM((144 * Z, 128), F32),
            pltpu.VMEM((STEM_X + 1, Z, 128), BF),
            pltpu.VMEM((STEM_PAIRS, 2, STEM_X, Z, 128), BF),
            pltpu.VMEM((INNER_PAIRS, 2, INNER_X, Z, 128), BF),
            pltpu.VMEM((BLOCK_PAIRS, 2, BLOCK_X, Z, 256), BF),
            pltpu.VMEM((TX // 2, 2, Z, 128), F32),
            pltpu.SemaphoreType.DMA((8,)),
            pltpu.SemaphoreType.DMA((8,)),
            pltpu.SemaphoreType.DMA((8,)),
            pltpu.SemaphoreType.DMA((2,)),
            pltpu.SemaphoreType.DMA((2,)),
        ],
        compiler_params=pltpu.CompilerParams(
            collective_id=0, has_side_effects=True, vmem_limit_bytes=56 * 2**20
        ),
        name="convnet",
    )(
        intensity, place, first_kernel.reshape(9, 3, C),
        second_kernel.reshape(27, C, C), third_kernel.reshape(27, C, C), head_weight, columns, blend,
    )


def solution(mesh):
    in_specs = (P(None, "gy", "gx"), P(), P(), P(), P())
    out_specs = P(None, None, "gy", "gx")
    return jax.shard_map(local, mesh=mesh, in_specs=in_specs, out_specs=out_specs, check_vma=False)
```

```python
import functools

import jax
import jax.numpy as jnp
import numpy as np
from jax import lax
from jax.experimental import pallas as pl
from jax.experimental.pallas import tpu as pltpu
from jax.sharding import PartitionSpec as P

R = 2
C = 64
Z = 16
TY = 8
TX = 128
BF = jnp.bfloat16
F32 = jnp.float32
MESH = pl.DeviceIdType.MESH


STEM_PAIRS = 6
INNER_PAIRS = 5
BLOCK_PAIRS = 4
STEM_X = 68
INNER_X = 67
BLOCK_X = 66
XB = 64
STEM_OWN, STEM_SIDES = ((3, 65),), ((0, 3), (65, STEM_X))
INNER_OWN, INNER_SIDES = ((3, 64),), ((0, 3), (64, INNER_X))
AROUND = [(dy, dx) for dy in (-1, 0, 1) for dx in (-1, 0, 1) if (dy, dx) != (0, 0)]


def join(parts):
    return parts[0] if len(parts) == 1 else jnp.concatenate(parts, axis=0)


def conv_rows(ref, pair, spans, near, far):
    count = sum(end - begin for begin, end in spans)

    def operand(offsets):
        parts = []
        for offset in offsets:
            for k in range(2):
                at = offset // 2
                part = join([ref[pair + k, offset % 2, begin + at : end + at] for begin, end in spans])
                parts.append(part.reshape(count * Z, 2 * C))
        return jnp.concatenate(parts, axis=1)

    row = lax.broadcasted_iota(jnp.int32, (1, Z, 2 * C), 1)
    third = jnp.dot(operand(range(4)), far[...], preferred_element_type=F32)
    out = []
    for qx in range(2):
        both = jnp.dot(operand(range(qx, qx + 3)), near[...], preferred_element_type=F32)
        below = both[:, :128].reshape(count, Z, 128)
        above = third[:, qx * 128 : qx * 128 + 128].reshape(count, Z, 128)
        total = both[:, 128:].reshape(count, Z, 128)
        total += jnp.where(row == 0, 0.0, pltpu.roll(below, 1, axis=1))
        total += jnp.where(row == Z - 1, 0.0, pltpu.roll(above, Z - 1, axis=1))
        out.append(total)
    return out


def build_conv_weights(kernel_ref, near, far):
    zero = jnp.zeros((C, C), BF)

    def band(dz, dx, source):
        blocks = []
        for qy in range(2):
            dy = source - qy
            inside = 0 <= dx < 3 and 0 <= dy < 3
            blocks.append(kernel_ref[(dz * 3 + dy) * 3 + dx] if inside else zero)
        return jnp.concatenate(blocks, axis=1)

    for source in range(4):
        for dx in range(3):
            rows = (dx * 4 + source) * C
            for dz in range(2):
                near[rows : rows + C, dz * 128 : dz * 128 + 128] = band(dz, dx, source)
        for offset in range(4):
            rows = (offset * 4 + source) * C
            for qx in range(2):
                far[rows : rows + C, qx * 128 : qx * 128 + 128] = band(2, offset - qx, source)


def zero_columns(ref, columns):
    for pair in range(ref.shape[0]):
        for x in columns:
            ref[pair, x % 2, x // 2] = jnp.zeros((Z, 2 * C), BF)


def coverage_of(position, length):
    total = jnp.zeros(position.shape, F32)
    for b in range(2 * R + 1):
        source = position - (b - R)
        total += jnp.where((source >= 0) & (source < length), float(R + 1 - abs(b - R)), 0.0)
    return total


def compute_kernel(
    tile_hbm, place_hbm, first_hbm, second_hbm, third_hbm, head_hbm, columns_hbm, blend_hbm,
    out_ref,
    tile_ref, place, first_ref, second, third, head_ref, columns_ref, blend,
    strips, rows_in, sides_in, edge_out, edge_in,
    taps, w1, near2, far2, near3, far3, wh, main, edge, qf, qb, stem, inner, pred, total,
    load_sem, send_sem, recv_sem, edge_send_sem, edge_recv_sem,
):
    gx, gy = lax.axis_index("gx"), lax.axis_index("gy")
    nx, ny = lax.axis_size("gx"), lax.axis_size("gy")
    at_low_x, at_high_x = gx == 0, gx == nx - 1
    at_low_y, at_high_y = gy == 0, gy == ny - 1

    def device(dy, dx):
        return (lax.rem(gx + dx + nx, nx), lax.rem(gy + dy + ny, ny))

    def inside(dy, dx):
        found = None
        for step, low, high in ((dy, at_low_y, at_high_y), (dx, at_low_x, at_high_x)):
            if step:
                here = jnp.logical_not(low if step < 0 else high)
                found = here if found is None else found & here
        return found

    barrier = pltpu.get_barrier_semaphore()
    for dy, dx in AROUND:

        @pl.when(inside(dy, dx))
        def _():
            pl.semaphore_signal(barrier, inc=1, device_id=device(dy, dx), device_id_type=MESH)

    loads = []
    for n, (source, target) in enumerate(
        (
            (tile_hbm, tile_ref), (second_hbm, second), (third_hbm, third), (first_hbm, first_ref),
            (place_hbm, place), (head_hbm, head_ref), (columns_hbm, columns_ref), (blend_hbm, blend),
        )
    ):
        loads.append(pltpu.make_async_copy(source, target, load_sem.at[n]))
        loads[-1].start()

    loads[0].wait()
    turned = tile_ref[...].astype(F32).reshape(Z * TY, TX).T
    strips[0] = turned[0:16].astype(BF)
    strips[1] = turned[TX - 16 : TX].astype(BF)
    beside_y = 2 - at_low_y.astype(jnp.int32) - at_high_y.astype(jnp.int32)
    beside_x = 2 - at_low_x.astype(jnp.int32) - at_high_x.astype(jnp.int32)
    pl.semaphore_wait(barrier, (beside_y + 1) * (beside_x + 1) - 1)
    copies = []
    for n, (dy, dx) in enumerate(AROUND):
        if dx == 0:
            source, target = tile_ref, rows_in.at[0 if dy == 1 else 1]
        else:
            source, target = strips.at[0 if dx == -1 else 1], sides_in.at[1 - dy, 0 if dx == 1 else 1]
        copies.append(
            pltpu.make_async_remote_copy(
                src_ref=source,
                dst_ref=target,
                send_sem=send_sem.at[n],
                recv_sem=recv_sem.at[n],
                device_id=device(dy, dx),
                device_id_type=MESH,
            )
        )
        pl.when(inside(dy, dx))(copies[-1].start)

    for load in loads[1:]:
        load.wait()
    build_conv_weights(second, near2, far2)
    build_conv_weights(third, near3, far3)
    taps[...] = jnp.zeros((32, C), F32)
    for n in range(9):
        taps[3 * n : 3 * n + 3, :] = first_ref[n].astype(F32)
    tap = taps[...].astype(BF)
    nothing = jnp.zeros((32, C), BF)
    spread = jnp.concatenate(
        [jnp.concatenate([tap if i == q else nothing for i in range(4)], axis=1) for q in range(4)], axis=0
    )
    for pair in range(STEM_PAIRS):
        w1[pair] = jnp.dot(place[pair], spread, preferred_element_type=F32).astype(BF)
    for py in range(2):
        wh[py * C : py * C + C, :] = jnp.dot(
            head_ref[...], columns_ref[py], preferred_element_type=F32
        ).astype(BF)

    lane8 = lax.broadcasted_iota(jnp.int32, (TY, TX), 1)
    lane128 = lax.broadcasted_iota(jnp.int32, (Z * TY, TX), 1)
    end = lax.broadcasted_iota(jnp.int32, (1, TY, TX), 2) == TX - 1
    for buffer in (main, edge):
        for half in range(2):
            buffer[half, 0] = jnp.zeros((2 * TY, TX), F32)
            buffer[half, Z + 1] = jnp.zeros((2 * TY, TX), F32)
    filler = jnp.zeros((2 * TY, TX), F32)

    def turn(buffer, z):
        parts = []
        for half in range(2):
            parts += [buffer[half, z], buffer[half, z + 1], buffer[half, z + 2], filler]
        return jnp.concatenate(parts, axis=0).T

    own = tile_ref[...].astype(F32)
    main[0, 1 : Z + 1, 0:TY, :] = own
    main[1, 1 : Z + 1, 0:TY, :] = jnp.where(end, 0.0, pltpu.roll(own, TX - 1, axis=2))
    for half in range(2):
        main[half, 1 : Z + 1, TY : 2 * TY, :] = jnp.zeros((Z, TY, TX), F32)
    for z in range(Z):
        qf[pl.ds(8 * Z + z, TX, stride=Z), :] = turn(main, z)
    for m in range(3, STEM_X - 2):
        qb[m] = qf[(2 * m + 3) * Z : (2 * m + 4) * Z, :].astype(BF)

    def stem_rows(pair, spans):
        parts = []
        for k in range(2):
            part = join([qb[begin + k : end + k] for begin, end in spans])
            parts.append(part.reshape(-1, 128))
        acc = jnp.dot(jnp.concatenate(parts, axis=1), w1[pair], preferred_element_type=F32)
        outside = (at_low_y & (pair == 0)) | (at_high_y & (pair == STEM_PAIRS - 1))
        acc = jnp.maximum(acc, 0.0) * jnp.where(outside, 0.0, 1.0)
        for qx in range(2):
            value = acc[:, qx * 128 : qx * 128 + 128].astype(BF).reshape(-1, Z, 128)
            at = 0
            for begin, end in spans:
                stem[pair, qx, begin:end] = value[at : at + end - begin]
                at += end - begin

    upper = lax.broadcasted_iota(jnp.int32, (1, 1, 128), 2) // C

    def inner_rows(pair, spans):
        sums = conv_rows(stem, pair, spans, near2, far2)
        low = jnp.where(at_low_y & (pair == 0), 0, -1)
        high = jnp.where(at_high_y & (pair == INNER_PAIRS - 1), 1, -1)
        keep = jnp.where((upper == low) | (upper == high), 0.0, 1.0)
        for qx in range(2):
            value = (jnp.maximum(sums[qx], 0.0) * keep).astype(BF)
            at = 0
            for begin, end in spans:
                inner[pair, qx, begin:end] = value[at : at + end - begin]
                at += end - begin

    def loop(count, pair_of, body):
        def step(n, carry):
            body(pair_of(n))
            return carry

        lax.fori_loop(0, count, step, 0, unroll=True)

    loop(2, lambda n: n + 2, lambda pair: stem_rows(pair, STEM_OWN))
    inner_rows(2, INNER_OWN)

    for copy, (dy, dx) in zip(copies, AROUND):
        pl.when(inside(dy, dx))(copy.wait_send)
        pl.when(inside(-dy, -dx))(copy.wait_recv)

    right_ok = jnp.where(at_high_x, 0, 64)
    left_ok = jnp.where(at_low_x, 128, 64)
    between = jnp.zeros((TX - 32, Z * TY), F32)
    middles, sideways = [], []
    for ty in range(3):
        left, right = sides_in[ty, 0].astype(F32), sides_in[ty, 1].astype(F32)
        sides = jnp.concatenate([right, between, left], axis=0).T
        sides = jnp.where((lane128 < right_ok) | (lane128 >= left_ok), sides, 0.0)
        sides = sides.reshape(Z, TY, TX)
        middle = own if ty == 1 else rows_in[ty // 2].astype(F32)
        if ty != 1:
            outside = at_low_y if ty == 0 else at_high_y
            middle, sides = jnp.where(outside, 0.0, middle), jnp.where(outside, 0.0, sides)
        middles.append(middle)
        sideways.append(sides)
    row8 = lax.broadcasted_iota(jnp.int32, (1, TY, TX), 1)
    for part in range(2):
        if part == 0:
            middle, sides = middles[1], sideways[1]
        else:
            middle = jnp.where(row8 < 4, middles[2], middles[0])
            sides = jnp.where(row8 < 4, sideways[2], sideways[0])
        next_middle, next_sides = pltpu.roll(middle, TX - 1, axis=2), pltpu.roll(sides, TX - 1, axis=2)
        rows = slice(part * TY, part * TY + TY)
        main[0, 1 : Z + 1, rows, :] = middle
        main[1, 1 : Z + 1, rows, :] = jnp.where(end, next_sides, next_middle)
        edge[0, 1 : Z + 1, rows, :] = sides
        edge[1, 1 : Z + 1, rows, :] = jnp.where(end, next_middle, next_sides)
    for z in range(Z):
        sides = turn(edge, z)
        qf[pl.ds(8 * Z + z, TX, stride=Z), :] = turn(main, z)
        qf[pl.ds(z, 8, stride=Z), :] = sides[120:128]
        qf[pl.ds(136 * Z + z, 8, stride=Z), :] = sides[0:8]
    for m in range(STEM_X + 1):
        qb[m] = qf[(2 * m + 3) * Z : (2 * m + 4) * Z, :].astype(BF)

    loop(4, lambda n: n + n // 2 * 2, lambda pair: stem_rows(pair, ((0, STEM_X),)))
    loop(2, lambda n: n + 2, lambda pair: stem_rows(pair, STEM_SIDES))

    @pl.when(at_low_x)
    def _():
        zero_columns(stem, range(4))

    @pl.when(at_high_x)
    def _():
        zero_columns(stem, range(132, 136))

    loop(4, lambda n: n + n // 2, lambda pair: inner_rows(pair, ((0, INNER_X),)))
    inner_rows(2, INNER_SIDES)

    @pl.when(at_low_x)
    def _():
        zero_columns(inner, range(3))

    @pl.when(at_high_x)
    def _():
        zero_columns(inner, range(131, 134))

    def block_body(pair):
        sums = conv_rows(inner, pair, ((0, BLOCK_X),), near3, far3)
        for qx in range(2):
            old = stem[pair + 1, qx, 1 : 1 + BLOCK_X].astype(F32)
            value = jnp.maximum(sums[qx] + old, 0.0).astype(BF).reshape(BLOCK_X * Z, 128)
            logits = jnp.dot(value, wh[...], preferred_element_type=F32)
            pred[pair, qx] = jnp.tanh(logits).astype(BF).reshape(BLOCK_X, Z, 256)

        @pl.when(at_low_x)
        def _():
            for parity in range(2):
                pred[pair, parity, 0] = jnp.zeros((Z, 256), BF)

        @pl.when(at_high_x)
        def _():
            for parity in range(2):
                pred[pair, parity, BLOCK_X - 1] = jnp.zeros((Z, 256), BF)

    lanes = lax.broadcasted_iota(jnp.int32, (1, Z, 128), 2)

    def blend_rows(pairs, first, more):
        def body(step, carry):
            j = step * XB
            for qx in range(2):
                operands = []
                for pair in pairs:
                    for half in range(2):
                        chosen = None
                        for n, a in enumerate((0, 1, 2) if half == 0 else (2, 3, 4)):
                            at = qx - a + 4
                            part = pred[pair, at % 2, pl.ds(j + at // 2, XB), :, half * 128 : half * 128 + 128]
                            chosen = part if n == 0 else jnp.where(lanes >= A_START[half][n], part, chosen)
                        operands.append(chosen.reshape(XB * Z, 128))
                added = jnp.dot(
                    jnp.concatenate(operands, axis=1),
                    blend[first : first + 256 * len(pairs), :],
                    preferred_element_type=F32,
                )
                added = added.reshape(XB, Z, 128)
                at = pl.ds(j, XB)
                total[at, qx] = total[at, qx] + added if more else added
            return carry

        lax.fori_loop(0, TX // 2 // XB, body, 0)

    def turned_total(z):
        return total.reshape(TX * Z, 128)[pl.ds(z, TX, stride=Z), :].T

    def outer_body(step, carry):
        block_body(step * (BLOCK_PAIRS - 1))
        return carry

    lax.fori_loop(0, 2, outer_body, 0)
    blend_rows((0, BLOCK_PAIRS - 1), 0, False)
    for z in range(Z):
        both = turned_total(z)
        for side in range(2):
            edge_out[side, z] = both[24 + 8 * side : 32 + 8 * side]
    edges = []
    for side, dy in enumerate((-1, 1)):
        edges.append(
            pltpu.make_async_remote_copy(
                src_ref=edge_out.at[side],
                dst_ref=edge_in.at[side],
                send_sem=edge_send_sem.at[side],
                recv_sem=edge_recv_sem.at[side],
                device_id=device(dy, 0),
                device_id_type=MESH,
            )
        )
        pl.when(inside(dy, 0))(edges[-1].start)

    def middle_body(step, carry):
        block_body(step + 1)
        return carry

    lax.fori_loop(0, BLOCK_PAIRS - 2, middle_body, 0)
    blend_rows(tuple(range(1, BLOCK_PAIRS - 1)), 512, True)

    y8 = lax.broadcasted_iota(jnp.int32, (TY, TX), 0)
    scale = 0.5 / (coverage_of(gy * TY + y8, ny * TY) * coverage_of(gx * TX + lane8, nx * TX))
    from_above = (y8 < 2) & (gy > 0)
    from_below = (y8 >= TY - 2) & (gy < ny - 1)
    for copy, dy in zip(edges, (-1, 1)):
        pl.when(inside(dy, 0))(copy.wait_send)
        pl.when(inside(-dy, 0))(copy.wait_recv)
    for z in range(Z):
        both = turned_total(z)
        below, above = edge_in[0, z], edge_in[1, z]
        for c in range(3):
            added = both[c * TY : c * TY + TY, :]
            added += jnp.where(from_above, above if c == 0 else pltpu.roll(above, TY - 2 * c, axis=0), 0.0)
            added += jnp.where(from_below, pltpu.roll(below, TY - 2 - 2 * c, axis=0), 0.0)
            out_ref[c, z] = 0.5 + added * scale


def lane_plan():
    plan, starts = [], []
    for half in range(2):
        lanes, begin = [], []
        for a in (0, 1, 2) if half == 0 else (2, 3, 4):
            begin.append(len(lanes))
            for py in range(2):
                if a == 2 and py != half:
                    continue
                lanes += [(a, py, b, c) for b in range(5) for c in range(3)]
        plan.append(lanes)
        starts.append(begin)
    return plan, starts


LANES, A_START = lane_plan()


def constants():
    place = np.zeros((STEM_PAIRS, 4, 64, 128), np.float32)
    for pair in range(STEM_PAIRS):
        for qx in range(2):
            for qy in range(2):
                for dz in range(3):
                    for dy in range(3):
                        for dx in range(3):
                            y = (2 * pair + qy + dy - 3) % 16
                            place[pair, qx + dx, dz * 16 + y, (qx * 2 + qy) * 32 + (dz * 3 + dy) * 3 + dx] = 1
    columns = np.zeros((2, 75, 256), np.float32)
    pairs = (0, BLOCK_PAIRS - 1) + tuple(range(1, BLOCK_PAIRS - 1))
    blend = np.zeros((len(pairs), 256, 128), np.float32)
    for half in range(2):
        for n, (a, py, b, c) in enumerate(LANES[half]):
            columns[py, (a * 5 + b) * 3 + c, half * 128 + n] = 0.5
            for i, pair in enumerate(pairs):
                y = 2 * pair + py + b - R
                if y < 0:
                    lane = 24 + 2 * c + y + R
                elif y >= TY:
                    lane = 32 + 2 * c + y - TY
                else:
                    lane = c * TY + y
                blend[i, half * 128 + n, lane] = (R + 1 - abs(a - R)) * (R + 1 - abs(b - R))
    return (
        jnp.asarray(place.reshape(STEM_PAIRS, 256, 128), BF),
        jnp.asarray(columns, BF),
        jnp.asarray(blend.reshape(-1, 128), BF),
    )


def local(intensity, first_kernel, second_kernel, third_kernel, head_weight):
    place, columns, blend = constants()
    vmem = pl.BlockSpec(memory_space=pltpu.VMEM)
    hbm = pl.BlockSpec(memory_space=pltpu.HBM)
    return pl.pallas_call(
        compute_kernel,
        out_shape=pltpu.VMEM((3, Z, TY, TX), F32),
        in_specs=[hbm] * 8,
        out_specs=vmem,
        scratch_shapes=[
            pltpu.VMEM(intensity.shape, BF),
            pltpu.VMEM(place.shape, BF),
            pltpu.VMEM((9, 3, C), BF),
            pltpu.VMEM((27, C, C), BF),
            pltpu.VMEM((27, C, C), BF),
            pltpu.VMEM(head_weight.shape, BF),
            pltpu.VMEM(columns.shape, BF),
            pltpu.VMEM(blend.shape, BF),
            pltpu.VMEM((2, 16, Z * TY), BF),
            pltpu.VMEM((2, Z, TY, TX), BF),
            pltpu.VMEM((3, 2, 16, Z * TY), BF),
            pltpu.VMEM((2, Z, TY, TX), F32),
            pltpu.VMEM((2, Z, TY, TX), F32),
            pltpu.VMEM((32, C), F32),
            pltpu.VMEM((STEM_PAIRS, 256, 256), BF),
            pltpu.VMEM((768, 256), BF),
            pltpu.VMEM((1024, 256), BF),
            pltpu.VMEM((768, 256), BF),
            pltpu.VMEM((1024, 256), BF),
            pltpu.VMEM((128, 256), BF),
            pltpu.VMEM((2, Z + 2, 2 * TY, TX), F32),
            pltpu.VMEM((2, Z + 2, 2 * TY, TX), F32),
            pltpu.VMEM((144 * Z, 128), F32),
            pltpu.VMEM((STEM_X + 1, Z, 128), BF),
            pltpu.VMEM((STEM_PAIRS, 2, STEM_X, Z, 128), BF),
            pltpu.VMEM((INNER_PAIRS, 2, INNER_X, Z, 128), BF),
            pltpu.VMEM((BLOCK_PAIRS, 2, BLOCK_X, Z, 256), BF),
            pltpu.VMEM((TX // 2, 2, Z, 128), F32),
            pltpu.SemaphoreType.DMA((8,)),
            pltpu.SemaphoreType.DMA((8,)),
            pltpu.SemaphoreType.DMA((8,)),
            pltpu.SemaphoreType.DMA((2,)),
            pltpu.SemaphoreType.DMA((2,)),
        ],
        compiler_params=pltpu.CompilerParams(
            collective_id=0, has_side_effects=True, vmem_limit_bytes=56 * 2**20
        ),
        name="convnet",
    )(
        intensity, place, first_kernel.reshape(9, 3, C),
        second_kernel.reshape(27, C, C), third_kernel.reshape(27, C, C), head_weight, columns, blend,
    )


def solution(mesh):
    in_specs = (P(None, "gy", "gx"), P(), P(), P(), P())
    out_specs = P(None, None, "gy", "gx")
    return jax.shard_map(local, mesh=mesh, in_specs=in_specs, out_specs=out_specs, check_vma=False)
```

```python
import functools

import jax
import jax.numpy as jnp
import numpy as np
from jax import lax
from jax.experimental import pallas as pl
from jax.experimental.pallas import tpu as pltpu
from jax.sharding import PartitionSpec as P

R = 2
C = 64
Z = 16
TY = 8
TX = 128
BF = jnp.bfloat16
F32 = jnp.float32
MESH = pl.DeviceIdType.MESH


STEM_PAIRS = 6
INNER_PAIRS = 5
BLOCK_PAIRS = 4
STEM_X = 68
INNER_X = 67
BLOCK_X = 66
XB = 64
STEM_OWN, STEM_SIDES = ((3, 65),), ((0, 3), (65, STEM_X))
INNER_OWN, INNER_SIDES = ((3, 64),), ((0, 3), (64, INNER_X))
AROUND = [(dy, dx) for dy in (-1, 0, 1) for dx in (-1, 0, 1) if (dy, dx) != (0, 0)]


def join(parts):
    return parts[0] if len(parts) == 1 else jnp.concatenate(parts, axis=0)


def conv_rows(ref, spans, near, far):
    count = sum(end - begin for _, begin, end in spans)

    def operand(offsets):
        parts = []
        for offset in offsets:
            for k in range(2):
                at = offset // 2
                part = join([ref[pair + k, offset % 2, begin + at : end + at] for pair, begin, end in spans])
                parts.append(part.reshape(count * Z, 2 * C))
        return jnp.concatenate(parts, axis=1)

    row = lax.broadcasted_iota(jnp.int32, (1, Z, 2 * C), 1)
    third = jnp.dot(operand(range(4)), far[...], preferred_element_type=F32)
    out = []
    for qx in range(2):
        both = jnp.dot(operand(range(qx, qx + 3)), near[...], preferred_element_type=F32)
        below = both[:, :128].reshape(count, Z, 128)
        above = third[:, qx * 128 : qx * 128 + 128].reshape(count, Z, 128)
        total = both[:, 128:].reshape(count, Z, 128)
        total += jnp.where(row == 0, 0.0, pltpu.roll(below, 1, axis=1))
        total += jnp.where(row == Z - 1, 0.0, pltpu.roll(above, Z - 1, axis=1))
        out.append(total)
    return out


def build_conv_weights(kernel_ref, near, far):
    zero = jnp.zeros((C, C), BF)

    def band(dz, dx, source):
        blocks = []
        for qy in range(2):
            dy = source - qy
            inside = 0 <= dx < 3 and 0 <= dy < 3
            blocks.append(kernel_ref[(dz * 3 + dy) * 3 + dx] if inside else zero)
        return jnp.concatenate(blocks, axis=1)

    for source in range(4):
        for dx in range(3):
            rows = (dx * 4 + source) * C
            for dz in range(2):
                near[rows : rows + C, dz * 128 : dz * 128 + 128] = band(dz, dx, source)
        for offset in range(4):
            rows = (offset * 4 + source) * C
            for qx in range(2):
                far[rows : rows + C, qx * 128 : qx * 128 + 128] = band(2, offset - qx, source)


def zero_columns(ref, columns):
    for pair in range(ref.shape[0]):
        for x in columns:
            ref[pair, x % 2, x // 2] = jnp.zeros((Z, 2 * C), BF)


def coverage_of(position, length):
    total = jnp.zeros(position.shape, F32)
    for b in range(2 * R + 1):
        source = position - (b - R)
        total += jnp.where((source >= 0) & (source < length), float(R + 1 - abs(b - R)), 0.0)
    return total


def compute_kernel(
    tile_hbm, place_hbm, first_hbm, second_hbm, third_hbm, head_hbm, columns_hbm, blend_hbm,
    out_ref,
    tile_ref, place, first_ref, second, third, head_ref, columns_ref, blend,
    strips, rows_in, sides_in, edge_out, edge_in,
    taps, w1, near2, far2, near3, far3, wh, main, edge, qf, qb, stem, inner, pred, total,
    load_sem, send_sem, recv_sem, edge_send_sem, edge_recv_sem,
):
    gx, gy = lax.axis_index("gx"), lax.axis_index("gy")
    nx, ny = lax.axis_size("gx"), lax.axis_size("gy")
    at_low_x, at_high_x = gx == 0, gx == nx - 1
    at_low_y, at_high_y = gy == 0, gy == ny - 1

    def device(dy, dx):
        return (lax.rem(gx + dx + nx, nx), lax.rem(gy + dy + ny, ny))

    def inside(dy, dx):
        found = None
        for step, low, high in ((dy, at_low_y, at_high_y), (dx, at_low_x, at_high_x)):
            if step:
                here = jnp.logical_not(low if step < 0 else high)
                found = here if found is None else found & here
        return found

    barrier = pltpu.get_barrier_semaphore()
    for dy, dx in AROUND:

        @pl.when(inside(dy, dx))
        def _():
            pl.semaphore_signal(barrier, inc=1, device_id=device(dy, dx), device_id_type=MESH)

    loads = []
    for n, (source, target) in enumerate(
        (
            (tile_hbm, tile_ref), (second_hbm, second), (third_hbm, third), (first_hbm, first_ref),
            (place_hbm, place), (head_hbm, head_ref), (columns_hbm, columns_ref), (blend_hbm, blend),
        )
    ):
        loads.append(pltpu.make_async_copy(source, target, load_sem.at[n]))
        loads[-1].start()

    loads[0].wait()
    turned = tile_ref[...].astype(F32).reshape(Z * TY, TX).T
    strips[0] = turned[0:16].astype(BF)
    strips[1] = turned[TX - 16 : TX].astype(BF)
    beside_y = 2 - at_low_y.astype(jnp.int32) - at_high_y.astype(jnp.int32)
    beside_x = 2 - at_low_x.astype(jnp.int32) - at_high_x.astype(jnp.int32)
    pl.semaphore_wait(barrier, (beside_y + 1) * (beside_x + 1) - 1)
    copies = []
    for n, (dy, dx) in enumerate(AROUND):
        if dx == 0:
            source, target = tile_ref, rows_in.at[0 if dy == 1 else 1]
        else:
            source, target = strips.at[0 if dx == -1 else 1], sides_in.at[1 - dy, 0 if dx == 1 else 1]
        copies.append(
            pltpu.make_async_remote_copy(
                src_ref=source,
                dst_ref=target,
                send_sem=send_sem.at[n],
                recv_sem=recv_sem.at[n],
                device_id=device(dy, dx),
                device_id_type=MESH,
            )
        )
        pl.when(inside(dy, dx))(copies[-1].start)

    for load in loads[1:]:
        load.wait()
    build_conv_weights(second, near2, far2)
    build_conv_weights(third, near3, far3)
    taps[...] = jnp.zeros((32, C), F32)
    for n in range(9):
        taps[3 * n : 3 * n + 3, :] = first_ref[n].astype(F32)
    tap = taps[...].astype(BF)
    nothing = jnp.zeros((32, C), BF)
    spread = jnp.concatenate(
        [jnp.concatenate([tap if i == q else nothing for i in range(4)], axis=1) for q in range(4)], axis=0
    )
    for pair in range(STEM_PAIRS):
        taken = jnp.dot(place[pair], spread, preferred_element_type=F32)
        if pair in (0, STEM_PAIRS - 1):
            taken = taken * jnp.where(at_low_y if pair == 0 else at_high_y, 0.0, 1.0)
        w1[pair] = taken.astype(BF)
    for py in range(2):
        wh[py * C : py * C + C, :] = jnp.dot(
            head_ref[...], columns_ref[py], preferred_element_type=F32
        ).astype(BF)

    lane8 = lax.broadcasted_iota(jnp.int32, (TY, TX), 1)
    lane128 = lax.broadcasted_iota(jnp.int32, (Z * TY, TX), 1)
    end = lax.broadcasted_iota(jnp.int32, (1, TY, TX), 2) == TX - 1
    for buffer in (main, edge):
        for half in range(2):
            buffer[half, 0] = jnp.zeros((2 * TY, TX), F32)
            buffer[half, Z + 1] = jnp.zeros((2 * TY, TX), F32)
    filler = jnp.zeros((2 * TY, TX), F32)

    def turn(buffer, z):
        parts = []
        for half in range(2):
            parts += [buffer[half, z], buffer[half, z + 1], buffer[half, z + 2], filler]
        return jnp.concatenate(parts, axis=0).T

    own = tile_ref[...].astype(F32)
    main[0, 1 : Z + 1, 0:TY, :] = own
    main[1, 1 : Z + 1, 0:TY, :] = jnp.where(end, 0.0, pltpu.roll(own, TX - 1, axis=2))
    for half in range(2):
        main[half, 1 : Z + 1, TY : 2 * TY, :] = jnp.zeros((Z, TY, TX), F32)
    for z in range(Z):
        qf[pl.ds(8 * Z + z, TX, stride=Z), :] = turn(main, z)
    for m in range(3, STEM_X - 2):
        qb[m] = qf[(2 * m + 3) * Z : (2 * m + 4) * Z, :].astype(BF)

    def stem_rows(pair, spans):
        parts = []
        for k in range(2):
            part = join([qb[begin + k : end + k] for begin, end in spans])
            parts.append(part.reshape(-1, 128))
        acc = jnp.dot(jnp.concatenate(parts, axis=1), w1[pair], preferred_element_type=F32)
        acc = jnp.maximum(acc, 0.0)
        for qx in range(2):
            value = acc[:, qx * 128 : qx * 128 + 128].astype(BF).reshape(-1, Z, 128)
            at = 0
            for begin, end in spans:
                stem[pair, qx, begin:end] = value[at : at + end - begin]
                at += end - begin

    upper = lax.broadcasted_iota(jnp.int32, (1, 1, 128), 2) // C

    def inner_rows(spans):
        sums = conv_rows(stem, spans, near2, far2)
        for qx in range(2):
            value = jnp.maximum(sums[qx], 0.0)
            at = 0
            for pair, begin, end in spans:
                part = value[at : at + end - begin]
                if pair == 0:
                    part = part * jnp.where(upper == jnp.where(at_low_y, 0, -1), 0.0, 1.0)
                if pair == INNER_PAIRS - 1:
                    part = part * jnp.where(upper == jnp.where(at_high_y, 1, -1), 0.0, 1.0)
                inner[pair, qx, begin:end] = part.astype(BF)
                at += end - begin

    def loop(count, pair_of, body):
        for n in range(count):
            body(pair_of(n))

    loop(2, lambda n: n + 2, lambda pair: stem_rows(pair, STEM_OWN))
    inner_rows([(2, begin, end) for begin, end in INNER_OWN])

    for copy, (dy, dx) in zip(copies, AROUND):
        pl.when(inside(dy, dx))(copy.wait_send)
        pl.when(inside(-dy, -dx))(copy.wait_recv)

    right_ok = jnp.where(at_high_x, 0, 64)
    left_ok = jnp.where(at_low_x, 128, 64)
    between = jnp.zeros((TX - 32, Z * TY), F32)
    middles, sideways = [], []
    for ty in range(3):
        left, right = sides_in[ty, 0].astype(F32), sides_in[ty, 1].astype(F32)
        sides = jnp.concatenate([right, between, left], axis=0).T
        sides = jnp.where((lane128 < right_ok) | (lane128 >= left_ok), sides, 0.0)
        sides = sides.reshape(Z, TY, TX)
        middle = own if ty == 1 else rows_in[ty // 2].astype(F32)
        if ty != 1:
            outside = at_low_y if ty == 0 else at_high_y
            middle, sides = jnp.where(outside, 0.0, middle), jnp.where(outside, 0.0, sides)
        middles.append(middle)
        sideways.append(sides)
    row8 = lax.broadcasted_iota(jnp.int32, (1, TY, TX), 1)
    for part in range(2):
        if part == 0:
            middle, sides = middles[1], sideways[1]
        else:
            middle = jnp.where(row8 < 4, middles[2], middles[0])
            sides = jnp.where(row8 < 4, sideways[2], sideways[0])
        next_middle, next_sides = pltpu.roll(middle, TX - 1, axis=2), pltpu.roll(sides, TX - 1, axis=2)
        rows = slice(part * TY, part * TY + TY)
        main[0, 1 : Z + 1, rows, :] = middle
        main[1, 1 : Z + 1, rows, :] = jnp.where(end, next_sides, next_middle)
        edge[0, 1 : Z + 1, rows, :] = sides
        edge[1, 1 : Z + 1, rows, :] = jnp.where(end, next_middle, next_sides)
    for z in range(Z):
        sides = turn(edge, z)
        qf[pl.ds(8 * Z + z, TX, stride=Z), :] = turn(main, z)
        qf[pl.ds(z, 8, stride=Z), :] = sides[120:128]
        qf[pl.ds(136 * Z + z, 8, stride=Z), :] = sides[0:8]
    for m in range(STEM_X + 1):
        qb[m] = qf[(2 * m + 3) * Z : (2 * m + 4) * Z, :].astype(BF)

    loop(4, lambda n: n + n // 2 * 2, lambda pair: stem_rows(pair, ((0, STEM_X),)))
    loop(2, lambda n: n + 2, lambda pair: stem_rows(pair, STEM_SIDES))

    @pl.when(at_low_x)
    def _():
        zero_columns(stem, range(4))

    @pl.when(at_high_x)
    def _():
        zero_columns(stem, range(132, 136))

    for pair in (0, 1, 3):
        inner_rows([(pair, 0, INNER_X)])
    inner_rows([(4, 0, INNER_X)] + [(2, begin, end) for begin, end in INNER_SIDES])

    @pl.when(at_low_x)
    def _():
        zero_columns(inner, range(3))

    @pl.when(at_high_x)
    def _():
        zero_columns(inner, range(131, 134))

    def block_body(pair):
        sums = conv_rows(inner, [(pair, 0, BLOCK_X)], near3, far3)
        for qx in range(2):
            old = stem[pair + 1, qx, 1 : 1 + BLOCK_X].astype(F32)
            value = jnp.maximum(sums[qx] + old, 0.0).astype(BF).reshape(BLOCK_X * Z, 128)
            logits = jnp.dot(value, wh[...], preferred_element_type=F32)
            pred[pair, qx] = jnp.tanh(logits).astype(BF).reshape(BLOCK_X, Z, 256)

        @pl.when(at_low_x)
        def _():
            for parity in range(2):
                pred[pair, parity, 0] = jnp.zeros((Z, 256), BF)

        @pl.when(at_high_x)
        def _():
            for parity in range(2):
                pred[pair, parity, BLOCK_X - 1] = jnp.zeros((Z, 256), BF)

    lanes = lax.broadcasted_iota(jnp.int32, (1, Z, 128), 2)

    def blend_rows(pairs, first, more):
        def body(step, carry):
            j = step * XB
            for qx in range(2):
                operands = []
                for pair in pairs:
                    for half in range(2):
                        chosen = None
                        for n, a in enumerate((0, 1, 2) if half == 0 else (2, 3, 4)):
                            at = qx - a + 4
                            part = pred[pair, at % 2, pl.ds(j + at // 2, XB), :, half * 128 : half * 128 + 128]
                            chosen = part if n == 0 else jnp.where(lanes >= A_START[half][n], part, chosen)
                        operands.append(chosen.reshape(XB * Z, 128))
                added = jnp.dot(
                    jnp.concatenate(operands, axis=1),
                    blend[first : first + 256 * len(pairs), :],
                    preferred_element_type=F32,
                )
                added = added.reshape(XB, Z, 128)
                at = pl.ds(j, XB)
                total[at, qx] = total[at, qx] + added if more else added
            return carry

        lax.fori_loop(0, TX // 2 // XB, body, 0)

    def turned_total(z):
        return total.reshape(TX * Z, 128)[pl.ds(z, TX, stride=Z), :][:, :40].T

    def outer_body(step, carry):
        block_body(step * (BLOCK_PAIRS - 1))
        return carry

    lax.fori_loop(0, 2, outer_body, 0)
    blend_rows((0, BLOCK_PAIRS - 1), 0, False)
    for z in range(Z):
        both = turned_total(z)
        for side in range(2):
            edge_out[side, z] = both[24 + 8 * side : 32 + 8 * side]
    edges = []
    for side, dy in enumerate((-1, 1)):
        edges.append(
            pltpu.make_async_remote_copy(
                src_ref=edge_out.at[side],
                dst_ref=edge_in.at[side],
                send_sem=edge_send_sem.at[side],
                recv_sem=edge_recv_sem.at[side],
                device_id=device(dy, 0),
                device_id_type=MESH,
            )
        )
        pl.when(inside(dy, 0))(edges[-1].start)

    def middle_body(step, carry):
        block_body(step + 1)
        return carry

    lax.fori_loop(0, BLOCK_PAIRS - 2, middle_body, 0)
    blend_rows(tuple(range(1, BLOCK_PAIRS - 1)), 512, True)

    y8 = lax.broadcasted_iota(jnp.int32, (TY, TX), 0)
    scale = 0.5 / (coverage_of(gy * TY + y8, ny * TY) * coverage_of(gx * TX + lane8, nx * TX))
    from_above = (y8 < 2) & (gy > 0)
    from_below = (y8 >= TY - 2) & (gy < ny - 1)
    for copy, dy in zip(edges, (-1, 1)):
        pl.when(inside(dy, 0))(copy.wait_send)
        pl.when(inside(-dy, 0))(copy.wait_recv)
    for z in range(Z):
        both = turned_total(z)
        below, above = edge_in[0, z], edge_in[1, z]
        for c in range(3):
            added = both[c * TY : c * TY + TY, :]
            added += jnp.where(from_above, above if c == 0 else pltpu.roll(above, TY - 2 * c, axis=0), 0.0)
            added += jnp.where(from_below, pltpu.roll(below, TY - 2 - 2 * c, axis=0), 0.0)
            out_ref[c, z] = 0.5 + added * scale


def lane_plan():
    plan, starts = [], []
    for half in range(2):
        lanes, begin = [], []
        for a in (0, 1, 2) if half == 0 else (2, 3, 4):
            begin.append(len(lanes))
            for py in range(2):
                if a == 2 and py != half:
                    continue
                lanes += [(a, py, b, c) for b in range(5) for c in range(3)]
        plan.append(lanes)
        starts.append(begin)
    return plan, starts


LANES, A_START = lane_plan()


def constants():
    place = np.zeros((STEM_PAIRS, 4, 64, 128), np.float32)
    for pair in range(STEM_PAIRS):
        for qx in range(2):
            for qy in range(2):
                for dz in range(3):
                    for dy in range(3):
                        for dx in range(3):
                            y = (2 * pair + qy + dy - 3) % 16
                            place[pair, qx + dx, dz * 16 + y, (qx * 2 + qy) * 32 + (dz * 3 + dy) * 3 + dx] = 1
    columns = np.zeros((2, 75, 256), np.float32)
    pairs = (0, BLOCK_PAIRS - 1) + tuple(range(1, BLOCK_PAIRS - 1))
    blend = np.zeros((len(pairs), 256, 128), np.float32)
    for half in range(2):
        for n, (a, py, b, c) in enumerate(LANES[half]):
            columns[py, (a * 5 + b) * 3 + c, half * 128 + n] = 0.5
            for i, pair in enumerate(pairs):
                y = 2 * pair + py + b - R
                if y < 0:
                    lane = 24 + 2 * c + y + R
                elif y >= TY:
                    lane = 32 + 2 * c + y - TY
                else:
                    lane = c * TY + y
                blend[i, half * 128 + n, lane] = (R + 1 - abs(a - R)) * (R + 1 - abs(b - R))
    return (
        jnp.asarray(place.reshape(STEM_PAIRS, 256, 128), BF),
        jnp.asarray(columns, BF),
        jnp.asarray(blend.reshape(-1, 128), BF),
    )


def local(intensity, first_kernel, second_kernel, third_kernel, head_weight):
    place, columns, blend = constants()
    vmem = pl.BlockSpec(memory_space=pltpu.VMEM)
    hbm = pl.BlockSpec(memory_space=pltpu.HBM)
    return pl.pallas_call(
        compute_kernel,
        out_shape=pltpu.VMEM((3, Z, TY, TX), F32),
        in_specs=[hbm] * 8,
        out_specs=vmem,
        scratch_shapes=[
            pltpu.VMEM(intensity.shape, BF),
            pltpu.VMEM(place.shape, BF),
            pltpu.VMEM((9, 3, C), BF),
            pltpu.VMEM((27, C, C), BF),
            pltpu.VMEM((27, C, C), BF),
            pltpu.VMEM(head_weight.shape, BF),
            pltpu.VMEM(columns.shape, BF),
            pltpu.VMEM(blend.shape, BF),
            pltpu.VMEM((2, 16, Z * TY), BF),
            pltpu.VMEM((2, Z, TY, TX), BF),
            pltpu.VMEM((3, 2, 16, Z * TY), BF),
            pltpu.VMEM((2, Z, TY, TX), F32),
            pltpu.VMEM((2, Z, TY, TX), F32),
            pltpu.VMEM((32, C), F32),
            pltpu.VMEM((STEM_PAIRS, 256, 256), BF),
            pltpu.VMEM((768, 256), BF),
            pltpu.VMEM((1024, 256), BF),
            pltpu.VMEM((768, 256), BF),
            pltpu.VMEM((1024, 256), BF),
            pltpu.VMEM((128, 256), BF),
            pltpu.VMEM((2, Z + 2, 2 * TY, TX), F32),
            pltpu.VMEM((2, Z + 2, 2 * TY, TX), F32),
            pltpu.VMEM((144 * Z, 128), F32),
            pltpu.VMEM((STEM_X + 1, Z, 128), BF),
            pltpu.VMEM((STEM_PAIRS, 2, STEM_X, Z, 128), BF),
            pltpu.VMEM((INNER_PAIRS, 2, INNER_X, Z, 128), BF),
            pltpu.VMEM((BLOCK_PAIRS, 2, BLOCK_X, Z, 256), BF),
            pltpu.VMEM((TX // 2, 2, Z, 128), F32),
            pltpu.SemaphoreType.DMA((8,)),
            pltpu.SemaphoreType.DMA((8,)),
            pltpu.SemaphoreType.DMA((8,)),
            pltpu.SemaphoreType.DMA((2,)),
            pltpu.SemaphoreType.DMA((2,)),
        ],
        compiler_params=pltpu.CompilerParams(
            collective_id=0, has_side_effects=True, vmem_limit_bytes=56 * 2**20
        ),
        name="convnet",
    )(
        intensity, place, first_kernel.reshape(9, 3, C),
        second_kernel.reshape(27, C, C), third_kernel.reshape(27, C, C), head_weight, columns, blend,
    )


def solution(mesh):
    in_specs = (P(None, "gy", "gx"), P(), P(), P(), P())
    out_specs = P(None, None, "gy", "gx")
    return jax.shard_map(local, mesh=mesh, in_specs=in_specs, out_specs=out_specs, check_vma=False)
```

```python
import functools

import jax
import jax.numpy as jnp
import numpy as np
from jax import lax
from jax.experimental import pallas as pl
from jax.experimental.pallas import tpu as pltpu
from jax.sharding import PartitionSpec as P

R = 2
C = 64
Z = 16
TY = 8
TX = 128
BF = jnp.bfloat16
F32 = jnp.float32
MESH = pl.DeviceIdType.MESH


STEM_PAIRS = 6
INNER_PAIRS = 5
BLOCK_PAIRS = 4
STEM_X = 68
INNER_X = 67
BLOCK_X = 66
XB = 64
STEM_OWN, STEM_SIDES = ((3, 65),), ((0, 3), (65, STEM_X))
INNER_OWN, INNER_SIDES = ((3, 64),), ((0, 3), (64, INNER_X))
AROUND = [(dy, dx) for dy in (-1, 0, 1) for dx in (-1, 0, 1) if (dy, dx) != (0, 0)]


def join(parts):
    return parts[0] if len(parts) == 1 else jnp.concatenate(parts, axis=0)


def conv_rows(ref, spans, near, far):
    count = sum(end - begin for _, begin, end in spans)

    def operand(offsets):
        parts = []
        for offset in offsets:
            for k in range(2):
                at = offset // 2
                part = join([ref[pair + k, offset % 2, begin + at : end + at] for pair, begin, end in spans])
                parts.append(part.reshape(count * Z, 2 * C))
        return jnp.concatenate(parts, axis=1)

    row = lax.broadcasted_iota(jnp.int32, (1, Z, 2 * C), 1)
    third = jnp.dot(operand(range(4)), far[...], preferred_element_type=F32)
    out = []
    for qx in range(2):
        both = jnp.dot(operand(range(qx, qx + 3)), near[...], preferred_element_type=F32)
        below = both[:, :128].reshape(count, Z, 128)
        above = third[:, qx * 128 : qx * 128 + 128].reshape(count, Z, 128)
        total = both[:, 128:].reshape(count, Z, 128)
        total += jnp.where(row == 0, 0.0, pltpu.roll(below, 1, axis=1))
        total += jnp.where(row == Z - 1, 0.0, pltpu.roll(above, Z - 1, axis=1))
        out.append(total)
    return out


def build_conv_weights(kernel_ref, near, far):
    zero = jnp.zeros((C, C), BF)

    def band(dz, dx, source):
        blocks = []
        for qy in range(2):
            dy = source - qy
            inside = 0 <= dx < 3 and 0 <= dy < 3
            blocks.append(kernel_ref[(dz * 3 + dy) * 3 + dx] if inside else zero)
        return jnp.concatenate(blocks, axis=1)

    for source in range(4):
        for dx in range(3):
            rows = (dx * 4 + source) * C
            for dz in range(2):
                near[rows : rows + C, dz * 128 : dz * 128 + 128] = band(dz, dx, source)
        for offset in range(4):
            rows = (offset * 4 + source) * C
            for qx in range(2):
                far[rows : rows + C, qx * 128 : qx * 128 + 128] = band(2, offset - qx, source)


def zero_columns(ref, columns):
    for pair in range(ref.shape[0]):
        for x in columns:
            ref[pair, x % 2, x // 2] = jnp.zeros((Z, 2 * C), BF)


def coverage_of(position, length):
    total = jnp.zeros(position.shape, F32)
    for b in range(2 * R + 1):
        source = position - (b - R)
        total += jnp.where((source >= 0) & (source < length), float(R + 1 - abs(b - R)), 0.0)
    return total


def compute_kernel(
    tile_hbm, place_hbm, first_hbm, second_hbm, third_hbm, head_hbm, columns_hbm, blend_hbm,
    out_ref,
    tile_ref, place, first_ref, second, third, head_ref, columns_ref, blend,
    strips, rows_in, sides_in, edge_out, edge_in,
    taps, w1, near2, far2, near3, far3, wh, main, edge, qf, qb, stem, inner, pred, total,
    load_sem, send_sem, recv_sem, edge_send_sem, edge_recv_sem,
):
    gx, gy = lax.axis_index("gx"), lax.axis_index("gy")
    nx, ny = lax.axis_size("gx"), lax.axis_size("gy")
    at_low_x, at_high_x = gx == 0, gx == nx - 1
    at_low_y, at_high_y = gy == 0, gy == ny - 1

    def device(dy, dx):
        return (lax.rem(gx + dx + nx, nx), lax.rem(gy + dy + ny, ny))

    def inside(dy, dx):
        found = None
        for step, low, high in ((dy, at_low_y, at_high_y), (dx, at_low_x, at_high_x)):
            if step:
                here = jnp.logical_not(low if step < 0 else high)
                found = here if found is None else found & here
        return found

    barrier = pltpu.get_barrier_semaphore()
    for dy, dx in AROUND:

        @pl.when(inside(dy, dx))
        def _():
            pl.semaphore_signal(barrier, inc=1, device_id=device(dy, dx), device_id_type=MESH)

    loads = []
    for n, (source, target) in enumerate(
        (
            (tile_hbm, tile_ref), (second_hbm, second), (third_hbm, third), (first_hbm, first_ref),
            (place_hbm, place), (head_hbm, head_ref), (columns_hbm, columns_ref), (blend_hbm, blend),
        )
    ):
        loads.append(pltpu.make_async_copy(source, target, load_sem.at[n]))
        loads[-1].start()

    loads[0].wait()
    turned = tile_ref[...].astype(F32).reshape(Z * TY, TX).T
    strips[0] = turned[0:16].astype(BF)
    strips[1] = turned[TX - 16 : TX].astype(BF)
    for load in loads[1:]:
        load.wait()
    build_conv_weights(second, near2, far2)
    build_conv_weights(third, near3, far3)
    taps[...] = jnp.zeros((32, C), F32)
    for n in range(9):
        taps[3 * n : 3 * n + 3, :] = first_ref[n].astype(F32)
    tap = taps[...].astype(BF)
    nothing = jnp.zeros((32, C), BF)
    spread = jnp.concatenate(
        [jnp.concatenate([tap if i == q else nothing for i in range(4)], axis=1) for q in range(4)], axis=0
    )
    for pair in range(STEM_PAIRS):
        taken = jnp.dot(place[pair], spread, preferred_element_type=F32)
        if pair in (0, STEM_PAIRS - 1):
            taken = taken * jnp.where(at_low_y if pair == 0 else at_high_y, 0.0, 1.0)
        w1[pair] = taken.astype(BF)
    for py in range(2):
        wh[py * C : py * C + C, :] = jnp.dot(
            head_ref[...], columns_ref[py], preferred_element_type=F32
        ).astype(BF)

    beside_y = 2 - at_low_y.astype(jnp.int32) - at_high_y.astype(jnp.int32)
    beside_x = 2 - at_low_x.astype(jnp.int32) - at_high_x.astype(jnp.int32)
    pl.semaphore_wait(barrier, (beside_y + 1) * (beside_x + 1) - 1)
    copies = []
    for n, (dy, dx) in enumerate(AROUND):
        if dx == 0:
            source, target = tile_ref, rows_in.at[0 if dy == 1 else 1]
        else:
            source, target = strips.at[0 if dx == -1 else 1], sides_in.at[1 - dy, 0 if dx == 1 else 1]
        copies.append(
            pltpu.make_async_remote_copy(
                src_ref=source,
                dst_ref=target,
                send_sem=send_sem.at[n],
                recv_sem=recv_sem.at[n],
                device_id=device(dy, dx),
                device_id_type=MESH,
            )
        )
        pl.when(inside(dy, dx))(copies[-1].start)

    lane8 = lax.broadcasted_iota(jnp.int32, (TY, TX), 1)
    lane128 = lax.broadcasted_iota(jnp.int32, (Z * TY, TX), 1)
    end = lax.broadcasted_iota(jnp.int32, (1, TY, TX), 2) == TX - 1
    for buffer in (main, edge):
        for half in range(2):
            buffer[half, 0] = jnp.zeros((2 * TY, TX), F32)
            buffer[half, Z + 1] = jnp.zeros((2 * TY, TX), F32)
    filler = jnp.zeros((2 * TY, TX), F32)

    def turn(buffer, z):
        parts = []
        for half in range(2):
            parts += [buffer[half, z], buffer[half, z + 1], buffer[half, z + 2], filler]
        return jnp.concatenate(parts, axis=0).T

    own = tile_ref[...].astype(F32)
    main[0, 1 : Z + 1, 0:TY, :] = own
    main[1, 1 : Z + 1, 0:TY, :] = jnp.where(end, 0.0, pltpu.roll(own, TX - 1, axis=2))
    for half in range(2):
        main[half, 1 : Z + 1, TY : 2 * TY, :] = jnp.zeros((Z, TY, TX), F32)
    for z in range(Z):
        qf[pl.ds(8 * Z + z, TX, stride=Z), :] = turn(main, z)
    for m in range(3, STEM_X - 2):
        qb[m] = qf[(2 * m + 3) * Z : (2 * m + 4) * Z, :].astype(BF)

    def stem_rows(pair, spans):
        parts = []
        for k in range(2):
            part = join([qb[begin + k : end + k] for begin, end in spans])
            parts.append(part.reshape(-1, 128))
        acc = jnp.dot(jnp.concatenate(parts, axis=1), w1[pair], preferred_element_type=F32)
        acc = jnp.maximum(acc, 0.0)
        for qx in range(2):
            value = acc[:, qx * 128 : qx * 128 + 128].astype(BF).reshape(-1, Z, 128)
            at = 0
            for begin, end in spans:
                stem[pair, qx, begin:end] = value[at : at + end - begin]
                at += end - begin

    upper = lax.broadcasted_iota(jnp.int32, (1, 1, 128), 2) // C

    def inner_rows(spans):
        sums = conv_rows(stem, spans, near2, far2)
        for qx in range(2):
            value = jnp.maximum(sums[qx], 0.0)
            at = 0
            for pair, begin, end in spans:
                part = value[at : at + end - begin]
                if pair == 0:
                    part = part * jnp.where(upper == jnp.where(at_low_y, 0, -1), 0.0, 1.0)
                if pair == INNER_PAIRS - 1:
                    part = part * jnp.where(upper == jnp.where(at_high_y, 1, -1), 0.0, 1.0)
                inner[pair, qx, begin:end] = part.astype(BF)
                at += end - begin

    def loop(count, pair_of, body):
        for n in range(count):
            body(pair_of(n))

    loop(2, lambda n: n + 2, lambda pair: stem_rows(pair, STEM_OWN))
    inner_rows([(2, begin, end) for begin, end in INNER_OWN])

    for copy, (dy, dx) in zip(copies, AROUND):
        pl.when(inside(dy, dx))(copy.wait_send)
        pl.when(inside(-dy, -dx))(copy.wait_recv)

    right_ok = jnp.where(at_high_x, 0, 64)
    left_ok = jnp.where(at_low_x, 128, 64)
    between = jnp.zeros((TX - 32, Z * TY), F32)
    middles, sideways = [], []
    for ty in range(3):
        left, right = sides_in[ty, 0].astype(F32), sides_in[ty, 1].astype(F32)
        sides = jnp.concatenate([right, between, left], axis=0).T
        sides = jnp.where((lane128 < right_ok) | (lane128 >= left_ok), sides, 0.0)
        sides = sides.reshape(Z, TY, TX)
        middle = own if ty == 1 else rows_in[ty // 2].astype(F32)
        if ty != 1:
            outside = at_low_y if ty == 0 else at_high_y
            middle, sides = jnp.where(outside, 0.0, middle), jnp.where(outside, 0.0, sides)
        middles.append(middle)
        sideways.append(sides)
    row8 = lax.broadcasted_iota(jnp.int32, (1, TY, TX), 1)
    for part in range(2):
        if part == 0:
            middle, sides = middles[1], sideways[1]
        else:
            middle = jnp.where(row8 < 4, middles[2], middles[0])
            sides = jnp.where(row8 < 4, sideways[2], sideways[0])
        next_middle, next_sides = pltpu.roll(middle, TX - 1, axis=2), pltpu.roll(sides, TX - 1, axis=2)
        rows = slice(part * TY, part * TY + TY)
        main[0, 1 : Z + 1, rows, :] = middle
        main[1, 1 : Z + 1, rows, :] = jnp.where(end, next_sides, next_middle)
        edge[0, 1 : Z + 1, rows, :] = sides
        edge[1, 1 : Z + 1, rows, :] = jnp.where(end, next_middle, next_sides)
    for z in range(Z):
        sides = turn(edge, z)
        qf[pl.ds(8 * Z + z, TX, stride=Z), :] = turn(main, z)
        qf[pl.ds(z, 8, stride=Z), :] = sides[120:128]
        qf[pl.ds(136 * Z + z, 8, stride=Z), :] = sides[0:8]
    for m in range(STEM_X + 1):
        qb[m] = qf[(2 * m + 3) * Z : (2 * m + 4) * Z, :].astype(BF)

    loop(4, lambda n: n + n // 2 * 2, lambda pair: stem_rows(pair, ((0, STEM_X),)))
    loop(2, lambda n: n + 2, lambda pair: stem_rows(pair, STEM_SIDES))

    @pl.when(at_low_x)
    def _():
        zero_columns(stem, range(4))

    @pl.when(at_high_x)
    def _():
        zero_columns(stem, range(132, 136))

    for pair in (0, 1, 3):
        inner_rows([(pair, 0, INNER_X)])
    inner_rows([(4, 0, INNER_X)] + [(2, begin, end) for begin, end in INNER_SIDES])

    @pl.when(at_low_x)
    def _():
        zero_columns(inner, range(3))

    @pl.when(at_high_x)
    def _():
        zero_columns(inner, range(131, 134))

    def block_body(pair):
        sums = conv_rows(inner, [(pair, 0, BLOCK_X)], near3, far3)
        for qx in range(2):
            old = stem[pair + 1, qx, 1 : 1 + BLOCK_X].astype(F32)
            value = jnp.maximum(sums[qx] + old, 0.0).astype(BF).reshape(BLOCK_X * Z, 128)
            logits = jnp.dot(value, wh[...], preferred_element_type=F32)
            pred[pair, qx] = jnp.tanh(logits).astype(BF).reshape(BLOCK_X, Z, 256)

        @pl.when(at_low_x)
        def _():
            for parity in range(2):
                pred[pair, parity, 0] = jnp.zeros((Z, 256), BF)

        @pl.when(at_high_x)
        def _():
            for parity in range(2):
                pred[pair, parity, BLOCK_X - 1] = jnp.zeros((Z, 256), BF)

    lanes = lax.broadcasted_iota(jnp.int32, (1, Z, 128), 2)

    def blend_rows(pairs, first, more):
        def body(step, carry):
            j = step * XB
            for qx in range(2):
                operands = []
                for pair in pairs:
                    for half in range(2):
                        chosen = None
                        for n, a in enumerate((0, 1, 2) if half == 0 else (2, 3, 4)):
                            at = qx - a + 4
                            part = pred[pair, at % 2, pl.ds(j + at // 2, XB), :, half * 128 : half * 128 + 128]
                            chosen = part if n == 0 else jnp.where(lanes >= A_START[half][n], part, chosen)
                        operands.append(chosen.reshape(XB * Z, 128))
                added = jnp.dot(
                    jnp.concatenate(operands, axis=1),
                    blend[first : first + 256 * len(pairs), :],
                    preferred_element_type=F32,
                )
                added = added.reshape(XB, Z, 128)
                at = pl.ds(j, XB)
                total[at, qx] = total[at, qx] + added if more else added
            return carry

        lax.fori_loop(0, TX // 2 // XB, body, 0)

    def turned_total(z):
        return total.reshape(TX * Z, 128)[pl.ds(z, TX, stride=Z), :][:, :40].T

    def outer_body(step, carry):
        block_body(step * (BLOCK_PAIRS - 1))
        return carry

    lax.fori_loop(0, 2, outer_body, 0)
    blend_rows((0, BLOCK_PAIRS - 1), 0, False)
    for z in range(Z):
        both = turned_total(z)
        for side in range(2):
            edge_out[side, z] = both[24 + 8 * side : 32 + 8 * side]
    edges = []
    for side, dy in enumerate((-1, 1)):
        edges.append(
            pltpu.make_async_remote_copy(
                src_ref=edge_out.at[side],
                dst_ref=edge_in.at[side],
                send_sem=edge_send_sem.at[side],
                recv_sem=edge_recv_sem.at[side],
                device_id=device(dy, 0),
                device_id_type=MESH,
            )
        )
        pl.when(inside(dy, 0))(edges[-1].start)

    def middle_body(step, carry):
        block_body(step + 1)
        return carry

    lax.fori_loop(0, BLOCK_PAIRS - 2, middle_body, 0)
    blend_rows(tuple(range(1, BLOCK_PAIRS - 1)), 512, True)

    y8 = lax.broadcasted_iota(jnp.int32, (TY, TX), 0)
    scale = 0.5 / (coverage_of(gy * TY + y8, ny * TY) * coverage_of(gx * TX + lane8, nx * TX))
    from_above = (y8 < 2) & (gy > 0)
    from_below = (y8 >= TY - 2) & (gy < ny - 1)
    for copy, dy in zip(edges, (-1, 1)):
        pl.when(inside(dy, 0))(copy.wait_send)
        pl.when(inside(-dy, 0))(copy.wait_recv)
    for z in range(Z):
        both = turned_total(z)
        below, above = edge_in[0, z], edge_in[1, z]
        for c in range(3):
            added = both[c * TY : c * TY + TY, :]
            added += jnp.where(from_above, above if c == 0 else pltpu.roll(above, TY - 2 * c, axis=0), 0.0)
            added += jnp.where(from_below, pltpu.roll(below, TY - 2 - 2 * c, axis=0), 0.0)
            out_ref[c, z] = 0.5 + added * scale


def lane_plan():
    plan, starts = [], []
    for half in range(2):
        lanes, begin = [], []
        for a in (0, 1, 2) if half == 0 else (2, 3, 4):
            begin.append(len(lanes))
            for py in range(2):
                if a == 2 and py != half:
                    continue
                lanes += [(a, py, b, c) for b in range(5) for c in range(3)]
        plan.append(lanes)
        starts.append(begin)
    return plan, starts


LANES, A_START = lane_plan()


def constants():
    place = np.zeros((STEM_PAIRS, 4, 64, 128), np.float32)
    for pair in range(STEM_PAIRS):
        for qx in range(2):
            for qy in range(2):
                for dz in range(3):
                    for dy in range(3):
                        for dx in range(3):
                            y = (2 * pair + qy + dy - 3) % 16
                            place[pair, qx + dx, dz * 16 + y, (qx * 2 + qy) * 32 + (dz * 3 + dy) * 3 + dx] = 1
    columns = np.zeros((2, 75, 256), np.float32)
    pairs = (0, BLOCK_PAIRS - 1) + tuple(range(1, BLOCK_PAIRS - 1))
    blend = np.zeros((len(pairs), 256, 128), np.float32)
    for half in range(2):
        for n, (a, py, b, c) in enumerate(LANES[half]):
            columns[py, (a * 5 + b) * 3 + c, half * 128 + n] = 0.5
            for i, pair in enumerate(pairs):
                y = 2 * pair + py + b - R
                if y < 0:
                    lane = 24 + 2 * c + y + R
                elif y >= TY:
                    lane = 32 + 2 * c + y - TY
                else:
                    lane = c * TY + y
                blend[i, half * 128 + n, lane] = (R + 1 - abs(a - R)) * (R + 1 - abs(b - R))
    return (
        jnp.asarray(place.reshape(STEM_PAIRS, 256, 128), BF),
        jnp.asarray(columns, BF),
        jnp.asarray(blend.reshape(-1, 128), BF),
    )


def local(intensity, first_kernel, second_kernel, third_kernel, head_weight):
    place, columns, blend = constants()
    vmem = pl.BlockSpec(memory_space=pltpu.VMEM)
    hbm = pl.BlockSpec(memory_space=pltpu.HBM)
    return pl.pallas_call(
        compute_kernel,
        out_shape=pltpu.VMEM((3, Z, TY, TX), F32),
        in_specs=[hbm] * 8,
        out_specs=vmem,
        scratch_shapes=[
            pltpu.VMEM(intensity.shape, BF),
            pltpu.VMEM(place.shape, BF),
            pltpu.VMEM((9, 3, C), BF),
            pltpu.VMEM((27, C, C), BF),
            pltpu.VMEM((27, C, C), BF),
            pltpu.VMEM(head_weight.shape, BF),
            pltpu.VMEM(columns.shape, BF),
            pltpu.VMEM(blend.shape, BF),
            pltpu.VMEM((2, 16, Z * TY), BF),
            pltpu.VMEM((2, Z, TY, TX), BF),
            pltpu.VMEM((3, 2, 16, Z * TY), BF),
            pltpu.VMEM((2, Z, TY, TX), F32),
            pltpu.VMEM((2, Z, TY, TX), F32),
            pltpu.VMEM((32, C), F32),
            pltpu.VMEM((STEM_PAIRS, 256, 256), BF),
            pltpu.VMEM((768, 256), BF),
            pltpu.VMEM((1024, 256), BF),
            pltpu.VMEM((768, 256), BF),
            pltpu.VMEM((1024, 256), BF),
            pltpu.VMEM((128, 256), BF),
            pltpu.VMEM((2, Z + 2, 2 * TY, TX), F32),
            pltpu.VMEM((2, Z + 2, 2 * TY, TX), F32),
            pltpu.VMEM((144 * Z, 128), F32),
            pltpu.VMEM((STEM_X + 1, Z, 128), BF),
            pltpu.VMEM((STEM_PAIRS, 2, STEM_X, Z, 128), BF),
            pltpu.VMEM((INNER_PAIRS, 2, INNER_X, Z, 128), BF),
            pltpu.VMEM((BLOCK_PAIRS, 2, BLOCK_X, Z, 256), BF),
            pltpu.VMEM((TX // 2, 2, Z, 128), F32),
            pltpu.SemaphoreType.DMA((8,)),
            pltpu.SemaphoreType.DMA((8,)),
            pltpu.SemaphoreType.DMA((8,)),
            pltpu.SemaphoreType.DMA((2,)),
            pltpu.SemaphoreType.DMA((2,)),
        ],
        compiler_params=pltpu.CompilerParams(
            collective_id=0, has_side_effects=True, vmem_limit_bytes=56 * 2**20
        ),
        name="convnet",
    )(
        intensity, place, first_kernel.reshape(9, 3, C),
        second_kernel.reshape(27, C, C), third_kernel.reshape(27, C, C), head_weight, columns, blend,
    )


def solution(mesh):
    in_specs = (P(None, "gy", "gx"), P(), P(), P(), P())
    out_specs = P(None, None, "gy", "gx")
    return jax.shard_map(local, mesh=mesh, in_specs=in_specs, out_specs=out_specs, check_vma=False)
```

```python
import functools

import jax
import jax.numpy as jnp
import numpy as np
from jax import lax
from jax.experimental import pallas as pl
from jax.experimental.pallas import tpu as pltpu
from jax.sharding import PartitionSpec as P

R = 2
C = 64
Z = 16
TY = 8
TX = 128
BF = jnp.bfloat16
F32 = jnp.float32
MESH = pl.DeviceIdType.MESH


STEM_PAIRS = 6
INNER_PAIRS = 5
BLOCK_PAIRS = 4
STEM_X = 68
INNER_X = 67
BLOCK_X = 66
XB = 64
STEM_OWN, STEM_SIDES = ((3, 65),), ((0, 3), (65, STEM_X))
INNER_OWN, INNER_SIDES = ((3, 64),), ((0, 3), (64, INNER_X))
AROUND = [(dy, dx) for dy in (-1, 0, 1) for dx in (-1, 0, 1) if (dy, dx) != (0, 0)]


def join(parts):
    return parts[0] if len(parts) == 1 else jnp.concatenate(parts, axis=0)


def conv_rows(ref, spans, near, far):
    count = sum(end - begin for _, begin, end in spans)

    def operand(offsets):
        parts = []
        for offset in offsets:
            for k in range(2):
                at = offset // 2
                part = join([ref[pair + k, offset % 2, begin + at : end + at] for pair, begin, end in spans])
                parts.append(part.reshape(count * Z, 2 * C))
        return jnp.concatenate(parts, axis=1)

    row = lax.broadcasted_iota(jnp.int32, (1, Z, 2 * C), 1)
    third = jnp.dot(operand(range(4)), far[...], preferred_element_type=F32)
    out = []
    for qx in range(2):
        both = jnp.dot(operand(range(qx, qx + 3)), near[...], preferred_element_type=F32)
        below = both[:, :128].reshape(count, Z, 128)
        above = third[:, qx * 128 : qx * 128 + 128].reshape(count, Z, 128)
        total = both[:, 128:].reshape(count, Z, 128)
        total += jnp.where(row == 0, 0.0, pltpu.roll(below, 1, axis=1))
        total += jnp.where(row == Z - 1, 0.0, pltpu.roll(above, Z - 1, axis=1))
        out.append(total)
    return out


def build_conv_weights(kernel_ref, near, far):
    zero = jnp.zeros((C, C), BF)

    def band(dz, dx, source):
        blocks = []
        for qy in range(2):
            dy = source - qy
            inside = 0 <= dx < 3 and 0 <= dy < 3
            blocks.append(kernel_ref[(dz * 3 + dy) * 3 + dx] if inside else zero)
        return jnp.concatenate(blocks, axis=1)

    for source in range(4):
        for dx in range(3):
            rows = (dx * 4 + source) * C
            for dz in range(2):
                near[rows : rows + C, dz * 128 : dz * 128 + 128] = band(dz, dx, source)
        for offset in range(4):
            rows = (offset * 4 + source) * C
            for qx in range(2):
                far[rows : rows + C, qx * 128 : qx * 128 + 128] = band(2, offset - qx, source)


def zero_columns(ref, columns):
    for pair in range(ref.shape[0]):
        for x in columns:
            ref[pair, x % 2, x // 2] = jnp.zeros((Z, 2 * C), BF)


def coverage_of(position, length):
    total = jnp.zeros(position.shape, F32)
    for b in range(2 * R + 1):
        source = position - (b - R)
        total += jnp.where((source >= 0) & (source < length), float(R + 1 - abs(b - R)), 0.0)
    return total


def compute_kernel(
    tile_hbm, place_hbm, first_hbm, second_hbm, third_hbm, head_hbm, columns_hbm, blend_hbm,
    out_ref,
    tile_ref, place, first_ref, second, third, head_ref, columns_ref, blend,
    strips, rows_in, sides_in, edge_out, edge_in,
    taps, w1, near2, far2, near3, far3, wh, main, edge, qf, qb, stem, inner, pred, total,
    load_sem, send_sem, recv_sem, edge_send_sem, edge_recv_sem,
):
    gx, gy = lax.axis_index("gx"), lax.axis_index("gy")
    nx, ny = lax.axis_size("gx"), lax.axis_size("gy")
    at_low_x, at_high_x = gx == 0, gx == nx - 1
    at_low_y, at_high_y = gy == 0, gy == ny - 1

    def device(dy, dx):
        return (lax.rem(gx + dx + nx, nx), lax.rem(gy + dy + ny, ny))

    def inside(dy, dx):
        found = None
        for step, low, high in ((dy, at_low_y, at_high_y), (dx, at_low_x, at_high_x)):
            if step:
                here = jnp.logical_not(low if step < 0 else high)
                found = here if found is None else found & here
        return found

    barrier = pltpu.get_barrier_semaphore()
    for dy, dx in AROUND:

        @pl.when(inside(dy, dx))
        def _():
            pl.semaphore_signal(barrier, inc=1, device_id=device(dy, dx), device_id_type=MESH)

    loads = []
    for n, (source, target) in enumerate(
        (
            (tile_hbm, tile_ref), (second_hbm, second), (third_hbm, third), (first_hbm, first_ref),
            (place_hbm, place), (head_hbm, head_ref), (columns_hbm, columns_ref), (blend_hbm, blend),
        )
    ):
        loads.append(pltpu.make_async_copy(source, target, load_sem.at[n]))
        loads[-1].start()

    loads[0].wait()
    turned = tile_ref[...].astype(F32).reshape(Z * TY, TX).T
    strips[0] = turned[0:16].astype(BF)
    strips[1] = turned[TX - 16 : TX].astype(BF)
    for load in loads[1:]:
        load.wait()
    build_conv_weights(second, near2, far2)
    build_conv_weights(third, near3, far3)
    taps[...] = jnp.zeros((32, C), F32)
    for n in range(9):
        taps[3 * n : 3 * n + 3, :] = first_ref[n].astype(F32)
    tap = taps[...].astype(BF)
    nothing = jnp.zeros((32, C), BF)
    spread = jnp.concatenate(
        [jnp.concatenate([tap if i == q else nothing for i in range(4)], axis=1) for q in range(4)], axis=0
    )
    for pair in range(STEM_PAIRS):
        taken = jnp.dot(place[pair], spread, preferred_element_type=F32)
        if pair in (0, STEM_PAIRS - 1):
            taken = taken * jnp.where(at_low_y if pair == 0 else at_high_y, 0.0, 1.0)
        w1[pair] = taken.astype(BF)
    for py in range(2):
        wh[py * C : py * C + C, :] = jnp.dot(
            head_ref[...], columns_ref[py], preferred_element_type=F32
        ).astype(BF)

    beside_y = 2 - at_low_y.astype(jnp.int32) - at_high_y.astype(jnp.int32)
    beside_x = 2 - at_low_x.astype(jnp.int32) - at_high_x.astype(jnp.int32)
    pl.semaphore_wait(barrier, (beside_y + 1) * (beside_x + 1) - 1)
    copies = []
    for n, (dy, dx) in enumerate(AROUND):
        if dx == 0:
            source, target = tile_ref, rows_in.at[0 if dy == 1 else 1]
        else:
            source, target = strips.at[0 if dx == -1 else 1], sides_in.at[1 - dy, 0 if dx == 1 else 1]
        copies.append(
            pltpu.make_async_remote_copy(
                src_ref=source,
                dst_ref=target,
                send_sem=send_sem.at[n],
                recv_sem=recv_sem.at[n],
                device_id=device(dy, dx),
                device_id_type=MESH,
            )
        )
        pl.when(inside(dy, dx))(copies[-1].start)

    lane8 = lax.broadcasted_iota(jnp.int32, (TY, TX), 1)
    lane128 = lax.broadcasted_iota(jnp.int32, (Z * TY, TX), 1)
    end = lax.broadcasted_iota(jnp.int32, (1, TY, TX), 2) == TX - 1
    for buffer in (main, edge):
        for half in range(2):
            buffer[half, 0] = jnp.zeros((2 * TY, TX), F32)
            buffer[half, Z + 1] = jnp.zeros((2 * TY, TX), F32)
    filler = jnp.zeros((2 * TY, TX), F32)

    def turn(buffer, z):
        parts = []
        for half in range(2):
            parts += [buffer[half, z], buffer[half, z + 1], buffer[half, z + 2], filler]
        whole = jnp.concatenate(parts, axis=0)
        return (whole if buffer is main else whole[:, :24]).T

    own = tile_ref[...].astype(F32)
    main[0, 1 : Z + 1, 0:TY, :] = own
    main[1, 1 : Z + 1, 0:TY, :] = jnp.where(end, 0.0, pltpu.roll(own, TX - 1, axis=2))
    for half in range(2):
        main[half, 1 : Z + 1, TY : 2 * TY, :] = jnp.zeros((Z, TY, TX), F32)
    for z in range(Z):
        qf[pl.ds(8 * Z + z, TX, stride=Z), :] = turn(main, z)
    for m in range(3, STEM_X - 2):
        qb[m] = qf[(2 * m + 3) * Z : (2 * m + 4) * Z, :].astype(BF)

    def stem_rows(pair, spans):
        parts = []
        for k in range(2):
            part = join([qb[begin + k : end + k] for begin, end in spans])
            parts.append(part.reshape(-1, 128))
        acc = jnp.dot(jnp.concatenate(parts, axis=1), w1[pair], preferred_element_type=F32)
        acc = jnp.maximum(acc, 0.0)
        for qx in range(2):
            value = acc[:, qx * 128 : qx * 128 + 128].astype(BF).reshape(-1, Z, 128)
            at = 0
            for begin, end in spans:
                stem[pair, qx, begin:end] = value[at : at + end - begin]
                at += end - begin

    upper = lax.broadcasted_iota(jnp.int32, (1, 1, 128), 2) // C

    def inner_rows(spans):
        sums = conv_rows(stem, spans, near2, far2)
        for qx in range(2):
            value = jnp.maximum(sums[qx], 0.0)
            at = 0
            for pair, begin, end in spans:
                part = value[at : at + end - begin]
                if pair == 0:
                    part = part * jnp.where(upper == jnp.where(at_low_y, 0, -1), 0.0, 1.0)
                if pair == INNER_PAIRS - 1:
                    part = part * jnp.where(upper == jnp.where(at_high_y, 1, -1), 0.0, 1.0)
                inner[pair, qx, begin:end] = part.astype(BF)
                at += end - begin

    def loop(count, pair_of, body):
        for n in range(count):
            body(pair_of(n))

    loop(2, lambda n: n + 2, lambda pair: stem_rows(pair, STEM_OWN))
    inner_rows([(2, begin, end) for begin, end in INNER_OWN])

    for copy, (dy, dx) in zip(copies, AROUND):
        pl.when(inside(dy, dx))(copy.wait_send)
        pl.when(inside(-dy, -dx))(copy.wait_recv)

    right_ok = jnp.where(at_high_x, 0, 64)
    left_ok = jnp.where(at_low_x, 128, 64)
    between = jnp.zeros((TX - 32, Z * TY), F32)
    middles, sideways = [], []
    for ty in range(3):
        left, right = sides_in[ty, 0].astype(F32), sides_in[ty, 1].astype(F32)
        sides = jnp.concatenate([right, between, left], axis=0).T
        sides = jnp.where((lane128 < right_ok) | (lane128 >= left_ok), sides, 0.0)
        sides = sides.reshape(Z, TY, TX)
        middle = own if ty == 1 else rows_in[ty // 2].astype(F32)
        if ty != 1:
            outside = at_low_y if ty == 0 else at_high_y
            middle, sides = jnp.where(outside, 0.0, middle), jnp.where(outside, 0.0, sides)
        middles.append(middle)
        sideways.append(sides)
    row8 = lax.broadcasted_iota(jnp.int32, (1, TY, TX), 1)
    for part in range(2):
        if part == 0:
            middle, sides = middles[1], sideways[1]
        else:
            middle = jnp.where(row8 < 4, middles[2], middles[0])
            sides = jnp.where(row8 < 4, sideways[2], sideways[0])
        next_middle, next_sides = pltpu.roll(middle, TX - 1, axis=2), pltpu.roll(sides, TX - 1, axis=2)
        rows = slice(part * TY, part * TY + TY)
        main[0, 1 : Z + 1, rows, :] = middle
        main[1, 1 : Z + 1, rows, :] = jnp.where(end, next_sides, next_middle)
        edge[0, 1 : Z + 1, rows, :] = pltpu.roll(sides, 16, axis=2)
        edge[1, 1 : Z + 1, rows, :] = pltpu.roll(jnp.where(end, next_middle, next_sides), 16, axis=2)
    for z in range(Z):
        sides = turn(edge, z)
        qf[pl.ds(8 * Z + z, TX, stride=Z), :] = turn(main, z)
        qf[pl.ds(z, 8, stride=Z), :] = sides[8:16]
        qf[pl.ds(136 * Z + z, 8, stride=Z), :] = sides[16:24]
    for m in range(STEM_X + 1):
        qb[m] = qf[(2 * m + 3) * Z : (2 * m + 4) * Z, :].astype(BF)

    loop(4, lambda n: n + n // 2 * 2, lambda pair: stem_rows(pair, ((0, STEM_X),)))
    loop(2, lambda n: n + 2, lambda pair: stem_rows(pair, STEM_SIDES))

    @pl.when(at_low_x)
    def _():
        zero_columns(stem, range(4))

    @pl.when(at_high_x)
    def _():
        zero_columns(stem, range(132, 136))

    for pair in (0, 1, 3):
        inner_rows([(pair, 0, INNER_X)])
    inner_rows([(4, 0, INNER_X)] + [(2, begin, end) for begin, end in INNER_SIDES])

    @pl.when(at_low_x)
    def _():
        zero_columns(inner, range(3))

    @pl.when(at_high_x)
    def _():
        zero_columns(inner, range(131, 134))

    def block_body(pair):
        sums = conv_rows(inner, [(pair, 0, BLOCK_X)], near3, far3)
        for qx in range(2):
            old = stem[pair + 1, qx, 1 : 1 + BLOCK_X].astype(F32)
            value = jnp.maximum(sums[qx] + old, 0.0).astype(BF).reshape(BLOCK_X * Z, 128)
            logits = jnp.dot(value, wh[...], preferred_element_type=F32)
            pred[pair, qx] = jnp.tanh(logits).astype(BF).reshape(BLOCK_X, Z, 256)

        @pl.when(at_low_x)
        def _():
            for parity in range(2):
                pred[pair, parity, 0] = jnp.zeros((Z, 256), BF)

        @pl.when(at_high_x)
        def _():
            for parity in range(2):
                pred[pair, parity, BLOCK_X - 1] = jnp.zeros((Z, 256), BF)

    lanes = lax.broadcasted_iota(jnp.int32, (1, Z, 128), 2)

    def blend_rows(pairs, first, more):
        def body(step, carry):
            j = step * XB
            for qx in range(2):
                operands = []
                for pair in pairs:
                    for half in range(2):
                        chosen = None
                        for n, a in enumerate((0, 1, 2) if half == 0 else (2, 3, 4)):
                            at = qx - a + 4
                            part = pred[pair, at % 2, pl.ds(j + at // 2, XB), :, half * 128 : half * 128 + 128]
                            chosen = part if n == 0 else jnp.where(lanes >= A_START[half][n], part, chosen)
                        operands.append(chosen.reshape(XB * Z, 128))
                added = jnp.dot(
                    jnp.concatenate(operands, axis=1),
                    blend[first : first + 256 * len(pairs), :],
                    preferred_element_type=F32,
                )
                added = added.reshape(XB, Z, 128)
                at = pl.ds(j, XB)
                total[at, qx] = total[at, qx] + added if more else added
            return carry

        lax.fori_loop(0, TX // 2 // XB, body, 0)

    def turned_total(z):
        return total.reshape(TX * Z, 128)[pl.ds(z, TX, stride=Z), :][:, :40].T

    def outer_body(step, carry):
        block_body(step * (BLOCK_PAIRS - 1))
        return carry

    lax.fori_loop(0, 2, outer_body, 0)
    blend_rows((0, BLOCK_PAIRS - 1), 0, False)
    for z in range(Z):
        both = turned_total(z)
        for side in range(2):
            edge_out[side, z] = both[24 + 8 * side : 32 + 8 * side]
    edges = []
    for side, dy in enumerate((-1, 1)):
        edges.append(
            pltpu.make_async_remote_copy(
                src_ref=edge_out.at[side],
                dst_ref=edge_in.at[side],
                send_sem=edge_send_sem.at[side],
                recv_sem=edge_recv_sem.at[side],
                device_id=device(dy, 0),
                device_id_type=MESH,
            )
        )
        pl.when(inside(dy, 0))(edges[-1].start)

    def middle_body(step, carry):
        block_body(step + 1)
        return carry

    lax.fori_loop(0, BLOCK_PAIRS - 2, middle_body, 0)
    blend_rows(tuple(range(1, BLOCK_PAIRS - 1)), 512, True)

    y8 = lax.broadcasted_iota(jnp.int32, (TY, TX), 0)
    scale = 0.5 / (coverage_of(gy * TY + y8, ny * TY) * coverage_of(gx * TX + lane8, nx * TX))
    from_above = (y8 < 2) & (gy > 0)
    from_below = (y8 >= TY - 2) & (gy < ny - 1)
    for copy, dy in zip(edges, (-1, 1)):
        pl.when(inside(dy, 0))(copy.wait_send)
        pl.when(inside(-dy, 0))(copy.wait_recv)
    for z in range(Z):
        both = turned_total(z)
        below, above = edge_in[0, z], edge_in[1, z]
        for c in range(3):
            added = both[c * TY : c * TY + TY, :]
            added += jnp.where(from_above, above if c == 0 else pltpu.roll(above, TY - 2 * c, axis=0), 0.0)
            added += jnp.where(from_below, pltpu.roll(below, TY - 2 - 2 * c, axis=0), 0.0)
            out_ref[c, z] = 0.5 + added * scale


def lane_plan():
    plan, starts = [], []
    for half in range(2):
        lanes, begin = [], []
        for a in (0, 1, 2) if half == 0 else (2, 3, 4):
            begin.append(len(lanes))
            for py in range(2):
                if a == 2 and py != half:
                    continue
                lanes += [(a, py, b, c) for b in range(5) for c in range(3)]
        plan.append(lanes)
        starts.append(begin)
    return plan, starts


LANES, A_START = lane_plan()


def constants():
    place = np.zeros((STEM_PAIRS, 4, 64, 128), np.float32)
    for pair in range(STEM_PAIRS):
        for qx in range(2):
            for qy in range(2):
                for dz in range(3):
                    for dy in range(3):
                        for dx in range(3):
                            y = (2 * pair + qy + dy - 3) % 16
                            place[pair, qx + dx, dz * 16 + y, (qx * 2 + qy) * 32 + (dz * 3 + dy) * 3 + dx] = 1
    columns = np.zeros((2, 75, 256), np.float32)
    pairs = (0, BLOCK_PAIRS - 1) + tuple(range(1, BLOCK_PAIRS - 1))
    blend = np.zeros((len(pairs), 256, 128), np.float32)
    for half in range(2):
        for n, (a, py, b, c) in enumerate(LANES[half]):
            columns[py, (a * 5 + b) * 3 + c, half * 128 + n] = 0.5
            for i, pair in enumerate(pairs):
                y = 2 * pair + py + b - R
                if y < 0:
                    lane = 24 + 2 * c + y + R
                elif y >= TY:
                    lane = 32 + 2 * c + y - TY
                else:
                    lane = c * TY + y
                blend[i, half * 128 + n, lane] = (R + 1 - abs(a - R)) * (R + 1 - abs(b - R))
    return (
        jnp.asarray(place.reshape(STEM_PAIRS, 256, 128), BF),
        jnp.asarray(columns, BF),
        jnp.asarray(blend.reshape(-1, 128), BF),
    )


def local(intensity, first_kernel, second_kernel, third_kernel, head_weight):
    place, columns, blend = constants()
    vmem = pl.BlockSpec(memory_space=pltpu.VMEM)
    hbm = pl.BlockSpec(memory_space=pltpu.HBM)
    return pl.pallas_call(
        compute_kernel,
        out_shape=pltpu.VMEM((3, Z, TY, TX), F32),
        in_specs=[hbm] * 8,
        out_specs=vmem,
        scratch_shapes=[
            pltpu.VMEM(intensity.shape, BF),
            pltpu.VMEM(place.shape, BF),
            pltpu.VMEM((9, 3, C), BF),
            pltpu.VMEM((27, C, C), BF),
            pltpu.VMEM((27, C, C), BF),
            pltpu.VMEM(head_weight.shape, BF),
            pltpu.VMEM(columns.shape, BF),
            pltpu.VMEM(blend.shape, BF),
            pltpu.VMEM((2, 16, Z * TY), BF),
            pltpu.VMEM((2, Z, TY, TX), BF),
            pltpu.VMEM((3, 2, 16, Z * TY), BF),
            pltpu.VMEM((2, Z, TY, TX), F32),
            pltpu.VMEM((2, Z, TY, TX), F32),
            pltpu.VMEM((32, C), F32),
            pltpu.VMEM((STEM_PAIRS, 256, 256), BF),
            pltpu.VMEM((768, 256), BF),
            pltpu.VMEM((1024, 256), BF),
            pltpu.VMEM((768, 256), BF),
            pltpu.VMEM((1024, 256), BF),
            pltpu.VMEM((128, 256), BF),
            pltpu.VMEM((2, Z + 2, 2 * TY, TX), F32),
            pltpu.VMEM((2, Z + 2, 2 * TY, TX), F32),
            pltpu.VMEM((144 * Z, 128), F32),
            pltpu.VMEM((STEM_X + 1, Z, 128), BF),
            pltpu.VMEM((STEM_PAIRS, 2, STEM_X, Z, 128), BF),
            pltpu.VMEM((INNER_PAIRS, 2, INNER_X, Z, 128), BF),
            pltpu.VMEM((BLOCK_PAIRS, 2, BLOCK_X, Z, 256), BF),
            pltpu.VMEM((TX // 2, 2, Z, 128), F32),
            pltpu.SemaphoreType.DMA((8,)),
            pltpu.SemaphoreType.DMA((8,)),
            pltpu.SemaphoreType.DMA((8,)),
            pltpu.SemaphoreType.DMA((2,)),
            pltpu.SemaphoreType.DMA((2,)),
        ],
        compiler_params=pltpu.CompilerParams(
            collective_id=0, has_side_effects=True, vmem_limit_bytes=56 * 2**20
        ),
        name="convnet",
    )(
        intensity, place, first_kernel.reshape(9, 3, C),
        second_kernel.reshape(27, C, C), third_kernel.reshape(27, C, C), head_weight, columns, blend,
    )


def solution(mesh):
    in_specs = (P(None, "gy", "gx"), P(), P(), P(), P())
    out_specs = P(None, None, "gy", "gx")
    return jax.shard_map(local, mesh=mesh, in_specs=in_specs, out_specs=out_specs, check_vma=False)
```
